32 devices in a mesh: dp: 4 (over x, core), blk: 2 (over y), head: 4 (over z).
Axes of the slice: x: 2, y: 2, z: 4, core: 2. Of those that a mesh axis runs over, the one named last changes fastest.
Arguments:
- dec_in: bfloat16 [1024, 768], P(('dp', 'blk')), may hold values from -6 to 6
- enc_out: bfloat16 [61440, 768], P(('dp', 'blk', 'head')), may hold values from -6 to 6
- passage_len: int32 [160], P(('dp', 'blk')), may hold values from 288 to 384
- dec_len: int32 [8], P(('dp', 'blk')), may hold values from 64 to 128
- passage_owner: int32 [160], P(('dp', 'blk')), may hold values from 0 to 1, as said below
- gain_self: bfloat16 [768], replicated, may hold values from 0.099609375 to 1.8984375
- gain_cross: bfloat16 [768], replicated, may hold values from 0.099609375 to 1.8984375
- gain_ffn: bfloat16 [768], replicated, may hold values from 0.099609375 to 1.8984375
- w_query: bfloat16 [768, 768], P('head'), may hold values from -0.109375 to 0.109375
- w_key: bfloat16 [768, 768], P('head'), may hold values from -0.109375 to 0.109375
- w_value: bfloat16 [768, 768], P('head'), may hold values from -0.21875 to 0.21875
- w_out: bfloat16 [768, 768], P('head'), may hold values from -0.3125 to 0.3125
- c_query: bfloat16 [768, 768], P('head'), may hold values from -0.109375 to 0.109375
- c_key: bfloat16 [768, 768], P('head'), may hold values from -0.109375 to 0.109375
- c_value: bfloat16 [768, 768], P('head'), may hold values from -0.21875 to 0.21875
- c_out: bfloat16 [768, 768], P('head'), may hold values from -2.5 to 2.5
- w_in: bfloat16 [768, 3072], P(None, 'head'), may hold values from -0.21875 to 0.21875
- w_back: bfloat16 [3072, 768], P('head'), may hold values from -0.15625 to 0.15625
- cotangent: bfloat16 [1024, 768], P(('dp', 'blk')), may hold values from -6 to 6
Outputs:
- layer_out: bfloat16 [1024, 768], P(('dp', 'blk'))
- grad_in: float32 [1024, 768], P(('dp', 'blk'))
- grad_enc: float32 [61440, 768], P(('dp', 'blk', 'head'))
- grad_gain_self: float32 [768], replicated
- grad_gain_cross: float32 [768], replicated
- grad_gain_ffn: float32 [768], replicated
- grad_w_query: float32 [768, 768], P('head')
- grad_w_key: float32 [768, 768], P('head')
- grad_w_value: float32 [768, 768], P('head')
- grad_w_out: float32 [768, 768], P('head')
- grad_c_query: float32 [768, 768], P('head')
- grad_c_key: float32 [768, 768], P('head')
- grad_c_value: float32 [768, 768], P('head')
- grad_c_out: float32 [768, 768], P('head')
- grad_w_in: float32 [768, 3072], P(None, 'head')
- grad_w_back: float32 [3072, 768], P('head')
The draws below stay inside these ranges and needn't reach their ends.
Inputs may be any that keep to these rules, and one draw needn't show every extreme that they name: `passage_owner`: A question number of its dp group (question g of a group has its decoder tokens on the device of index g // 1 along blk). Each question owns exactly 20 passages of its group, at least one and at most 10 among the 20 passages of any one device of blk; on every device some question owns exactly 10.
All inputs are finite; a program needn't handle non-finite values.
Results may differ from the reference program's by a relative error of at most 0.035.
The reference program's roundings to bfloat16 on the way count: a program that leaves them out, or rounds other values in their place, can miss the bound.
Values may be sent and summed in bfloat16 or wider, within the bound.
No kernel may reach another device: no remote copies, remote signals or barrier semaphores. Data moves between devices by JAX's collectives and lax.ppermute only.
A program may use at most 192 MiB of HBM per device.

```python
import jax
import jax.numpy as jnp
from jax import lax

D = 768
HEADS = 12
DHEAD = 64
FF = 3072
LQ = 128
LP = 384
NPASS = 20
QDEV = 1
QUESTIONS = 2
PDEV = 20
DTOKENS = 1024
PASSAGES = 160
ETOKENS = 61440
N_DP = 4
N_BLK = 2


def draw_passage_owner(key, part):
    key = jax.random.fold_in(key, 11)
    most = (NPASS + N_BLK - 1) // N_BLK
    questions = QDEV * N_BLK
    others = max(N_BLK - 1, 1)
    ranked = jnp.arange(NPASS, dtype=jnp.int32)
    filler = 1 + (ranked - N_BLK - most + 1) % others
    ranked = jnp.where(ranked < N_BLK, ranked, jnp.where(ranked < N_BLK + most - 1, 0, filler))

    def one_class(class_key):
        chosen = jax.random.permutation(jax.random.fold_in(class_key, 1), N_BLK).astype(jnp.int32)
        placed = jax.random.permutation(jax.random.fold_in(class_key, 2), NPASS).astype(jnp.int32)
        return jnp.take(chosen, jnp.take(ranked, placed))

    def one_group(group_key):
        columns = jax.vmap(one_class)(jax.random.split(group_key, QDEV))
        offsets = jnp.arange(QDEV, dtype=jnp.int32)[None, :] + QDEV * columns.T
        offsets = offsets.reshape(PDEV)
        devices = jnp.arange(N_BLK, dtype=jnp.int32)[:, None] * QDEV
        owners = (devices + offsets[None, :]) % questions
        shuffles = jax.vmap(lambda device_key: jax.random.permutation(device_key, PDEV))(jax.random.split(jax.random.fold_in(group_key, 5), N_BLK))
        return jnp.take_along_axis(owners, shuffles.astype(jnp.int32), axis=1)
    groups = jax.vmap(one_group)(jax.random.split(key, N_DP))
    return groups.reshape(N_DP * N_BLK * PDEV).astype(jnp.int32)


def place_ends(array, key, smallest, largest):
    longest = array.shape.index(max(array.shape))
    spots = []
    for shift in (0, 1):
        where = [jax.random.randint(jax.random.fold_in(key, axis), (), 0, length) for axis, length in enumerate(array.shape)]
        where[longest] = (where[longest] + shift) % array.shape[longest]
        spots.append(tuple(where))
    return array.at[spots[0]].set(smallest).at[spots[1]].set(largest)


def level_of(key, shape, cuts, least, high):
    level, own = 1.0, jax.random.fold_in(key, 6)
    for dim, parts in cuts:
        heights = jnp.exp(jax.random.uniform(jax.random.fold_in(own, dim), (parts,), jnp.float32, least / len(cuts), high / len(cuts)))
        level = level * jnp.repeat(heights, shape[dim] // parts).reshape([-1 if axis == dim else 1 for axis in range(len(shape))])
    return level


def normal_values(stream_key, extent, spread, reach, pieces=(), kind=jnp.bfloat16):
    values = jax.random.normal(stream_key, extent, jnp.float32) * spread
    if len(pieces) > 0:
        values = level_of(stream_key, extent, pieces, -0.22, 0.18) * values
    return jnp.clip(values, min=-reach, max=reach).astype(kind)


def setup_inputs(seed: int = 0) -> dict:
    seeds = jax.random.split(jax.random.key(seed), 20)
    return {
        "dec_in": normal_values(seeds[0], (DTOKENS, D), 1.0, 6.0, ((0, 8),)),
        "enc_out": normal_values(seeds[1], (ETOKENS, D), 1.0, 6.0, ((0, 32),)),
        "passage_len": place_ends(jax.random.randint(seeds[2], (PASSAGES,), 3 * LP // 4, LP + 1), jax.random.fold_in(seeds[2], 1), 3 * LP // 4, LP).astype(jnp.int32),
        "dec_len": place_ends(jax.random.randint(seeds[3], (N_DP * QUESTIONS,), LQ // 2, LQ + 1), jax.random.fold_in(seeds[3], 1), LQ // 2, LQ).astype(jnp.int32),
        "passage_owner": draw_passage_owner(jax.random.fold_in(seeds[19], 71), 0),
        "gain_self": jnp.clip(1.0 + 0.18 * jax.random.normal(seeds[5], (D,), jnp.float32), 0.099609375, 1.8984375).astype(jnp.bfloat16),
        "gain_cross": jnp.clip(1.0 + 0.18 * jax.random.normal(seeds[6], (D,), jnp.float32), 0.099609375, 1.8984375).astype(jnp.bfloat16),
        "gain_ffn": jnp.clip(1.0 + 0.18 * jax.random.normal(seeds[7], (D,), jnp.float32), 0.099609375, 1.8984375).astype(jnp.bfloat16),
        "w_query": normal_values(seeds[8], (D, D), (4 * D) ** -0.5, 0.109375, ((0, 4),)),
        "w_key": normal_values(seeds[9], (D, D), (4 * D) ** -0.5, 0.109375, ((0, 4),)),
        "w_value": normal_values(seeds[10], (D, D), D ** -0.5, 0.21875, ((0, 4),)),
        "w_out": normal_values(seeds[11], (D, D), (D // 2) ** -0.5, 0.3125, ((0, 4),)),
        "c_query": normal_values(seeds[12], (D, D), (4 * D) ** -0.5, 0.109375, ((0, 4),)),
        "c_key": normal_values(seeds[13], (D, D), (4 * D) ** -0.5, 0.109375, ((0, 4),)),
        "c_value": normal_values(seeds[14], (D, D), D ** -0.5, 0.21875, ((0, 4),)),
        "c_out": normal_values(seeds[15], (D, D), (max(D // 128, 1)) ** -0.5, 2.5, ((0, 4),)),
        "w_in": normal_values(seeds[16], (D, FF), D ** -0.5, 0.21875, ((1, 4),)),
        "w_back": normal_values(seeds[17], (FF, D), (FF // 2) ** -0.5, 0.15625, ((0, 4),)),
        "cotangent": normal_values(seeds[18], (DTOKENS, D), 1.0, 6.0, ((0, 8),)),
    }


@jax.custom_vjp
def low(v):
    return lax.optimization_barrier(v.astype(jnp.bfloat16)).astype(jnp.float32)

@jax.custom_vjp
def low_back(v):
    return v

def low_keep(v):
    return (low(v), None)

def low_pass(kept, grad):
    return (grad,)

def back_keep(v):
    return (v, None)

def back_low(kept, grad):
    return (low(grad),)
low.defvjp(low_keep, low_pass)
low_back.defvjp(back_keep, back_low)
norm_epsilon = 1e-06
masked_score = -1e+30

def rounded(values):
    return low(low_back(values))

def normalize(values, gain):
    return values * lax.rsqrt(lax.optimization_barrier(jnp.mean(values * values, axis=-1, keepdims=True)) + norm_epsilon) * gain

def product(left, right):
    return jnp.dot(left, right, precision=lax.Precision.HIGHEST, preferred_element_type=jnp.float32)

def heads_of(values):
    return values.reshape(values.shape[0], HEADS, DHEAD)

def attend(queries, key_rows, value_rows, allowed):
    scores = low_back(jnp.einsum('qhd,khd->hqk', queries, key_rows, precision=lax.Precision.HIGHEST))
    scores = jnp.where(allowed[None], scores, masked_score)
    soft_weights = jax.nn.softmax(scores, axis=-1)
    return jnp.einsum('hqk,khd->qhd', low(soft_weights), value_rows, precision=lax.Precision.HIGHEST)

def layer(dec_rows, enc_rows, self_allowed, cross_allowed, gain_self, gain_cross, gain_ffn, w_query, w_key, w_value, w_out, c_query, c_key, c_value, c_out, w_in, w_back):
    normed = low(normalize(dec_rows, gain_self))
    attended = attend(heads_of(rounded(product(normed, w_query.T))), heads_of(rounded(product(normed, w_key.T))), heads_of(rounded(product(normed, w_value.T))), self_allowed)
    attended = rounded(attended.reshape(LQ, D))
    first = dec_rows + low_back(product(attended, w_out))
    normed = low(normalize(first, gain_cross))
    crossed = attend(heads_of(rounded(product(normed, c_query.T))), heads_of(rounded(product(enc_rows, c_key.T))), heads_of(rounded(product(enc_rows, c_value.T))), cross_allowed)
    crossed = rounded(crossed.reshape(LQ, D))
    second = first + low_back(product(crossed, c_out))
    normed = low(normalize(second, gain_ffn))
    hidden = low(jax.nn.gelu(low_back(product(normed, w_in))))
    return second + product(hidden, w_back)

def reference(dec_in, enc_out, passage_len, dec_len, passage_owner, gain_self, gain_cross, gain_ffn, w_query, w_key, w_value, w_out, c_query, c_key, c_value, c_out, w_in, w_back, cotangent):
    params = tuple((tensor.astype(jnp.float32) for tensor in (gain_self, gain_cross, gain_ffn, w_query, w_key, w_value, w_out, c_query, c_key, c_value, c_out, w_in, w_back)))
    group_size = PDEV * N_BLK
    owners = passage_owner.reshape(N_DP, group_size)
    ordering = jnp.argsort(owners, axis=1, stable=True).astype(jnp.int32)
    ordering = ordering + (jnp.arange(N_DP, dtype=jnp.int32) * group_size)[:, None]
    flat_order = ordering.reshape(PASSAGES)
    passage_sets = flat_order.reshape(N_DP * QUESTIONS, NPASS)
    enc_blocks = enc_out.reshape(PASSAGES, LP, D)
    dec_blocks = dec_in.reshape(N_DP * QUESTIONS, LQ, D)
    cot_blocks = cotangent.reshape(N_DP * QUESTIONS, LQ, D)
    positions = jnp.arange(LQ, dtype=jnp.int32)
    causal = positions[None, :] <= positions[:, None]
    slots = jnp.arange(LP, dtype=jnp.int32)

    def one_question(carried, inputs):
        dec_rows, cot_rows, length_now, members = inputs
        enc_rows = jnp.take(enc_blocks, members, axis=0).reshape(NPASS * LP, D).astype(jnp.float32)
        lengths = jnp.take(passage_len, members, axis=0)
        cross_allowed = (slots[None, :] < lengths[:, None]).reshape(1, NPASS * LP)
        self_allowed = causal & (positions[None, :] < length_now)

        def forward(dec_float, enc_float, *weights):
            return layer(dec_float, enc_float, self_allowed, cross_allowed, *weights)
        result, pull_back = jax.vjp(forward, dec_rows.astype(jnp.float32), enc_rows, *params)
        grads = pull_back(cot_rows.astype(jnp.float32))
        carried = tuple((total + term for total, term in zip(carried, grads[2:])))
        return (carried, (result.astype(jnp.bfloat16), grads[0], grads[1]))
    start_sums = tuple((jnp.zeros(tensor.shape, jnp.float32) for tensor in params))
    sums, stacked = lax.scan(one_question, start_sums, (dec_blocks, cot_blocks, dec_len, passage_sets))
    outputs, grad_rows, grad_encs = stacked
    inverse = jnp.argsort(flat_order).astype(jnp.int32)
    grad_enc = jnp.take(grad_encs.reshape(PASSAGES, LP, D), inverse, axis=0).reshape(PASSAGES * LP, D)
    return (outputs.reshape(DTOKENS, D), grad_rows.reshape(DTOKENS, D), grad_enc, sums[0], sums[1], sums[2], sums[3], sums[4], sums[5], sums[6], sums[7], sums[8], sums[9], sums[10], sums[11], sums[12])
```

```python
import functools

import jax
import jax.numpy as jnp
from jax import lax
from jax.experimental import pallas as pl
from jax.experimental.pallas import tpu as pltpu
from jax.sharding import PartitionSpec as P

DHEAD = 64
LP = 384
norm_epsilon = 1e-06
masked_score = -1e30
bf16 = jnp.bfloat16
f32 = jnp.float32
PAIR = 2 * DHEAD
STATS = 128
DELTA_LANE = 16
SPLIT_LANE = 32


def nn(left, right):
    return lax.dot_general(left, right, (((1,), (0,)), ((), ())), preferred_element_type=f32)


def nt(left, right):
    return lax.dot_general(left, right, (((1,), (1,)), ((), ())), preferred_element_type=f32)


def tn(left, right):
    return lax.dot_general(left, right, (((0,), (0,)), ((), ())), preferred_element_type=f32)


def exact_nn(left, right):
    return lax.dot_general(
        left,
        right,
        (((1,), (0,)), ((), ())),
        precision=lax.Precision.HIGHEST,
        preferred_element_type=f32,
    )


def norm_scale(values):
    return lax.rsqrt(jnp.mean(values * values, axis=-1, keepdims=True) + norm_epsilon)


def normalize(values, gain):
    return values * norm_scale(values) * gain


def norm_back(upstream, values, gain):
    scale = norm_scale(values)
    unit = values * scale
    scaled = upstream * gain
    grad = scale * (scaled - unit * jnp.mean(scaled * unit, axis=-1, keepdims=True))
    return grad, jnp.sum(upstream * unit, axis=0, keepdims=True)


def vmem():
    return pl.BlockSpec(memory_space=pltpu.VMEM)


def smem():
    return pl.BlockSpec(memory_space=pltpu.SMEM)


def shaped(shape, dtype):
    return jax.ShapeDtypeStruct(shape, dtype)


def call(kernel, outs, scalars, arrays, scratch=(), megabytes=40):
    return pl.pallas_call(
        kernel,
        out_shape=tuple(outs),
        in_specs=[smem()] * len(scalars) + [vmem()] * len(arrays),
        out_specs=tuple(vmem() for _ in outs),
        scratch_shapes=list(scratch),
        compiler_params=pltpu.CompilerParams(vmem_limit_bytes=megabytes * 1024 * 1024),
    )(*scalars, *arrays)


def rows_of(place, count):
    return pl.ds(pl.multiple_of(place * count, count), count)


def head_blocks(width, head_count, shift):
    return [(j ^ shift) * width for j in range(head_count)]


def permuted(values, width, head_count, shift):
    if shift == 0:
        return values
    return jnp.concatenate(
        [values[:, o : o + width] for o in head_blocks(width, head_count, shift)], axis=1
    )


def self_kernel(
    len_ref, dec_ref, gain_ref, wq_ref, wk_ref, wv_ref, normed_ref, qkv_ref, out_ref
):
    rows = dec_ref.shape[0]
    width = wq_ref.shape[0]
    normed = normalize(dec_ref[...].astype(f32), gain_ref[...].astype(f32)).astype(bf16)
    normed_ref[...] = normed
    for i, weight in enumerate((wq_ref, wk_ref, wv_ref)):
        qkv_ref[:, i * width : (i + 1) * width] = nt(normed, weight[...]).astype(bf16)
    at_q = lax.broadcasted_iota(jnp.int32, (rows, rows), 0)
    at_k = lax.broadcasted_iota(jnp.int32, (rows, rows), 1)
    allowed = (at_k <= at_q) & (at_k < len_ref[0])
    outs = []
    for h in range(width // DHEAD):
        o = h * DHEAD
        q = qkv_ref[:, o : o + DHEAD]
        k = qkv_ref[:, width + o : width + o + DHEAD]
        v = qkv_ref[:, 2 * width + o : 2 * width + o + DHEAD]
        scores = jnp.where(allowed, nt(q, k), masked_score)
        raised = jnp.exp(scores - jnp.max(scores, axis=-1, keepdims=True))
        probs = raised / jnp.sum(raised, axis=-1, keepdims=True)
        outs.append(nn(probs.astype(bf16), v))
    out_ref[...] = jnp.concatenate(outs, axis=1).astype(bf16)


def query_kernel(blk_count, head_count, *refs):
    chunks = refs[: blk_count * head_count]
    refs = refs[blk_count * head_count :]
    decs = refs[:blk_count]
    w_out_ref, c_query_ref, gain_ref, first_ref, normed_ref, q_ref = refs[blk_count:]
    gain = gain_ref[...].astype(f32)
    for kb in range(blk_count):
        attended = jnp.concatenate(
            [chunks[kb * head_count + kh][...] for kh in range(head_count)], axis=1
        )
        first = decs[kb][...].astype(f32) + nn(attended, w_out_ref[...])
        normed = normalize(first, gain).astype(bf16)
        if kb == 0:
            first_ref[...] = first
            normed_ref[...] = normed
        q_ref[kb] = nt(normed, c_query_ref[...]).astype(bf16)


def spread_pairs(values, target, kb):
    rows = values.shape[0]
    for j in range(values.shape[1] // PAIR):
        pair = values[:, j * PAIR : (j + 1) * PAIR]
        lane = lax.broadcasted_iota(jnp.int32, pair.shape, 1)
        zero = jnp.zeros_like(pair)
        target[kb, j, 0:rows, :] = jnp.where(lane < DHEAD, pair, zero)
        target[kb, j, rows : 2 * rows, :] = jnp.where(lane < DHEAD, zero, pair)


def cross_forward_kernel(blk_count, head_count, width, *refs):
    slot_ref, len_ref, me_ref, q_ref, k_ref, vt_ref = refs[:6]
    chunk_count = blk_count * head_count
    out_refs = refs[6 : 6 + chunk_count]
    q2, acc, highest, totals, stat, flat, flat_stat = refs[6 + chunk_count :]
    rows, depth = q_ref.shape[1], q_ref.shape[2]
    pairs = depth // PAIR
    step = pl.program_id(0)

    @pl.when(step == 0)
    def _():
        for kb in range(blk_count):
            spread_pairs(q_ref[kb], q2, kb)
        highest[...] = jnp.full(highest.shape, masked_score, f32)
        totals[...] = jnp.zeros(totals.shape, f32)
        acc[...] = jnp.zeros(acc.shape, f32)

    slot = slot_ref[step]
    valid = lax.broadcasted_iota(jnp.int32, (LP, 2 * rows), 0) < len_ref[step]
    for j in range(pairs):
        span = slice(j * PAIR, (j + 1) * PAIR)
        scores = jnp.where(valid, nt(k_ref[:, span], q2[slot, j]), masked_score)
        before = highest[slot, j : j + 1, :]
        newest = jnp.maximum(before, jnp.max(scores, axis=0, keepdims=True))
        raised = jnp.exp(scores - newest)
        factor = jnp.exp(before - newest)
        highest[slot, j : j + 1, :] = newest
        totals[slot, j : j + 1, :] = totals[slot, j : j + 1, :] * factor + jnp.sum(
            raised, axis=0, keepdims=True
        )
        update = nn(vt_ref[span, :], raised.astype(bf16))
        low = slice(j * PAIR, j * PAIR + DHEAD)
        high = slice(j * PAIR + DHEAD, (j + 1) * PAIR)
        acc[slot, low, :] = acc[slot, low, :] * factor[:, :rows] + update[:DHEAD, :rows]
        acc[slot, high, :] = acc[slot, high, :] * factor[:, rows:] + update[DHEAD:, rows:]

    @pl.when(step == pl.num_programs(0) - 1)
    def _():
        stat[...] = jnp.zeros(stat.shape, f32)
        piece = rows // head_count
        per = width // DHEAD
        for kb in range(blk_count):
            flat[...] = acc[kb].T
            for kh in range(head_count):
                for head in range(depth // DHEAD):
                    at = ((head // per) ^ kh) * per + head % per
                    lanes = slice((head % 2) * rows, (head % 2 + 1) * rows)
                    stat[at : at + 1, :] = highest[kb, head // 2 : head // 2 + 1, lanes]
                    stat[DHEAD + at : DHEAD + at + 1, :] = totals[
                        kb, head // 2 : head // 2 + 1, lanes
                    ]
                flat_stat[...] = stat[...].T
                mine = rows_of(me_ref[0] ^ kh, piece)
                target = out_refs[kb * head_count + kh]
                target[:, :depth] = permuted(flat[mine, :], width, head_count, kh)
                target[:, depth:] = flat_stat[mine, :]


def cross_forward(slots, lengths, me, queries, keys, values_t, head_count, width):
    blk_count, rows, depth = queries.shape
    passages = slots.shape[0]
    piece = rows // head_count
    chunk_count = blk_count * head_count
    pairs = depth // PAIR
    grid = pltpu.PrefetchScalarGridSpec(
        num_scalar_prefetch=3,
        grid=(passages,),
        in_specs=[
            pl.BlockSpec((blk_count, rows, depth), lambda p, *_: (0, 0, 0)),
            pl.BlockSpec((LP, depth), lambda p, *_: (p, 0)),
            pl.BlockSpec((depth, LP), lambda p, *_: (0, p)),
        ],
        out_specs=tuple(
            pl.BlockSpec((piece, depth + STATS), lambda p, *_: (0, 0)) for _ in range(chunk_count)
        ),
        scratch_shapes=[
            pltpu.VMEM((blk_count, pairs, 2 * rows, PAIR), bf16),
            pltpu.VMEM((blk_count, depth, rows), f32),
            pltpu.VMEM((blk_count, 8, 2 * rows), f32),
            pltpu.VMEM((blk_count, 8, 2 * rows), f32),
            pltpu.VMEM((STATS, rows), f32),
            pltpu.VMEM((rows, depth), f32),
            pltpu.VMEM((rows, STATS), f32),
        ],
    )
    return pl.pallas_call(
        functools.partial(cross_forward_kernel, blk_count, head_count, width),
        out_shape=tuple(shaped((piece, depth + STATS), f32) for _ in range(chunk_count)),
        grid_spec=grid,
        compiler_params=pltpu.CompilerParams(
            vmem_limit_bytes=50 * 1024 * 1024, dimension_semantics=("arbitrary",)
        ),
    )(slots, lengths, me, queries, keys, values_t)


def head_matrix(depth):
    head = lax.broadcasted_iota(jnp.int32, (STATS, depth), 0)
    column = lax.broadcasted_iota(jnp.int32, (STATS, depth), 1)
    return (head == column // DHEAD).astype(f32)


def combine_kernel(chunk_count, me_ref, *refs):
    chunks = refs[:chunk_count]
    first_ref, c_out_ref, gain_ref, cross_ref, second_ref, logsum_ref, message_ref = refs[
        chunk_count:
    ]
    piece, depth = cross_ref.shape
    stats = [chunk[:, depth:] for chunk in chunks]
    highest = stats[0]
    for other in stats[1:]:
        highest = jnp.maximum(highest, other)
    lane = lax.broadcasted_iota(jnp.int32, (piece, STATS), 1)
    real = lane < depth // DHEAD
    weights = [jnp.where(real, jnp.exp(one - highest), 0.0) for one in stats]
    total = sum(w * pltpu.roll(one, STATS - DHEAD, 1) for w, one in zip(weights, stats))
    total = jnp.where(real, total, 1.0)
    logsum_ref[...] = jnp.where(real, highest + jnp.log(total), 0.0)
    spread = head_matrix(depth)
    weighted = exact_nn(jnp.concatenate(weights, axis=0), spread)
    cross = sum(
        chunk[:, :depth] * weighted[i * piece : (i + 1) * piece] for i, chunk in enumerate(chunks)
    )
    cross = cross / exact_nn(total, spread)
    cross_ref[...] = cross
    rounded = cross.astype(bf16)
    first = first_ref[rows_of(me_ref[0], piece), :]
    second = first + nn(rounded, c_out_ref[...])
    second_ref[...] = second
    message_ref[:, :depth] = normalize(second, gain_ref[...].astype(f32)).astype(bf16)
    message_ref[:, depth:] = rounded


def ffn_kernel(head_count, width, me_ref, *refs):
    chunks = refs[:head_count]
    cot_ref, w_in_ref, w_back_ref = refs[head_count : head_count + 3]
    grads = refs[head_count + 3 : 2 * head_count + 3]
    normed_ref, hidden_ref, pre_grad_ref, cols_ref, partial_ref, total = refs[2 * head_count + 3 :]
    piece, depth = grads[0].shape
    for k, chunk in enumerate(chunks):
        mine = rows_of(me_ref[0] ^ k, piece)
        normed_ref[mine, :] = chunk[:, :depth]
        cols_ref[mine, :] = chunk[:, depth + k * width : depth + (k + 1) * width]
    before = nn(normed_ref[...], w_in_ref[...])
    root = 0.7978845608028654
    cube = 0.044715
    square = before * before
    bend = jnp.tanh(root * (before + cube * before * square))
    hidden_ref[...] = (0.5 * before * (1.0 + bend)).astype(bf16)
    slope = 0.5 * (1.0 + bend) + 0.5 * before * (1.0 - bend * bend) * root * (
        1.0 + 3.0 * cube * square
    )
    pre_grad_ref[...] = (nt(cot_ref[...], w_back_ref[...]) * slope).astype(bf16)
    total[...] = nt(pre_grad_ref[...], w_in_ref[...])
    for k, grad in enumerate(grads):
        grad[...] = total[rows_of(me_ref[0] ^ k, piece), :]
    partial_ref[...] = nn(hidden_ref[...], w_back_ref[...])


def branch_kernel(head_count, width, me_ref, *refs):
    chunks = refs[:head_count]
    second_ref, gain_ref, cot_ref, c_out_ref, cross_ref, logsum_ref = refs[
        head_count : head_count + 6
    ]
    grad_ref, gain_grad_ref = refs[head_count + 6 : head_count + 8]
    messages = refs[head_count + 8 :]
    piece, depth = second_ref.shape
    upstream = sum(chunk[...] for chunk in chunks)
    grad, gain_grad_ref[...] = norm_back(upstream, second_ref[...], gain_ref[...].astype(f32))
    grad = cot_ref[rows_of(me_ref[0], piece), :].astype(f32) + grad
    grad_ref[...] = grad
    branch = grad.astype(bf16)
    grad_cross = nt(branch, c_out_ref[...]).astype(bf16).astype(f32)
    spread = head_matrix(depth)
    deltas = lax.dot_general(
        grad_cross * cross_ref[...],
        spread,
        (((1,), (1,)), ((), ())),
        precision=lax.Precision.HIGHEST,
        preferred_element_type=f32,
    )
    stats = logsum_ref[...] + pltpu.roll(deltas, DELTA_LANE, 1)
    per = width // DHEAD
    heads = depth // DHEAD
    source = lax.broadcasted_iota(jnp.int32, (STATS, STATS), 0)
    target = lax.broadcasted_iota(jnp.int32, (STATS, STATS), 1)
    place = source % DELTA_LANE
    for k, message in enumerate(messages):
        moved = (source - place) + ((place // per) ^ k) * per + place % per
        shuffle = ((target == moved) & (place < heads) & (source < 2 * DELTA_LANE)).astype(f32)
        aligned = exact_nn(stats, shuffle)
        high = aligned.astype(bf16).astype(f32)
        middle = (aligned - high).astype(bf16).astype(f32)
        lowest = aligned - high - middle
        message[:, :depth] = branch
        message[:, depth:] = (
            high + pltpu.roll(middle, SPLIT_LANE, 1) + pltpu.roll(lowest, 2 * SPLIT_LANE, 1)
        ).astype(bf16)


def cross_backward_kernel(blk_count, head_count, width, *refs):
    slot_ref, len_ref, me_ref, q_ref, c_out_ref, k_ref, v_ref = refs[:7]
    chunk_count = blk_count * head_count
    chunks = refs[7 : 7 + chunk_count]
    refs = refs[7 + chunk_count :]
    out_refs = refs[:chunk_count]
    branch_ref, grad_k_ref, grad_v_ref = refs[chunk_count : chunk_count + 3]
    q2, g2, stats, branch, flat_stat, grad_q = refs[chunk_count + 3 :]
    rows, depth = q_ref.shape[1], q_ref.shape[2]
    pairs = depth // PAIR
    piece = rows // head_count
    step = pl.program_id(0)

    @pl.when(step == 0)
    def _():
        for kb in range(blk_count):
            for kh in range(head_count):
                chunk = chunks[kb * head_count + kh]
                mine = rows_of(me_ref[0] ^ kh, piece)
                branch[mine, :] = chunk[:, :depth]
                packed = chunk[:, depth:].astype(f32)
                flat_stat[mine, :] = (
                    packed
                    + pltpu.roll(packed, STATS - SPLIT_LANE, 1)
                    + pltpu.roll(packed, STATS - 2 * SPLIT_LANE, 1)
                )
            if kb == 0:
                branch_ref[...] = branch[...]
            stats[kb] = flat_stat[...].T
            spread_pairs(q_ref[kb], q2, kb)
            spread_pairs(nt(branch[...], c_out_ref[...]).astype(bf16), g2, kb)
        grad_q[...] = jnp.zeros(grad_q.shape, f32)

    slot = slot_ref[step]
    valid = lax.broadcasted_iota(jnp.int32, (LP, 2 * rows), 0) < len_ref[step]
    lane = lax.broadcasted_iota(jnp.int32, (rows, PAIR), 1)
    for j in range(pairs):
        span = slice(j * PAIR, (j + 1) * PAIR)
        logsum = jnp.concatenate(
            [stats[slot, 2 * j : 2 * j + 1, :], stats[slot, 2 * j + 1 : 2 * j + 2, :]], axis=1
        )
        o = DELTA_LANE + 2 * j
        delta = jnp.concatenate([stats[slot, o : o + 1, :], stats[slot, o + 1 : o + 2, :]], axis=1)
        scores = nt(k_ref[:, span], q2[slot, j])
        probs = jnp.where(valid, jnp.exp(scores - logsum), 0.0)
        grad_probs = nt(v_ref[:, span], g2[slot, j])
        grad_scores = (probs * (grad_probs - delta)).astype(bf16)
        grad_v_ref[:, span] = nn(probs.astype(bf16), g2[slot, j]).astype(bf16)
        grad_k_ref[:, span] = nn(grad_scores, q2[slot, j]).astype(bf16)
        both = tn(grad_scores, k_ref[:, span])
        grad_q[slot, :, span] = grad_q[slot, :, span] + jnp.where(
            lane < DHEAD, both[:rows], both[rows:]
        )

    @pl.when(step == pl.num_programs(0) - 1)
    def _():
        for kb in range(blk_count):
            for kh in range(head_count):
                mine = rows_of(me_ref[0] ^ kh, piece)
                out_refs[kb * head_count + kh][...] = permuted(
                    grad_q[kb, mine, :], width, head_count, kh
                )


def cross_backward(slots, lengths, me, queries, c_out, keys, values, chunks, head_count, width):
    blk_count, rows, depth = queries.shape
    passages = slots.shape[0]
    piece = rows // head_count
    chunk_count = blk_count * head_count
    pairs = depth // PAIR
    whole = lambda shape: pl.BlockSpec(shape, lambda p, *_: (0,) * len(shape))
    passage = pl.BlockSpec((LP, depth), lambda p, *_: (p, 0))
    grid = pltpu.PrefetchScalarGridSpec(
        num_scalar_prefetch=3,
        grid=(passages,),
        in_specs=[
            whole((blk_count, rows, depth)),
            whole((depth, depth)),
            passage,
            passage,
            *[whole((piece, depth + STATS)) for _ in range(chunk_count)],
        ],
        out_specs=(
            *[whole((piece, depth)) for _ in range(chunk_count)],
            whole((rows, depth)),
            passage,
            passage,
        ),
        scratch_shapes=[
            pltpu.VMEM((blk_count, pairs, 2 * rows, PAIR), bf16),
            pltpu.VMEM((blk_count, pairs, 2 * rows, PAIR), bf16),
            pltpu.VMEM((blk_count, STATS, rows), f32),
            pltpu.VMEM((rows, depth), bf16),
            pltpu.VMEM((rows, STATS), f32),
            pltpu.VMEM((blk_count, rows, depth), f32),
        ],
    )
    return pl.pallas_call(
        functools.partial(cross_backward_kernel, blk_count, head_count, width),
        out_shape=(
            *[shaped((piece, depth), f32) for _ in range(chunk_count)],
            shaped((rows, depth), bf16),
            shaped(keys.shape, bf16),
            shaped(keys.shape, bf16),
        ),
        grid_spec=grid,
        compiler_params=pltpu.CompilerParams(
            vmem_limit_bytes=56 * 1024 * 1024, dimension_semantics=("arbitrary",)
        ),
    )(slots, lengths, me, queries, c_out, keys, values, *chunks)


def first_kernel(chunk_count, me_ref, *refs):
    chunks = refs[:chunk_count]
    first_ref, gain_ref, c_query_ref, second_grad_ref, grad_ref, gain_grad_ref, message_ref = refs[
        chunk_count:
    ]
    piece, depth = grad_ref.shape
    grad_q = sum(chunk[...] for chunk in chunks).astype(bf16)
    upstream = nn(grad_q, c_query_ref[...])
    first = first_ref[rows_of(me_ref[0], piece), :]
    grad, gain_grad_ref[...] = norm_back(upstream, first, gain_ref[...].astype(f32))
    grad = second_grad_ref[...] + grad
    grad_ref[...] = grad
    message_ref[:, :depth] = grad.astype(bf16)
    message_ref[:, depth:] = grad_q


def self_back_kernel(head_count, len_ref, me_ref, *refs):
    chunks = refs[:head_count]
    w_out_ref, qkv_ref, wq_ref, wk_ref, wv_ref = refs[head_count : head_count + 5]
    grads = refs[head_count + 5 : 2 * head_count + 5]
    branch_ref, cols_ref, grad_qkv_ref, total = refs[2 * head_count + 5 :]
    rows, depth = branch_ref.shape
    width = wq_ref.shape[0]
    piece = rows // head_count
    for k, chunk in enumerate(chunks):
        mine = rows_of(me_ref[0] ^ k, piece)
        branch_ref[mine, :] = chunk[:, :depth]
        cols_ref[mine, :] = chunk[:, depth + k * width : depth + (k + 1) * width]
    grad_self = nt(branch_ref[...], w_out_ref[...]).astype(bf16)
    at_q = lax.broadcasted_iota(jnp.int32, (rows, rows), 0)
    at_k = lax.broadcasted_iota(jnp.int32, (rows, rows), 1)
    allowed = (at_k <= at_q) & (at_k < len_ref[0])
    grad_q, grad_k, grad_v = [], [], []
    for h in range(width // DHEAD):
        o = h * DHEAD
        q = qkv_ref[:, o : o + DHEAD]
        k = qkv_ref[:, width + o : width + o + DHEAD]
        v = qkv_ref[:, 2 * width + o : 2 * width + o + DHEAD]
        g = grad_self[:, o : o + DHEAD]
        scores = jnp.where(allowed, nt(q, k), masked_score)
        raised = jnp.exp(scores - jnp.max(scores, axis=-1, keepdims=True))
        probs = raised / jnp.sum(raised, axis=-1, keepdims=True)
        grad_probs = nt(g, v)
        delta = jnp.sum(probs * grad_probs, axis=-1, keepdims=True)
        grad_scores = (probs * (grad_probs - delta)).astype(bf16)
        grad_q.append(nn(grad_scores, k))
        grad_k.append(tn(grad_scores, q))
        grad_v.append(tn(probs.astype(bf16), g))
    for i, parts in enumerate((grad_q, grad_k, grad_v)):
        grad_qkv_ref[:, i * width : (i + 1) * width] = jnp.concatenate(parts, axis=1).astype(bf16)
    total[...] = (
        nn(grad_qkv_ref[:, :width], wq_ref[...])
        + nn(grad_qkv_ref[:, width : 2 * width], wk_ref[...])
        + nn(grad_qkv_ref[:, 2 * width :], wv_ref[...])
    )
    for k, grad in enumerate(grads):
        grad[...] = total[rows_of(me_ref[0] ^ k, piece), :]


def input_kernel(head_count, me_ref, *refs):
    chunks = refs[:head_count]
    dec_ref, gain_ref, first_grad_ref, grad_ref, gain_grad_ref = refs[head_count:]
    piece, depth = grad_ref.shape
    upstream = sum(chunk[...] for chunk in chunks)
    values = dec_ref[rows_of(me_ref[0], piece), :].astype(f32)
    grad, gain_grad_ref[...] = norm_back(upstream, values, gain_ref[...].astype(f32))
    grad_ref[...] = first_grad_ref[...] + grad


def place_kernel(head_count, me_ref, *refs):
    out_ref = refs[head_count]
    for k in range(head_count):
        out_ref[rows_of(me_ref[0] ^ k, refs[k].shape[0]), :] = refs[k][...]


def partner(array, axis, by):
    size = lax.axis_size(axis)
    return lax.ppermute(array, axis, [(i, i ^ by) for i in range(size)])


def group_gather(array, count):
    return [array] + [partner(array, ("blk", "head"), k) for k in range(1, count)]


def group_exchange(arrays):
    return [arrays[0]] + [partner(arrays[k], ("blk", "head"), k) for k in range(1, len(arrays))]


def head_gather(array):
    return [array] + [partner(array, "head", k) for k in range(1, lax.axis_size("head"))]


def head_exchange(arrays):
    return [arrays[0]] + [partner(arrays[k], "head", k) for k in range(1, len(arrays))]


def gather_pair(one, two, core):
    mine = jnp.where(core == 0, one, two)
    half = mine.shape[0] // 2
    near = partner(mine, "head", 1)
    far = partner(mine, "head", 3)
    lower = partner(far[:half], "head", 1)
    upper = partner(near[half:], "head", 3)
    whole = jnp.concatenate([mine, near, lower, upper, far], axis=0)
    other = partner(whole, "dp", 1)
    return jnp.where(core == 0, whole, other), jnp.where(core == 0, other, whole)


def plane_gather(array):
    array = jnp.concatenate([array, partner(array, "blk", 1)], axis=0)
    array = jnp.concatenate([array, partner(array, "dp", 2)], axis=0)
    return array, partner(array, "dp", 1)


def weight_grad(left, right):
    return sum(tn(a, b) for a, b in zip(left, right))


def body(
    dec_in,
    enc_out,
    passage_len,
    dec_len,
    passage_owner,
    gain_self,
    gain_cross,
    gain_ffn,
    w_query,
    w_key,
    w_value,
    w_out,
    c_query,
    c_key,
    c_value,
    c_out,
    w_in,
    w_back,
    cotangent,
):
    blk_count = lax.axis_size("blk")
    dp_count = lax.axis_size("dp")
    head_count = lax.axis_size("head")
    small = blk_count * dp_count == 8
    chunk_count = blk_count * head_count
    width, depth = w_query.shape
    rows = dec_in.shape[0]
    piece = rows // head_count
    passages = enc_out.shape[0] // LP
    head_place = lax.axis_index("head")
    blk_place = lax.axis_index("blk")
    core = lax.axis_index("dp") % 2
    me = head_place.astype(jnp.int32).reshape(1)
    gain_one = gain_self.reshape(1, depth)
    gain_two = gain_cross.reshape(1, depth)
    gain_three = gain_ffn.reshape(1, depth)

    key_full, value_full = gather_pair(c_key, c_value, core)
    out_full, query_full = gather_pair(w_out, c_query, core)
    cross_out_full, _ = gather_pair(c_out, c_out, core)

    slots = lax.dynamic_slice_in_dim(passage_owner, head_place * passages, passages) ^ blk_place
    lengths = lax.dynamic_slice_in_dim(passage_len, head_place * passages, passages)

    normed_one, self_qkv, self_flat = call(
        self_kernel,
        [shaped((rows, depth), bf16), shaped((rows, 3 * width), bf16), shaped((rows, width), bf16)],
        [dec_len],
        [dec_in, gain_one, w_query, w_key, w_value],
    )
    decs = [dec_in] + [partner(dec_in, "blk", k) for k in range(1, blk_count)]
    self_chunks = group_gather(self_flat, chunk_count)
    first, normed_two, queries = call(
        functools.partial(query_kernel, blk_count, head_count),
        [
            shaped((rows, depth), f32),
            shaped((rows, depth), bf16),
            shaped((blk_count, rows, depth), bf16),
        ],
        [],
        [*self_chunks, *decs, out_full, query_full, gain_two],
    )
    enc_keys = nt(enc_out, key_full).astype(bf16)
    enc_values_t = nt(value_full, enc_out).astype(bf16)
    enc_values = nt(enc_out, value_full).astype(bf16)

    partials = cross_forward(
        slots, lengths, me, queries, enc_keys, enc_values_t, head_count, width
    )
    partials = group_exchange(partials)
    cross, second, logsum, message = call(
        functools.partial(combine_kernel, chunk_count),
        [
            shaped((piece, depth), f32),
            shaped((piece, depth), f32),
            shaped((piece, STATS), f32),
            shaped((piece, 2 * depth), bf16),
        ],
        [me],
        [*partials, first, cross_out_full, gain_three],
    )
    messages = head_gather(message)
    outs = call(
        functools.partial(ffn_kernel, head_count, width),
        [shaped((piece, depth), f32)] * head_count
        + [
            shaped((rows, depth), bf16),
            shaped((rows, w_in.shape[1]), bf16),
            shaped((rows, w_in.shape[1]), bf16),
            shaped((rows, width), bf16),
            shaped((rows, depth), f32),
        ],
        [me],
        [*messages, cotangent, w_in, w_back],
        [pltpu.VMEM((rows, depth), f32)],
    )
    normed_three, hidden, grad_pre, cross_cols, ffn_partial = outs[head_count:]
    upstream = head_exchange(outs[:head_count])
    outs = call(
        functools.partial(branch_kernel, head_count, width),
        [shaped((piece, depth), f32), shaped((1, depth), f32)]
        + [shaped((piece, depth + STATS), bf16)] * head_count,
        [me],
        [*upstream, second, gain_three, cotangent, cross_out_full, cross, logsum],
    )
    grad_second, gain_ffn_part = outs[:2]
    messages = [outs[2 + k % head_count] for k in range(chunk_count)]
    branches = group_exchange(messages)
    outs = cross_backward(
        slots,
        lengths,
        me,
        queries,
        cross_out_full,
        enc_keys,
        enc_values,
        branches,
        head_count,
        width,
    )
    branch_two, enc_key_grads, enc_value_grads = outs[chunk_count:]
    query_grads = group_exchange(outs[:chunk_count])
    grad_first, gain_cross_part, message = call(
        functools.partial(first_kernel, chunk_count),
        [shaped((piece, depth), f32), shaped((1, depth), f32), shaped((piece, 2 * depth), bf16)],
        [me],
        [*query_grads, first, gain_two, query_full, grad_second],
    )
    messages = head_gather(message)
    outs = call(
        functools.partial(self_back_kernel, head_count),
        [shaped((piece, depth), f32)] * head_count
        + [
            shaped((rows, depth), bf16),
            shaped((rows, width), bf16),
            shaped((rows, 3 * width), bf16),
        ],
        [dec_len, me],
        [*messages, w_out, self_qkv, w_query, w_key, w_value],
        [pltpu.VMEM((rows, depth), f32)],
    )
    branch_one, grad_query_cols, grad_qkv = outs[head_count:]
    upstream = head_exchange(outs[:head_count])
    grad_in_rows, gain_self_part = call(
        functools.partial(input_kernel, head_count),
        [shaped((piece, depth), f32), shaped((1, depth), f32)],
        [me],
        [*upstream, dec_in, gain_one, grad_first],
    )
    (grad_in,) = call(
        functools.partial(place_kernel, head_count),
        [shaped((rows, depth), f32)],
        [me],
        head_gather(grad_in_rows),
    )

    layer_rows = lax.psum(ffn_partial, "head")
    (second_all,) = call(
        functools.partial(place_kernel, head_count),
        [shaped((rows, depth), f32)],
        [me],
        head_gather(second),
    )
    layer_out = (second_all + layer_rows).astype(bf16)

    grad_enc = nn(enc_key_grads, key_full) + nn(enc_value_grads, value_full)

    key_part = tn(enc_key_grads, enc_out).astype(bf16)
    value_part = tn(enc_value_grads, enc_out).astype(bf16)
    theirs = partner(jnp.where(core == 0, value_part, key_part), "dp", 1)
    own = jnp.where(core == 0, key_part, value_part).astype(f32) + theirs.astype(f32)
    own = own.astype(bf16).reshape(head_count, width, depth)
    shares = head_exchange([own[k] for k in range(head_count)])
    share = sum(part.astype(f32) for part in shares)
    for bit in range(1, dp_count.bit_length() - 1):
        share = share + partner(share.astype(bf16), "dp", 2**bit).astype(f32)
    for bit in range(blk_count.bit_length() - 1):
        share = share + partner(share.astype(bf16), "blk", 2**bit).astype(f32)
    other = partner(share, "dp", 1)
    grad_c_key = jnp.where(core == 0, share, other)
    grad_c_value = jnp.where(core == 0, other, share)

    if small:
        together = plane_gather
    else:
        together = lambda array: (array,)
    early = together(jnp.concatenate([normed_one, cotangent], axis=1))
    later = together(jnp.concatenate([normed_two, self_flat], axis=1))
    middle = together(jnp.concatenate([normed_three, hidden, grad_pre], axis=1))
    cross_side = together(jnp.concatenate([branch_two, cross_cols], axis=1))
    self_side = together(jnp.concatenate([branch_one, grad_query_cols], axis=1))
    last = together(grad_qkv)
    cols = lambda arrays, start, count: [array[:, start : start + count] for array in arrays]
    hidden_width = w_in.shape[1]
    sums = [
        weight_grad(last, cols(early, 0, depth)),
        weight_grad(cols(later, depth, width), cols(self_side, 0, depth)),
        weight_grad(cols(self_side, depth, width), cols(later, 0, depth)),
        weight_grad(cols(cross_side, depth, width), cols(cross_side, 0, depth)),
        weight_grad(cols(middle, 0, depth), cols(middle, depth + hidden_width, hidden_width)),
        weight_grad(cols(middle, depth, hidden_width), cols(early, depth, depth)),
    ]
    if not small:
        sums = lax.psum(tuple(sums), ("dp", "blk"))
    gains = lax.psum(
        jnp.concatenate([gain_self_part, gain_cross_part, gain_ffn_part], axis=0),
        ("dp", "blk", "head"),
    )
    return (
        layer_out,
        grad_in,
        grad_enc,
        gains[0],
        gains[1],
        gains[2],
        sums[0][:width],
        sums[0][width : 2 * width],
        sums[0][2 * width :],
        sums[1],
        sums[2],
        grad_c_key,
        grad_c_value,
        sums[3],
        sums[4],
        sums[5],
    )


def solution(mesh):
    rows = P(("dp", "blk"), None)
    enc = P(("dp", "blk", "head"), None)
    each = P(("dp", "blk"))
    heads = P("head", None)
    return jax.shard_map(
        body,
        mesh=mesh,
        in_specs=(
            rows,
            enc,
            each,
            each,
            each,
            P(),
            P(),
            P(),
            *[heads] * 8,
            P(None, "head"),
            heads,
            rows,
        ),
        out_specs=(rows, rows, enc, P(), P(), P(), *[heads] * 8, P(None, "head"), heads),
        check_vma=False,
    )
```

```python
import functools

import jax
import jax.numpy as jnp
from jax import lax
from jax.experimental import pallas as pl
from jax.experimental.pallas import tpu as pltpu
from jax.sharding import PartitionSpec as P

CFG = dict(
    s_w=0, s_p=1, s_c=1, s_y=0, t_cost=0.05,
    t_late="a2a", t_rsz="perm", t_agz="perm", t_latep=0, t_sh=1, t_shq=0, t_enc=0, t_broad=0,
    cost=1.0, w_k8=1, t_cs=1, m_early=0,
)
DHEAD = 64
LP = 384
LEAST = 3 * LP // 4
norm_epsilon = 1e-06
masked_score = -1e30
bf16 = jnp.bfloat16
f32 = jnp.float32
PAIR = 2 * DHEAD
STATS = 128
SECOND_LANE = 16
SPLIT_LANE = 32
VMEM_BYTES = 60 * 1024 * 1024


def nn(left, right):
    return lax.dot_general(left, right, (((1,), (0,)), ((), ())), preferred_element_type=f32)


def nt(left, right):
    return lax.dot_general(left, right, (((1,), (1,)), ((), ())), preferred_element_type=f32)


def tn(left, right):
    return lax.dot_general(left, right, (((0,), (0,)), ((), ())), preferred_element_type=f32)


def exact_nn(left, right):
    return lax.dot_general(
        left,
        right,
        (((1,), (0,)), ((), ())),
        precision=lax.Precision.HIGHEST,
        preferred_element_type=f32,
    )


def norm_scale(values):
    return lax.rsqrt(jnp.mean(values * values, axis=-1, keepdims=True) + norm_epsilon)


def normalize(values, gain):
    return values * norm_scale(values) * gain


def norm_back(upstream, values, gain):
    scale = norm_scale(values)
    unit = values * scale
    scaled = upstream * gain
    grad = scale * (scaled - unit * jnp.mean(scaled * unit, axis=-1, keepdims=True))
    return grad, jnp.sum(upstream * unit, axis=0, keepdims=True)


def cost(micros):
    return pl.CostEstimate(flops=0, bytes_accessed=int(micros * CFG["cost"] * 3e6), transcendentals=0)


def smem():
    return pl.BlockSpec(memory_space=pltpu.SMEM)


def shaped(shape, dtype):
    return jax.ShapeDtypeStruct(shape, dtype)


def whole(shape):
    return pl.BlockSpec(shape, lambda *_: (0,) * len(shape), pipeline_mode=pl.Buffered(1))


def call(kernel, outs, scalars, arrays, scratch=(), micros=3.5):
    return pl.pallas_call(
        kernel,
        grid=(1,),
        out_shape=tuple(outs),
        in_specs=[smem()] * len(scalars) + [whole(array.shape) for array in arrays],
        out_specs=tuple(whole(out.shape) for out in outs),
        scratch_shapes=list(scratch),
        cost_estimate=cost(micros),
        compiler_params=pltpu.CompilerParams(
            vmem_limit_bytes=VMEM_BYTES, dimension_semantics=("arbitrary",)
        ),
    )(*scalars, *arrays)


def my_head():
    return lax.axis_index("head")


def my_core():
    return lax.axis_index("dp") % 2


def my_blk():
    return lax.axis_index("blk")


def my_chip():
    return lax.axis_index("dp") // 2 * 2 + lax.axis_index("blk") % 2


def pack_stats(values):
    high = values.astype(bf16).astype(f32)
    middle = (values - high).astype(bf16).astype(f32)
    lowest = values - high - middle
    return (
        high + pltpu.roll(middle, SPLIT_LANE, 1) + pltpu.roll(lowest, 2 * SPLIT_LANE, 1)
    ).astype(bf16)


def unpack_stats(packed):
    packed = packed.astype(f32)
    return (
        packed
        + pltpu.roll(packed, STATS - SPLIT_LANE, 1)
        + pltpu.roll(packed, STATS - 2 * SPLIT_LANE, 1)
    )


def group_place(head_count, kb, kh):
    return (my_blk() ^ kb) * head_count + (my_head() ^ kh)


def rows_of(place, count):
    if isinstance(place, int):
        return slice(place * count, (place + 1) * count)
    return pl.ds(pl.multiple_of(place * count, count), count)


def head_blocks(width, head_count, shift):
    return [(j ^ shift) * width for j in range(head_count)]


def permuted(values, width, head_count, shift):
    if shift == 0:
        return values
    return jnp.concatenate(
        [values[:, o : o + width] for o in head_blocks(width, head_count, shift)], axis=1
    )


def self_probs(q, k, allowed):
    scores = jnp.where(allowed, nt(q, k), masked_score)
    raised = jnp.exp(scores - jnp.max(scores, axis=-1, keepdims=True))
    return raised / jnp.sum(raised, axis=-1, keepdims=True)


def causal(rows, length):
    at_q = lax.broadcasted_iota(jnp.int32, (rows, rows), 0)
    at_k = lax.broadcasted_iota(jnp.int32, (rows, rows), 1)
    return (at_k <= at_q) & (at_k.astype(f32) < length)


def self_kernel(dec_ref, len_ref, gain_ref, wq_ref, wk_ref, wv_ref, w_out_ref, *refs):
    normed_ref, qkv_ref, out_ref, *partials = refs[:-1]
    total = refs[-1]
    rows = normed_ref.shape[0]
    width = wq_ref.shape[0]
    normed = normalize(dec_ref[...].astype(f32), gain_ref[...].astype(f32)[None, :]).astype(bf16)
    normed_ref[...] = normed
    for i, weight in enumerate((wq_ref, wk_ref, wv_ref)):
        qkv_ref[:, i * width : (i + 1) * width] = nt(normed, weight[...]).astype(bf16)
    allowed = causal(rows, len_ref[0].astype(f32))
    outs = []
    for h in range(width // DHEAD):
        o = h * DHEAD
        probs = self_probs(
            qkv_ref[:, o : o + DHEAD], qkv_ref[:, width + o : width + o + DHEAD], allowed
        )
        outs.append(nn(probs.astype(bf16), qkv_ref[:, 2 * width + o : 2 * width + o + DHEAD]))
    attended = jnp.concatenate(outs, axis=1).astype(bf16)
    out_ref[...] = attended
    total[...] = nn(attended, w_out_ref[...])
    piece = rows // len(partials)
    for k, partial in enumerate(partials):
        partial[...] = total[rows_of(my_head() ^ k, piece), :]


def call_self(dec_in, dec_len, gain, w_query, w_key, w_value, w_out, head_count):
    rows, depth = dec_in.shape
    width = w_query.shape[0]
    arrays = (dec_in, dec_len, gain, w_query, w_key, w_value, w_out)
    outs = [
        shaped((rows, depth), bf16),
        shaped((rows, 3 * width), bf16),
        shaped((rows, width), bf16),
    ] + [shaped((rows // head_count, depth), f32)] * head_count
    return pl.pallas_call(
        self_kernel,
        grid=(1,),
        out_shape=tuple(outs),
        in_specs=[smem() if array is dec_len else whole(array.shape) for array in arrays],
        out_specs=tuple(whole(out.shape) for out in outs),
        scratch_shapes=[pltpu.VMEM((rows, depth), f32)],
        cost_estimate=cost(4),
        compiler_params=pltpu.CompilerParams(
            vmem_limit_bytes=VMEM_BYTES, dimension_semantics=("arbitrary",)
        ),
    )(*arrays)


def normed_kernel(count, *refs):
    chunks = refs[:count]
    dec_ref, gain_ref, first_ref, message_ref = refs[count:]
    piece = first_ref.shape[0]
    first = dec_ref[rows_of(my_head(), piece), :].astype(f32) + sum(chunk[...] for chunk in chunks)
    first_ref[...] = first
    normed = normalize(first, gain_ref[...].astype(f32)[None, :]).astype(bf16)
    for i in range(message_ref.shape[0]):
        message_ref[i] = normed


def fill_weights(target, owns, pieces):
    count = owns[0].shape[0]
    size = count // 4
    for i, own in enumerate(owns):
        target[i, :count, :] = own[...]
    others = len(pieces) // 4
    for place, piece in enumerate(pieces):
        kind = place // others
        quarter = (my_core() ^ kind // 2) * 2 + (my_blk() % 2 ^ kind % 2)
        start = (place % others + 1) * count + quarter * size
        for i in range(len(owns)):
            target[i, pl.ds(pl.multiple_of(start, size), size), :] = piece[
                i * size : (i + 1) * size, :
            ]


def piece_spec(pieces, part, of, whole_parts):
    rows, depth = pieces[0].shape
    block = (rows // whole_parts * of, depth)
    spec = pl.BlockSpec(block, lambda *_: (part, 0), pipeline_mode=pl.Buffered(1))
    return [spec] * len(pieces)


def query_kernel(blk_count, head_count, chunks_ref, c_query_ref, one_ref, self_ref, *refs):
    pieces, (early_ref, q_ref, full_ref, weights, normed) = refs[:-5], refs[-5:]
    rows, depth = one_ref.shape
    width = self_ref.shape[1]
    piece = rows // head_count
    fill_weights(weights, (c_query_ref,), pieces)
    full_ref[...] = weights[0]
    for kb in range(blk_count):
        for i in range(head_count):
            place = (my_blk() ^ kb) * head_count + i
            normed[i * piece : (i + 1) * piece, :] = chunks_ref[place]
        if kb == 0:
            early_ref[:, :depth] = one_ref[...]
            early_ref[:, depth : 2 * depth] = normed[...]
            early_ref[:, 2 * depth : 2 * depth + width] = self_ref[...]
            early_ref[:, 2 * depth + width :] = jnp.zeros(
                (rows, early_ref.shape[1] - 2 * depth - width), bf16
            )
        q_ref[kb] = nt(normed[...], weights[0]).astype(bf16)


def make_queries(chunks, c_query, normed_one, self_flat, pieces, blk_count, head_count):
    rows, depth = normed_one.shape
    width = self_flat.shape[1]
    outs = (
        shaped((rows, -(-(2 * depth + width) // 256) * 256), bf16),
        shaped((blk_count, rows, depth), bf16),
        shaped((depth, depth), bf16),
    )
    arrays = (chunks, c_query, normed_one, self_flat)
    return pl.pallas_call(
        functools.partial(query_kernel, blk_count, head_count),
        grid=(1,),
        out_shape=outs,
        in_specs=[whole(array.shape) for array in arrays] + piece_spec(pieces, 2, 1, 3),
        out_specs=tuple(whole(out.shape) for out in outs),
        scratch_shapes=[pltpu.VMEM((1, depth, depth), bf16), pltpu.VMEM((rows, depth), bf16)],
        cost_estimate=cost(4),
        compiler_params=pltpu.CompilerParams(
            vmem_limit_bytes=VMEM_BYTES, dimension_semantics=("arbitrary",)
        ),
    )(*arrays, *pieces)


def project_kernel(enc_ref, *refs):
    owns, pieces = refs[:2], refs[2:-5]
    key_ref, value_ref, key_full_ref, value_full_ref, weights = refs[-5:]

    @pl.when(pl.program_id(0) == 0)
    def _():
        fill_weights(weights, owns, pieces)
        key_full_ref[...] = weights[0]
        value_full_ref[...] = weights[1]

    key_ref[...] = nt(enc_ref[...], weights[0]).astype(bf16)
    value_ref[...] = nt(enc_ref[...], weights[1]).astype(bf16)


def project(enc, owns, pieces):
    slots, depth = enc.shape
    block = pl.BlockSpec((LP, depth), lambda p: (p, 0))
    full = shaped((depth, depth), bf16)
    return pl.pallas_call(
        project_kernel,
        grid=(slots // LP,),
        in_specs=[block] + [whole(w.shape) for w in owns] + piece_spec(pieces, 0, 2, 3),
        out_specs=(block, block, whole(full.shape), whole(full.shape)),
        out_shape=(shaped(enc.shape, bf16), shaped(enc.shape, bf16), full, full),
        scratch_shapes=[pltpu.VMEM((2, depth, depth), bf16)],
        cost_estimate=cost(9),
        compiler_params=pltpu.CompilerParams(
            vmem_limit_bytes=VMEM_BYTES, dimension_semantics=("arbitrary",)
        ),
    )(enc, *owns, *pieces)


def assemble_kernel(own_ref, *refs):
    out_ref = refs[-1]
    others = (len(refs) - 1) // 2
    count = own_ref.shape[0]
    half = count // 2
    out_ref[:count, :] = own_ref[...]
    for k in range(others):
        start = (k + 1) * count
        out_ref[rows_of(start // half + my_core(), half), :] = refs[k][...]
        out_ref[rows_of(start // half + 1 - my_core(), half), :] = refs[others + k][...]


def spread_pairs(values, target, kb):
    rows = values.shape[0]
    for j in range(values.shape[1] // PAIR):
        pair = values[:, j * PAIR : (j + 1) * PAIR]
        lane = lax.broadcasted_iota(jnp.int32, pair.shape, 1)
        zero = jnp.zeros_like(pair)
        target[kb, j, 0:rows, :] = jnp.where(lane < DHEAD, pair, zero)
        target[kb, j, rows : 2 * rows, :] = jnp.where(lane < DHEAD, zero, pair)


def within(values, length, fill):
    place = LEAST + lax.broadcasted_iota(jnp.int32, (LP - LEAST, values.shape[1]), 0)
    last = jnp.where(place < length, values[LEAST:], fill)
    return jnp.concatenate([values[:LEAST], last], axis=0)


def pair_columns(j):
    return slice(j * PAIR, (j + 1) * PAIR)


def add_pair(target, slot, j, update, factor=None):
    rows = target.shape[2]
    for i in range(2):
        span = slice(j * PAIR + i * DHEAD, j * PAIR + (i + 1) * DHEAD)
        own = update[i * DHEAD : (i + 1) * DHEAD, i * rows : (i + 1) * rows]
        old = target[slot, span, :]
        if factor is not None:
            old = old * factor[:, i * rows : (i + 1) * rows]
        target[slot, span, :] = old + own


def cross_forward_kernel(blk_count, head_count, width, *refs):
    slot_ref, len_ref, q_ref, k_ref, v_ref = refs[:5]
    out_ref, q2, acc, highest, totals, stat, flat, flat_stat, held, probs, factors = refs[5:]
    rows, depth = q_ref.shape[1], q_ref.shape[2]
    pairs = depth // PAIR
    step = pl.program_id(0)

    @pl.when(step == 0)
    def _():
        for kb in range(blk_count):
            spread_pairs(q_ref[kb], q2, kb)
        highest[...] = jnp.full(highest.shape, masked_score, f32)
        totals[...] = jnp.zeros(totals.shape, f32)
        acc[...] = jnp.zeros(acc.shape, f32)

    slot = slot_ref[step]
    for j in range(pairs):
        scores = within(nt(k_ref[:, pair_columns(j)], q2[slot, j]), len_ref[step], masked_score)
        held[j] = scores
        before = highest[slot, j : j + 1, :]
        newest = jnp.maximum(before, jnp.max(scores, axis=0, keepdims=True))
        factors[j : j + 1, :] = jnp.exp(before - newest)
        highest[slot, j : j + 1, :] = newest
    for j in range(pairs):
        raised = jnp.exp(held[j] - highest[slot, j : j + 1, :])
        probs[j] = raised.astype(bf16)
        totals[slot, j : j + 1, :] = totals[slot, j : j + 1, :] * factors[
            j : j + 1, :
        ] + jnp.sum(raised, axis=0, keepdims=True)
    for j in range(pairs):
        update = tn(v_ref[:, pair_columns(j)], probs[j])
        add_pair(acc, slot, j, update, factors[j : j + 1, :])

    @pl.when(step == pl.num_programs(0) - 1)
    def _():
        stat[...] = jnp.zeros(stat.shape, f32)
        piece = rows // head_count
        per = width // DHEAD
        for kb in range(blk_count):
            flat[...] = acc[kb].T
            for kh in range(head_count):
                for head in range(depth // DHEAD):
                    at = ((head // per) ^ kh) * per + head % per
                    lanes = slice((head % 2) * rows, (head % 2 + 1) * rows)
                    stat[at : at + 1, :] = highest[kb, head // 2 : head // 2 + 1, lanes]
                    stat[SECOND_LANE + at : SECOND_LANE + at + 1, :] = totals[
                        kb, head // 2 : head // 2 + 1, lanes
                    ]
                flat_stat[...] = stat[...].T
                mine = rows_of(my_head() ^ kh, piece)
                place = group_place(head_count, kb, kh)
                out_ref[place, :, :depth] = permuted(
                    flat[mine, :].astype(bf16), width, head_count, kh
                )
                out_ref[place, :, depth:] = pack_stats(flat_stat[mine, :])


def cross_forward(slots, lengths, queries, keys, values, head_count, width):
    blk_count, rows, depth = queries.shape
    passages = slots.shape[0]
    piece = rows // head_count
    chunk_count = blk_count * head_count
    pairs = depth // PAIR
    grid = pltpu.PrefetchScalarGridSpec(
        num_scalar_prefetch=2,
        grid=(passages,),
        in_specs=[
            whole((blk_count, rows, depth)),
            pl.BlockSpec((LP, depth), lambda p, *_: (p, 0)),
            pl.BlockSpec((LP, depth), lambda p, *_: (p, 0)),
        ],
        out_specs=whole((chunk_count, piece, depth + STATS)),
        scratch_shapes=[
            pltpu.VMEM((blk_count, pairs, 2 * rows, PAIR), bf16),
            pltpu.VMEM((blk_count, depth, rows), f32),
            pltpu.VMEM((blk_count, 8, 2 * rows), f32),
            pltpu.VMEM((blk_count, 8, 2 * rows), f32),
            pltpu.VMEM((STATS, rows), f32),
            pltpu.VMEM((rows, depth), f32),
            pltpu.VMEM((rows, STATS), f32),
            pltpu.VMEM((pairs, LP, 2 * rows), f32),
            pltpu.VMEM((pairs, LP, 2 * rows), bf16),
            pltpu.VMEM((8, 2 * rows), f32),
        ],
    )
    return pl.pallas_call(
        functools.partial(cross_forward_kernel, blk_count, head_count, width),
        out_shape=shaped((chunk_count, piece, depth + STATS), bf16),
        cost_estimate=cost(15),
        grid_spec=grid,
        compiler_params=pltpu.CompilerParams(
            vmem_limit_bytes=VMEM_BYTES, dimension_semantics=("arbitrary",)
        ),
    )(slots, lengths, queries, keys, values)


def head_matrix(depth):
    head = lax.broadcasted_iota(jnp.int32, (STATS, depth), 0)
    column = lax.broadcasted_iota(jnp.int32, (STATS, depth), 1)
    return (head == column // DHEAD).astype(f32)


def combine_kernel(width, *refs):
    chunks, first_ref, c_out_ref, gain_ref, cross_ref, second_ref, logsum_ref = refs[:7]
    messages = refs[7:]
    piece, depth = cross_ref.shape
    stats = [unpack_stats(chunks[i, :, depth:]) for i in range(chunks.shape[0])]
    highest = stats[0]
    for other in stats[1:]:
        highest = jnp.maximum(highest, other)
    lane = lax.broadcasted_iota(jnp.int32, (piece, STATS), 1)
    real = lane < depth // DHEAD
    weights = [jnp.where(real, jnp.exp(one - highest), 0.0) for one in stats]
    total = sum(w * pltpu.roll(one, STATS - SECOND_LANE, 1) for w, one in zip(weights, stats))
    total = jnp.where(real, total, 1.0)
    logsum_ref[...] = jnp.where(real, highest + jnp.log(total), 0.0)
    spread = head_matrix(depth)
    weighted = exact_nn(jnp.concatenate(weights, axis=0), spread)
    cross = sum(
        chunks[i, :, :depth].astype(f32) * weighted[i * piece : (i + 1) * piece]
        for i in range(chunks.shape[0])
    )
    cross = cross / exact_nn(total, spread)
    cross_ref[...] = cross
    rounded = cross.astype(bf16)
    second = first_ref[...] + nn(rounded, c_out_ref[...])
    second_ref[...] = second
    normed = normalize(second, gain_ref[...].astype(f32)[None, :]).astype(bf16)
    for k, message in enumerate(messages):
        message[:, :depth] = normed
        message[:, depth:] = rounded[:, k * width : (k + 1) * width]


def ffn_kernel(count, *refs):
    chunks = refs[:count]
    cot_ref, w_in_ref, w_back_ref = refs[count : count + 3]
    grads = refs[count + 3 : 2 * count + 3]
    layer_ref, wide_ref, cols_ref, total = refs[2 * count + 3 :]
    piece, depth = grads[0].shape
    for k, chunk in enumerate(chunks):
        mine = rows_of(my_head() ^ k, piece)
        wide_ref[mine, :depth] = chunk[:, :depth]
        cols_ref[mine, :] = chunk[:, depth:]
    units = w_in_ref.shape[1]
    before = nn(wide_ref[:, :depth], w_in_ref[...])
    root = 0.7978845608028654
    cube = 0.044715
    square = before * before
    bend = jnp.tanh(root * (before + cube * before * square))
    hidden = (0.5 * before * (1.0 + bend)).astype(bf16)
    slope = 0.5 * (1.0 + bend) + 0.5 * before * (1.0 - bend * bend) * root * (
        1.0 + 3.0 * cube * square
    )
    pre_grad = (nt(cot_ref[...], w_back_ref[...]) * slope).astype(bf16)
    total[...] = nt(pre_grad, w_in_ref[...])
    wide_ref[:, depth : depth + units] = hidden
    wide_ref[:, depth + units : depth + 2 * units] = pre_grad
    wide_ref[:, depth + 2 * units :] = cot_ref[...]
    for k, grad in enumerate(grads):
        grad[...] = total[rows_of(my_head() ^ k, piece), :]
    total[...] = nn(hidden, w_back_ref[...])
    for i in range(count):
        layer_ref[i] = total[i * piece : (i + 1) * piece, :]


def branch_kernel(head_count, width, *refs):
    chunks = refs[:head_count]
    second_ref, gain_ref, cot_ref, c_out_ref, cross_ref, logsum_ref = refs[
        head_count : head_count + 6
    ]
    grad_ref, gain_grad_ref, message_ref = refs[head_count + 6 :]
    piece, depth = second_ref.shape
    upstream = sum(chunk[...] for chunk in chunks)
    grad, gain_grad_ref[...] = norm_back(upstream, second_ref[...], gain_ref[...].astype(f32)[None, :])
    grad = cot_ref[rows_of(my_head(), piece), :].astype(f32) + grad
    grad_ref[...] = grad
    branch = grad.astype(bf16)
    grad_cross = nt(branch, c_out_ref[...]).astype(bf16).astype(f32)
    spread = head_matrix(depth)
    deltas = lax.dot_general(
        grad_cross * cross_ref[...],
        spread,
        (((1,), (1,)), ((), ())),
        precision=lax.Precision.HIGHEST,
        preferred_element_type=f32,
    )
    stats = logsum_ref[...] + pltpu.roll(deltas, SECOND_LANE, 1)
    per = width // DHEAD
    heads = depth // DHEAD
    source = lax.broadcasted_iota(jnp.int32, (STATS, STATS), 0)
    target = lax.broadcasted_iota(jnp.int32, (STATS, STATS), 1)
    place = source % SECOND_LANE
    for k in range(head_count):
        moved = (source - place) + ((place // per) ^ k) * per + place % per
        shuffle = ((target == moved) & (place < heads) & (source < 2 * SECOND_LANE)).astype(f32)
        aligned = exact_nn(stats, shuffle)
        packed = pack_stats(aligned)
        for kb in range(message_ref.shape[0] // head_count):
            entry = group_place(head_count, kb, k)
            message_ref[entry, :, :depth] = branch
            message_ref[entry, :, depth:] = packed


def cross_backward_kernel(blk_count, head_count, width, *refs):
    slot_ref, len_ref, q_ref, c_out_ref, k_ref, v_ref = refs[:6]
    chunks, out_ref, branch_ref, grad_k_ref, grad_v_ref = refs[6:11]
    q2, g2, stats, branch, flat_stat, grad_q, flat = refs[11:18]
    held, grad_probs, probs, grad_scores = refs[18:]
    rows, depth = q_ref.shape[1], q_ref.shape[2]
    pairs = depth // PAIR
    piece = rows // head_count
    step = pl.program_id(0)

    @pl.when(step == 0)
    def _():
        for kb in range(blk_count):
            for i in range(head_count):
                place = (my_blk() ^ kb) * head_count + i
                span = slice(i * piece, (i + 1) * piece)
                branch[span, :] = chunks[place, :, :depth]
                flat_stat[span, :] = unpack_stats(chunks[place, :, depth:])
            if kb == 0:
                branch_ref[...] = branch[...]
            stats[kb] = flat_stat[...].T
            spread_pairs(q_ref[kb], q2, kb)
            spread_pairs(nt(branch[...], c_out_ref[...]).astype(bf16), g2, kb)
        grad_q[...] = jnp.zeros(grad_q.shape, f32)

    slot = slot_ref[step]

    def both_heads(first):
        return jnp.concatenate(
            [stats[slot, first : first + 1, :], stats[slot, first + 1 : first + 2, :]], axis=1
        )

    for j in range(pairs):
        held[j] = nt(k_ref[:, pair_columns(j)], q2[slot, j])
        grad_probs[j] = nt(v_ref[:, pair_columns(j)], g2[slot, j])
    for j in range(pairs):
        raised = within(jnp.exp(held[j] - both_heads(2 * j)), len_ref[step], 0.0)
        probs[j] = raised.astype(bf16)
        grad_scores[j] = (raised * (grad_probs[j] - both_heads(SECOND_LANE + 2 * j))).astype(bf16)
    for j in range(pairs):
        grad_v_ref[:, pair_columns(j)] = nn(probs[j], g2[slot, j]).astype(bf16)
        grad_k_ref[:, pair_columns(j)] = nn(grad_scores[j], q2[slot, j]).astype(bf16)
        add_pair(grad_q, slot, j, tn(k_ref[:, pair_columns(j)], grad_scores[j]))

    @pl.when(step == pl.num_programs(0) - 1)
    def _():
        for kb in range(blk_count):
            flat[...] = grad_q[kb].T
            for kh in range(head_count):
                mine = rows_of(my_head() ^ kh, piece)
                out_ref[group_place(head_count, kb, kh)] = permuted(
                    flat[mine, :].astype(bf16), width, head_count, kh
                )


def cross_backward(slots, lengths, queries, c_out, keys, values, chunks, head_count, width):
    blk_count, rows, depth = queries.shape
    passages = slots.shape[0]
    piece = rows // head_count
    chunk_count = blk_count * head_count
    pairs = depth // PAIR
    passage = pl.BlockSpec((LP, depth), lambda p, *_: (p, 0))
    grid = pltpu.PrefetchScalarGridSpec(
        num_scalar_prefetch=2,
        grid=(passages,),
        in_specs=[
            whole((blk_count, rows, depth)),
            whole((depth, depth)),
            passage,
            passage,
            whole(chunks.shape),
        ],
        out_specs=(
            whole((chunk_count, piece, depth)),
            whole((rows, depth)),
            passage,
            passage,
        ),
        scratch_shapes=[
            pltpu.VMEM((blk_count, pairs, 2 * rows, PAIR), bf16),
            pltpu.VMEM((blk_count, pairs, 2 * rows, PAIR), bf16),
            pltpu.VMEM((blk_count, STATS, rows), f32),
            pltpu.VMEM((rows, depth), bf16),
            pltpu.VMEM((rows, STATS), f32),
            pltpu.VMEM((blk_count, depth, rows), f32),
            pltpu.VMEM((rows, depth), f32),
            pltpu.VMEM((pairs, LP, 2 * rows), f32),
            pltpu.VMEM((pairs, LP, 2 * rows), f32),
            pltpu.VMEM((pairs, LP, 2 * rows), bf16),
            pltpu.VMEM((pairs, LP, 2 * rows), bf16),
        ],
    )
    return pl.pallas_call(
        functools.partial(cross_backward_kernel, blk_count, head_count, width),
        out_shape=(
            shaped((chunk_count, piece, depth), bf16),
            shaped((rows, depth), bf16),
            shaped(keys.shape, bf16),
            shaped(keys.shape, bf16),
        ),
        cost_estimate=cost(16),
        grid_spec=grid,
        compiler_params=pltpu.CompilerParams(
            vmem_limit_bytes=VMEM_BYTES, dimension_semantics=("arbitrary",)
        ),
    )(slots, lengths, queries, c_out, keys, values, chunks)


def first_kernel(count, *refs):
    chunks, first_ref, gain_ref, c_query_ref, second_grad_ref, second_ref = refs[:6]
    layer_ref, grad_ref, gain_grad_ref = refs[6:9]
    messages = refs[9:]
    piece, depth = grad_ref.shape
    width = messages[0].shape[1] - 2 * depth
    layer = (second_ref[...] + sum(layer_ref[i] for i in range(count))).astype(bf16)
    grad_q = sum(chunks[i].astype(f32) for i in range(chunks.shape[0])).astype(bf16)
    upstream = nn(grad_q, c_query_ref[...])
    grad, gain_grad_ref[...] = norm_back(upstream, first_ref[...], gain_ref[...].astype(f32)[None, :])
    grad = second_grad_ref[...] + grad
    grad_ref[...] = grad
    branch = grad.astype(bf16)
    for k, message in enumerate(messages):
        message[:, :depth] = branch
        message[:, depth : depth + width] = grad_q[:, k * width : (k + 1) * width]
        message[:, depth + width :] = layer


def self_back_kernel(count, len_ref, *refs):
    chunks = refs[:count]
    w_out_ref, qkv_ref, wq_ref, wk_ref, wv_ref = refs[count : count + 5]
    grads, (sides_ref, layer_ref, total, side_ref) = refs[count + 5 : -4], refs[-4:]
    width, depth = wq_ref.shape
    rows = side_ref.shape[0]
    piece = rows // count
    start = depth + width
    for k, chunk in enumerate(chunks):
        mine = rows_of(my_head() ^ k, piece)
        side_ref[mine, :start] = chunk[:, :start]
        layer_ref[mine, :] = chunk[:, start:]
    grad_self = nt(side_ref[:, :depth], w_out_ref[...]).astype(bf16)
    allowed = causal(rows, len_ref[0].astype(f32))
    grad_q, grad_k, grad_v = [], [], []
    for h in range(width // DHEAD):
        o = h * DHEAD
        q = qkv_ref[:, o : o + DHEAD]
        k = qkv_ref[:, width + o : width + o + DHEAD]
        v = qkv_ref[:, 2 * width + o : 2 * width + o + DHEAD]
        g = grad_self[:, o : o + DHEAD]
        probs = self_probs(q, k, allowed)
        grad_probs = nt(g, v)
        delta = jnp.sum(probs * grad_probs, axis=-1, keepdims=True)
        grad_scores = (probs * (grad_probs - delta)).astype(bf16)
        grad_q.append(nn(grad_scores, k))
        grad_k.append(tn(grad_scores, q))
        grad_v.append(tn(probs.astype(bf16), g))
    flat = [jnp.concatenate(parts, axis=1).astype(bf16) for parts in (grad_q, grad_k, grad_v)]
    for i, part in enumerate(flat):
        side_ref[:, start + i * width : start + (i + 1) * width] = part
    total[...] = nn(flat[0], wq_ref[...]) + nn(flat[1], wk_ref[...]) + nn(flat[2], wv_ref[...])
    if len(grads) == 1:
        for i in range(count):
            grads[0][i] = total[i * piece : (i + 1) * piece, :]
    else:
        for k, grad in enumerate(grads):
            grad[...] = total[rows_of(my_head() ^ k, piece), :]
    for i in range(sides_ref.shape[0]):
        sides_ref[i] = side_ref[...]


def input_kernel(count, *refs):
    chunks = refs[:count]
    dec_ref, gain_ref, first_grad_ref, cross_gain_ref, ffn_gain_ref, message_ref = refs[count:]
    if count == 1:
        chunks = [chunks[0].at[i] for i in range(chunks[0].shape[0])]
    piece, depth = chunks[0].shape
    upstream = sum(chunk[...] for chunk in chunks)
    values = dec_ref[rows_of(my_head(), piece), :].astype(f32)
    grad, self_gain = norm_back(upstream, values, gain_ref[...].astype(f32)[None, :])
    grad = first_grad_ref[...] + grad
    for i in range(message_ref.shape[0]):
        message_ref[i, :piece, :] = grad
        message_ref[i, piece:, :] = jnp.zeros((message_ref.shape[1] - piece, depth), f32)
        message_ref[i, piece : piece + 1, :] = self_gain
        message_ref[i, piece + 1 : piece + 2, :] = cross_gain_ref[...]
        message_ref[i, piece + 2 : piece + 3, :] = ffn_gain_ref[...]


def place_kernel(count, *refs):
    chunks, (out_ref, gain_ref) = refs[:-2], refs[-2:]
    piece = out_ref.shape[0] // count
    if len(chunks) == 1:
        chunks = [chunks[0].at[i] for i in range(count)]
        places = range(count)
    else:
        places = [my_head() ^ k for k in range(count)]
    for place, chunk in zip(places, chunks):
        out_ref[rows_of(place, piece), :] = chunk[:piece, :]
    gain_ref[...] = sum(chunk[piece:, :] for chunk in chunks)


def weight_kernel(early_count, late_count, width, *refs):
    early, late = refs[:early_count], refs[early_count : early_count + late_count]
    wq_ref, wk_ref, wv_ref, out_ref, query_ref, normed, side = refs[early_count + late_count :]
    depth = wq_ref.shape[1]
    stack_up(early, normed)
    stack_up(late, side)
    start = depth + width
    qkv = tn(side[:, start:], normed[:, :depth])
    for i, target in enumerate((wq_ref, wk_ref, wv_ref)):
        target[...] = qkv[i * width : (i + 1) * width]
    query_ref[...] = tn(side[:, depth:start], normed[:, depth : 2 * depth])
    out_ref[...] = tn(normed[:, 2 * depth : 2 * depth + width], side[:, :depth])


def stack_up(parts, target):
    start = 0
    if len(parts) == 1 and len(parts[0].shape) == 3:
        place = lax.axis_index("dp")
        entries = [(place ^ k) * 2 + (my_blk() ^ b) for k in (0, 2, 1, 3) for b in (0, 1)]
        rows = parts[0].shape[1]
        for i, entry in enumerate(entries):
            target[i * rows : (i + 1) * rows, :] = parts[0][entry]
        return
    for part in parts:
        target[start : start + part.shape[0], :] = part[...]
        start += part.shape[0]


def wide_kernel(count, *refs):
    in_ref, back_ref, stack = refs[count:]
    depth, units = in_ref.shape
    stack_up(refs[:count], stack)
    in_ref[...] = tn(stack[:, :depth], stack[:, depth + units : depth + 2 * units])
    back_ref[...] = tn(stack[:, depth : depth + units], stack[:, depth + 2 * units :])


def projection_grad_kernel(head_count, plane, *refs):
    keys_ref, values_ref, enc_ref, cols_ref, branch_ref, out_ref, total = refs
    step = pl.program_id(0)
    count, depth = total.shape
    width = cols_ref.shape[1]
    blocks = count // width

    @pl.when(step == 0)
    def _():
        cross = tn(cols_ref[...], branch_ref[...]).astype(bf16)
        if len(out_ref.shape) == 2:
            out_ref[2 * depth :, :] = cross
        else:
            size = width // plane
            for device in range(plane):
                start = depth // 4
                out_ref[device, start : start + size, :] = cross[device * size : (device + 1) * size]

    for weight, grad_ref in enumerate((keys_ref, values_ref)):
        total[...] = tn(grad_ref[...], enc_ref[...])
        if len(out_ref.shape) == 2:
            start = pl.multiple_of(weight * depth + step * count, 16)
            out_ref[pl.ds(start, count), :] = total[...].astype(bf16)
            continue
        size = width // 4
        for block in range(blocks):
            place = pl.multiple_of((step * blocks + block) * size, 16)
            for part in range(4):
                start = block * width + part * size
                device = (part // 2 * 2 + weight) * 2 + part % 2
                out_ref[device, pl.ds(place, size), :] = total[start : start + size, :].astype(bf16)


def projection_grads(key_grads, value_grads, enc, cross_cols, branch, plane, head_count):
    slots, depth = enc.shape
    width = cross_cols.shape[1]
    steps = 2
    block = pl.BlockSpec((slots, depth // steps), lambda j: (0, j))
    if plane == 8:
        out = shaped((plane, -(-(depth // 4 + width // plane) // 16) * 16, depth), bf16)
    else:
        out = shaped((2 * depth + width, depth), bf16)
    return pl.pallas_call(
        functools.partial(projection_grad_kernel, head_count, plane),
        grid=(steps,),
        in_specs=[block, block, whole(enc.shape), whole(cross_cols.shape), whole(branch.shape)],
        out_specs=whole(out.shape),
        out_shape=out,
        scratch_shapes=[pltpu.VMEM((depth // steps, depth), f32)],
        cost_estimate=cost(4),
        compiler_params=pltpu.CompilerParams(
            vmem_limit_bytes=VMEM_BYTES, dimension_semantics=("arbitrary",)
        ),
    )(key_grads, value_grads, enc, cross_cols, branch)


def encoder_grad_kernel(keys_ref, values_ref, key_ref, value_ref, out_ref):
    out_ref[...] = nn(keys_ref[...], key_ref[...]) + nn(values_ref[...], value_ref[...])


def encoder_grads(key_grads, value_grads, key_full, value_full):
    slots, depth = key_grads.shape
    block = pl.BlockSpec((LP, depth), lambda p: (p, 0))
    return pl.pallas_call(
        encoder_grad_kernel,
        grid=(slots // LP,),
        in_specs=[block, block, whole(key_full.shape), whole(value_full.shape)],
        out_specs=block,
        out_shape=shaped((slots, depth), f32),
        cost_estimate=cost(7 * CFG["t_cost"]),
        compiler_params=pltpu.CompilerParams(
            vmem_limit_bytes=VMEM_BYTES, dimension_semantics=("arbitrary",)
        ),
    )(key_grads, value_grads, key_full, value_full)


def share_kernel(shares_ref, blocks_ref, cross_ref):
    count, size = blocks_ref.shape[:2]
    total = sum(shares_ref[i].astype(f32) for i in range(shares_ref.shape[0]))
    for k in range(count):
        blocks_ref[my_head() ^ k] = total[k * size : (k + 1) * size].astype(bf16)
    cross_ref[...] = total[count * size : count * size + cross_ref.shape[0]].astype(bf16)


def spread_kernel(blocks_ref, cross_ref, gains_ref, out_ref):
    size, more = blocks_ref.shape[1], cross_ref.shape[0]
    block = sum(blocks_ref[i].astype(f32) for i in range(blocks_ref.shape[0])).astype(bf16)
    pieces = []
    for i in range(3):
        rest = gains_ref[i : i + 1, :]
        for step in range(3):
            pieces.append(rest.astype(bf16).astype(f32))
            rest = rest - pieces[-1]
    fill = out_ref.shape[1] - size - more - len(pieces)
    pieces.append(jnp.zeros((fill, out_ref.shape[2]), f32))
    tail = jnp.concatenate([cross_ref[...].astype(f32), *pieces], axis=0).astype(bf16)
    for device in range(out_ref.shape[0]):
        out_ref[device, :size, :] = block
        out_ref[device, size:, :] = tail


def collect_kernel(shares_ref, key_ref, value_ref, cross_ref, gains_ref):
    plane = shares_ref.shape[0]
    size = key_ref.shape[0] // 4
    more = cross_ref.shape[0] // plane
    total = 0.0
    for device in range(plane):
        place, blk = device // 2, device % 2
        target = value_ref if place % 2 else key_ref
        part = place // 2 * 2 + blk
        share = shares_ref[device].astype(f32)
        target[part * size : (part + 1) * size, :] = share[:size]
        cross_ref[device * more : (device + 1) * more, :] = share[size : size + more]
        total = total + share[size + more :]
    for i in range(3):
        gains_ref[i : i + 1, :] = jnp.sum(total[3 * i : 3 * i + 3, :], axis=0, keepdims=True)
    gains_ref[3:, :] = jnp.zeros((gains_ref.shape[0] - 3, gains_ref.shape[1]), f32)


def after(array, *others):
    return lax.optimization_barrier((array, *others))[0]


def hold(arrays, *others):
    arrays = tuple(arrays)
    return list(lax.optimization_barrier((*arrays, *others))[: len(arrays)])


def partner(array, axis, by):
    size = lax.axis_size(axis)
    return lax.ppermute(array, axis, [(i, i ^ by) for i in range(size)])


def hold_lists(one, two):
    together = hold([*one, *two])
    return together[: len(one)], together[len(one) :]


def exchange(array, *axes):
    return lax.all_to_all(array, axes, 0, 0)


def swap_parts(parts):
    return [parts[0]] + [partner(parts[k], "head", k) for k in range(1, len(parts))]


def share_heads(array):
    return [array] + [partner(array, "head", k) for k in range(1, lax.axis_size("head"))]


def across_core(parts):
    return [partner(part, "dp", 1) for part in parts]


def to_chip(array, k):
    axis, by = [("blk", 1), ("dp", 2), (("dp", "blk"), 5)][k - 1]
    return partner(array, axis, by)


def plane_gather(array):
    chips = [array] + [to_chip(array, k) for k in (1, 2, 3)]
    return chips + across_core(chips)


def plane_gather_wide(array, beside, small):
    if not small:
        return [array]
    both = jnp.concatenate([array, beside], axis=0)
    far = partner(both, "dp", 2)
    return [both, far]


def body(
    dec_in,
    enc_out,
    passage_len,
    dec_len,
    passage_owner,
    gain_self,
    gain_cross,
    gain_ffn,
    w_query,
    w_key,
    w_value,
    w_out,
    c_query,
    c_key,
    c_value,
    c_out,
    w_in,
    w_back,
    cotangent,
):
    blk_count = lax.axis_size("blk")
    dp_count = lax.axis_size("dp")
    head_count = lax.axis_size("head")
    small = blk_count == 2 and dp_count == 4
    chunk_count = blk_count * head_count
    plane = dp_count * blk_count
    width, depth = w_query.shape
    units = w_in.shape[1]
    rows = dec_in.shape[0]
    piece = rows // head_count
    passages = enc_out.shape[0] // LP
    head_place = lax.axis_index("head")
    blk_place = lax.axis_index("blk")
    core = lax.axis_index("dp") % 2
    gain_one, gain_two, gain_three = gain_self, gain_cross, gain_ffn

    half = width // 2
    slots = lax.dynamic_slice_in_dim(passage_owner, head_place * passages, passages) ^ blk_place
    lengths = lax.dynamic_slice_in_dim(passage_len, head_place * passages, passages)

    normed_one, self_qkv, self_flat, *partials = call_self(
        dec_in, dec_len, gain_one, w_query, w_key, w_value, w_out, head_count
    )
    quarter = (core * 2 + blk_place % 2) * (width // 4)
    if CFG["s_w"] == 1:
        quarter = after(quarter, self_flat)
    pieces = jnp.concatenate(
        [
            lax.dynamic_slice_in_dim(weight, quarter, width // 4, 0)
            for weight in (c_key, c_value, c_query)
        ],
        axis=0,
    )
    pieces = [partner(pieces, "head", k) for k in range(1, head_count)]
    if CFG["s_y"] == 1:
        pieces = hold(pieces, self_flat)
    near = pieces
    beside = [partner(piece_, "blk", 1) for piece_ in pieces]
    pieces = pieces + beside + across_core(pieces) + across_core(beside)
    partials = swap_parts(partials)
    if CFG["s_p"] == 2:
        partials = hold(partials, *near)
    elif CFG["s_p"] == 3:
        partials = hold(partials, near[0])
    first, message = call(
        functools.partial(normed_kernel, head_count),
        [shaped((piece, depth), f32), shaped((chunk_count, piece, depth), bf16)],
        [],
        [*partials, dec_in, gain_two],
    )
    if CFG["s_p"] == 1:
        (message,) = hold([message], *near)
    elif CFG["s_p"] == 4:
        (message,) = hold([message], near[0])
    chunks = exchange(message, "blk", "head")
    enc_keys, enc_values, key_full, value_full = project(enc_out, (c_key, c_value), pieces)
    early, queries, query_full = make_queries(
        chunks, c_query, normed_one, self_flat, pieces, blk_count, head_count
    )
    c_gate = {0: [queries], 1: [queries, enc_keys]}[CFG["s_c"]]
    mine = lax.dynamic_slice_in_dim(c_out, after(core, *c_gate) * half, half, 0)
    cross_out = [partner(mine, "head", k) for k in range(1, head_count)]
    early_beside = partner(after(early, *c_gate), "blk", 1)

    partials = cross_forward(
        slots, lengths, queries, enc_keys, enc_values, head_count, width
    )
    partials, early_beside, *cross_out = hold([partials, early_beside, *cross_out])
    (cross_out_full,) = call(
        assemble_kernel,
        [shaped((depth, depth), bf16)],
        [],
        [c_out, *cross_out, *across_core(cross_out)],
    )
    cross, second, logsum, *messages = call(
        functools.partial(combine_kernel, width),
        [
            shaped((piece, depth), f32),
            shaped((piece, depth), f32),
            shaped((piece, STATS), f32),
        ]
        + [shaped((piece, depth + width), bf16)] * head_count,
        [],
        [exchange(partials, "blk", "head"), first, cross_out_full, gain_three],
    )
    chunks = swap_parts(messages)
    outs = call(
        functools.partial(ffn_kernel, head_count),
        [shaped((piece, depth), f32)] * head_count
        + [
            shaped((head_count, piece, depth), f32),
            shaped((rows, 2 * depth + 2 * units), bf16),
            shaped((rows, width), bf16),
        ],
        [],
        [*chunks, cotangent, w_in, w_back],
        [pltpu.VMEM((rows, depth), f32)],
    )
    layer, wide, cross_cols = outs[head_count:]
    wide_beside = partner(wide, "blk", 1)
    if CFG["m_early"] == 0:
        early = plane_gather_wide(after(early, wide), early_beside, small)
    upstream = swap_parts(outs[:head_count])
    grad_second, gain_ffn_part, message = call(
        functools.partial(branch_kernel, head_count, width),
        [
            shaped((piece, depth), f32),
            shaped((1, depth), f32),
            shaped((chunk_count, piece, depth + STATS), bf16),
        ],
        [],
        [*upstream, second, gain_three, cotangent, cross_out_full, cross, logsum],
    )
    message, wide, wide_beside = hold([message, wide, wide_beside])
    branches = exchange(message, "blk", "head")
    branches, layer = hold([branches, layer])
    wide = plane_gather_wide(wide, wide_beside, small)
    if CFG["m_early"] == 1:
        early = plane_gather_wide(after(early, message), early_beside, small)
    layer = exchange(layer, "head")
    query_grads, branch_two, enc_key_grads, enc_value_grads = cross_backward(
        slots,
        lengths,
        queries,
        cross_out_full,
        enc_keys,
        enc_values,
        branches,
        head_count,
        width,
    )
    if CFG["m_early"] == 2:
        query_grads, layer = hold([query_grads, layer])
        early = plane_gather_wide(after(early, query_grads), early_beside, small)
    else:
        query_grads, layer, *early = hold([query_grads, layer, *early])
    query_grads = exchange(query_grads, "blk", "head")

    shares = projection_grads(
        enc_key_grads, enc_value_grads, enc_out, cross_cols, branch_two, plane, head_count
    )
    if CFG["t_cs"] == 1:
        query_grads, shares = hold([query_grads, shares])
    if CFG["w_k8"] == 1:
        (query_grads,) = hold([query_grads], *wide[1:])
    grad_first, gain_cross_part, *messages = call(
        functools.partial(first_kernel, head_count),
        [shaped((piece, depth), f32), shaped((1, depth), f32)]
        + [shaped((piece, 2 * depth + width), bf16)] * head_count,
        [],
        [query_grads, first, gain_two, query_full, grad_second, second, layer],
    )
    chunks = swap_parts(messages)
    if small:
        if CFG["t_shq"] == 1:
            shares = after(shares, messages[0])
        shares = exchange(shares, "dp", "blk")
        wide = wide + across_core(wide)
        early = early + across_core(early)
    else:
        early = early[:1]
    outs = call(
        functools.partial(self_back_kernel, head_count),
        (
            [shaped((piece, depth), f32)] * head_count
            if CFG["t_rsz"] == "perm"
            else [shaped((head_count, piece, depth), f32)]
        )
        + [
            shaped((plane if small else 1, rows, depth + 4 * width), bf16),
            shaped((rows, depth), bf16),
        ],
        [dec_len],
        [*chunks, w_out, self_qkv, w_query, w_key, w_value],
        [pltpu.VMEM((rows, depth), f32), pltpu.VMEM((rows, depth + 4 * width), bf16)],
    )
    late, layer_out = outs[-2:]
    shares_gate = {5: [chunks[len(chunks) > 1]], 0: [], 1: [late], 2: []}[CFG["t_sh"]]
    shares, *wide = hold([shares, *wide], *shares_gate)
    if not small:
        late = [late.reshape(late.shape[1:])]
    elif CFG["t_late"] == "a2a":
        late = [exchange(late, "dp", "blk")]
    else:
        late = plane_gather(late.reshape(late.shape[1:]))
    if CFG["t_rsz"] == "perm":
        upstream = swap_parts(outs[:head_count])
    else:
        upstream = [exchange(outs[0], "head")]
    if CFG["t_enc"] == 0:
        enc_grad_pair = hold([enc_key_grads, enc_value_grads], upstream[-1])
        grad_enc = encoder_grads(*enc_grad_pair, key_full, value_full)
    (message,) = call(
        functools.partial(input_kernel, len(upstream)),
        [shaped((head_count if CFG["t_agz"] == "a2a" else 1, piece + 8, depth), f32)],
        [],
        [*upstream, dec_in, gain_one, grad_first, gain_cross_part, gain_ffn_part],
        micros=3 * CFG["t_cost"],
    )
    if CFG["t_latep"] == 1:
        message = after(message, *late[: len(late) // 2 + 1])
    if CFG["t_sh"] == 2:
        shares = after(shares, message)
    if CFG["t_agz"] == "perm":
        chunks = share_heads(message.reshape(message.shape[1:]))
    else:
        chunks = [exchange(message, "head")]
    if CFG["t_latep"] == 2:
        chunks = hold(chunks, *late[: len(late) // 2 + 1])
    if CFG["t_enc"] == 1:
        enc_grad_pair = hold([enc_key_grads, enc_value_grads], message)
        grad_enc = encoder_grads(*enc_grad_pair, key_full, value_full)
    elif CFG["t_enc"] == 2:
        grad_enc = encoder_grads(enc_key_grads, enc_value_grads, key_full, value_full)
    elif CFG["t_enc"] == 3:
        enc_grad_pair = hold([enc_key_grads, enc_value_grads], chunks[-1])
        grad_enc = encoder_grads(*enc_grad_pair, key_full, value_full)
    grad_in, gains = call(
        functools.partial(place_kernel, head_count),
        [shaped((rows, depth), f32), shaped((8, depth), f32)],
        [],
        chunks,
        micros=3 * CFG["t_cost"],
    )
    if small:
        blocks, cross_share = call(
            share_kernel,
            [
                shaped((head_count, width // 4, depth), bf16),
                shaped((width // plane, depth), bf16),
            ],
            [],
            [shares],
            micros=3 * CFG["t_cost"],
        )
        blocks = exchange(blocks, "head")
        (shares,) = call(
            spread_kernel,
            [shaped((plane, width // 4 + width // plane + 24, depth), bf16)],
            [],
            [blocks, cross_share, gains],
            micros=3 * CFG["t_cost"],
        )
        grad_c_key, grad_c_value, grad_c_out, gains = call(
            collect_kernel,
            [shaped((width, depth), f32)] * 3 + [shaped((8, depth), f32)],
            [],
            [exchange(shares, "dp", "blk")],
            micros=3 * CFG["t_cost"],
        )
    else:
        gains, shares = lax.psum((gains, shares.astype(f32)), ("dp", "blk"))
        blocks = shares[: 2 * depth].reshape(2, head_count, width, depth)
        blocks = jnp.swapaxes(blocks, 0, 1)
        blocks = sum(swap_parts([blocks[k] for k in range(head_count)]))
        grad_c_key, grad_c_value = blocks[0], blocks[1]
        grad_c_out = shares[2 * depth :]


    if CFG["t_broad"] == 1:
        wide = hold(wide, message)
    elif CFG["t_broad"] == 2:
        wide = hold(wide, grad_in)
    broad = call(
        functools.partial(wide_kernel, len(wide)),
        [shaped((depth, units), f32), shaped((units, depth), f32)],
        [],
        wide,
        [pltpu.VMEM((sum(part.shape[0] for part in wide), wide[0].shape[1]), bf16)],
        8 * CFG["t_cost"],
    )
    slim = call(
        functools.partial(weight_kernel, len(early), len(late), width),
        [shaped((width, depth), f32)] * 5,
        [],
        [*early, *late],
        [
            pltpu.VMEM((sum(part.shape[0] for part in early), early[0].shape[1]), bf16),
            pltpu.VMEM((plane * rows if small else rows, late[0].shape[-1]), bf16),
        ],
        6 * CFG["t_cost"],
    )
    if not small:
        slim, broad = lax.psum((tuple(slim), tuple(broad)), ("dp", "blk"))
    return (
        layer_out,
        grad_in,
        grad_enc,
        gains[0],
        gains[1],
        gains[2],
        *slim,
        grad_c_key,
        grad_c_value,
        grad_c_out,
        *broad,
    )


def solution(mesh):
    rows = P(("dp", "blk"), None)
    enc = P(("dp", "blk", "head"), None)
    each = P(("dp", "blk"))
    heads = P("head", None)
    return jax.shard_map(
        body,
        mesh=mesh,
        in_specs=(
            rows,
            enc,
            each,
            each,
            each,
            P(),
            P(),
            P(),
            *[heads] * 8,
            P(None, "head"),
            heads,
            rows,
        ),
        out_specs=(rows, rows, enc, P(), P(), P(), *[heads] * 8, P(None, "head"), heads),
        check_vma=False,
    )
```

```python
import functools

import jax
import jax.numpy as jnp
from jax import lax
from jax.experimental import pallas as pl
from jax.experimental.pallas import tpu as pltpu
from jax.sharding import PartitionSpec as P

CFG = dict(
    s_o=1, s_a=1, s_xy=1, l_d=1, t_a=1, t_cost=0.05, k1=0.1, vmem=64, s_rs="bf16", m_e=1, t_shg=3, e_c=0, w_c=0,
    t_late="perm", t_rsz="perm", t_agz="perm", t_shq=1, sh_q=0, cost=1.0, t_cs=1,
    t_p=4, w_x=1, w_xy=1, l_p=0, l_xy=0, e_p=4, b_p=3, e_y=1,
)
DHEAD = 64
LP = 384
LEAST = 3 * LP // 4
norm_epsilon = 1e-06
masked_score = -1e30
bf16 = jnp.bfloat16
f32 = jnp.float32
PAIR = 2 * DHEAD
STATS = 128
SECOND_LANE = 16
SPLIT_LANE = 32
VMEM_BYTES = CFG["vmem"] * 1024 * 1024


def nn(left, right):
    return lax.dot_general(left, right, (((1,), (0,)), ((), ())), preferred_element_type=f32)


def nt(left, right):
    return lax.dot_general(left, right, (((1,), (1,)), ((), ())), preferred_element_type=f32)


def tn(left, right):
    return lax.dot_general(left, right, (((0,), (0,)), ((), ())), preferred_element_type=f32)


def exact_nn(left, right):
    return lax.dot_general(
        left,
        right,
        (((1,), (0,)), ((), ())),
        precision=lax.Precision.HIGHEST,
        preferred_element_type=f32,
    )


def norm_scale(values):
    return lax.rsqrt(jnp.mean(values * values, axis=-1, keepdims=True) + norm_epsilon)


def normalize(values, gain):
    return values * norm_scale(values) * gain


def norm_back(upstream, values, gain):
    scale = norm_scale(values)
    unit = values * scale
    scaled = upstream * gain
    grad = scale * (scaled - unit * jnp.mean(scaled * unit, axis=-1, keepdims=True))
    return grad, jnp.sum(upstream * unit, axis=0, keepdims=True)


def cost(micros):
    return pl.CostEstimate(flops=0, bytes_accessed=int(micros * CFG["cost"] * 3e6), transcendentals=0)


def smem():
    return pl.BlockSpec(memory_space=pltpu.SMEM)


def shaped(shape, dtype):
    return jax.ShapeDtypeStruct(shape, dtype)


def whole(shape):
    return pl.BlockSpec(shape, lambda *_: (0,) * len(shape), pipeline_mode=pl.Buffered(1))


class Weight:
    def __init__(self, array, index):
        self.array, self.index = array, index
        self.shape = array.shape[1:]


def spec_of(array):
    if isinstance(array, Weight):
        block = (None, *array.shape)
        index = array.index
        return pl.BlockSpec(block, lambda *_: (index, 0, 0), pipeline_mode=pl.Buffered(1))
    return whole(array.shape)


def value_of(array):
    return array.array if isinstance(array, Weight) else array


def call(kernel, outs, scalars, arrays, scratch=(), micros=3.5):
    return pl.pallas_call(
        kernel,
        grid=(1,),
        out_shape=tuple(outs),
        in_specs=[smem()] * len(scalars) + [spec_of(array) for array in arrays],
        out_specs=tuple(whole(out.shape) for out in outs),
        scratch_shapes=list(scratch),
        cost_estimate=cost(micros),
        compiler_params=pltpu.CompilerParams(
            vmem_limit_bytes=VMEM_BYTES, dimension_semantics=("arbitrary",)
        ),
    )(*scalars, *[value_of(array) for array in arrays])


def my_head():
    return lax.axis_index("head")


def my_core():
    return lax.axis_index("dp") % 2


def my_blk():
    return lax.axis_index("blk")


def my_chip():
    return lax.axis_index("dp") // 2 * 2 + lax.axis_index("blk") % 2


def pack_stats(values):
    high = values.astype(bf16).astype(f32)
    middle = (values - high).astype(bf16).astype(f32)
    lowest = values - high - middle
    return (
        high + pltpu.roll(middle, SPLIT_LANE, 1) + pltpu.roll(lowest, 2 * SPLIT_LANE, 1)
    ).astype(bf16)


def unpack_stats(packed):
    packed = packed.astype(f32)
    return (
        packed
        + pltpu.roll(packed, STATS - SPLIT_LANE, 1)
        + pltpu.roll(packed, STATS - 2 * SPLIT_LANE, 1)
    )


def group_place(head_count, kb, kh):
    return (my_blk() ^ kb) * head_count + (my_head() ^ kh)


def rows_of(place, count):
    if isinstance(place, int):
        return slice(place * count, (place + 1) * count)
    return pl.ds(pl.multiple_of(place * count, count), count)


def head_blocks(width, head_count, shift):
    return [(j ^ shift) * width for j in range(head_count)]


def permuted(values, width, head_count, shift):
    if shift == 0:
        return values
    return jnp.concatenate(
        [values[:, o : o + width] for o in head_blocks(width, head_count, shift)], axis=1
    )


def self_probs(q, k, allowed):
    scores = jnp.where(allowed, nt(q, k), masked_score)
    raised = jnp.exp(scores - jnp.max(scores, axis=-1, keepdims=True))
    return raised / jnp.sum(raised, axis=-1, keepdims=True)


def causal(rows, length):
    at_q = lax.broadcasted_iota(jnp.int32, (rows, rows), 0)
    at_k = lax.broadcasted_iota(jnp.int32, (rows, rows), 1)
    return (at_k <= at_q) & (at_k.astype(f32) < length)


def self_kernel(dec_ref, len_ref, gain_ref, wq_ref, wk_ref, wv_ref, w_out_ref, *refs):
    normed_ref, qkv_ref, out_ref, *partials = refs[:-1]
    total = refs[-1]
    rows = normed_ref.shape[0]
    width = wq_ref.shape[0]
    normed = normalize(dec_ref[...].astype(f32), gain_ref[...].astype(f32)[None, :]).astype(bf16)
    normed_ref[...] = normed
    for i, weight in enumerate((wq_ref, wk_ref, wv_ref)):
        qkv_ref[:, i * width : (i + 1) * width] = nt(normed, weight[...]).astype(bf16)
    allowed = causal(rows, len_ref[0].astype(f32))
    outs = []
    for h in range(width // DHEAD):
        o = h * DHEAD
        probs = self_probs(
            qkv_ref[:, o : o + DHEAD], qkv_ref[:, width + o : width + o + DHEAD], allowed
        )
        outs.append(nn(probs.astype(bf16), qkv_ref[:, 2 * width + o : 2 * width + o + DHEAD]))
    attended = jnp.concatenate(outs, axis=1).astype(bf16)
    out_ref[...] = attended
    total[...] = nn(attended, w_out_ref[...])
    piece = rows // len(partials)
    for k, partial in enumerate(partials):
        partial[...] = total[rows_of(my_head() ^ k, piece), :].astype(partial.dtype)


def call_self(dec_in, dec_len, gain, w_query, w_key, w_value, w_out, head_count):
    rows, depth = dec_in.shape
    width = w_query.shape[0]
    arrays = (dec_in, dec_len, gain, w_query, w_key, w_value, w_out)
    outs = [
        shaped((rows, depth), bf16),
        shaped((rows, 3 * width), bf16),
        shaped((rows, width), bf16),
    ] + [shaped((rows // head_count, depth), f32 if CFG["s_rs"] == "f32" else bf16)] * head_count
    return pl.pallas_call(
        self_kernel,
        grid=(1,),
        out_shape=tuple(outs),
        in_specs=[smem() if array is dec_len else whole(array.shape) for array in arrays],
        out_specs=tuple(whole(out.shape) for out in outs),
        scratch_shapes=[pltpu.VMEM((rows, depth), f32)],
        cost_estimate=cost(CFG["k1"]),
        compiler_params=pltpu.CompilerParams(
            vmem_limit_bytes=VMEM_BYTES, dimension_semantics=("arbitrary",)
        ),
    )(*arrays)


def normed_kernel(count, *refs):
    chunks = refs[:count]
    dec_ref, gain_ref, first_ref, message_ref = refs[count:]
    piece = first_ref.shape[0]
    first = dec_ref[rows_of(my_head(), piece), :].astype(f32) + sum(
        chunk[...].astype(f32) for chunk in chunks
    )
    first_ref[...] = first
    normed = normalize(first, gain_ref[...].astype(f32)[None, :]).astype(bf16)
    for i in range(message_ref.shape[0]):
        message_ref[i] = normed


def join_kernel(*refs):
    start = 0
    for part in refs[:-1]:
        refs[-1][start : start + part.shape[0], :] = part[...]
        start += part.shape[0]


def put_weights(count, owns, arrays, out_ref):
    rows = owns[0].shape[0]
    half = rows // 2
    for weight, own in enumerate(owns):
        out_ref[weight, :rows, :] = own[...]
    pair = lax.axis_index("dp") // 2 % 2
    for place, array in enumerate(arrays):
        weight = (my_core() ^ place // 4) * 2 + (pair ^ place // 2 % 2)
        side = my_blk() % 2 ^ place % 2
        for k in range(count):
            start = pl.multiple_of((k + 1) * rows + side * half, half)
            out_ref[weight, pl.ds(start, half), :] = array[k * half : (k + 1) * half, :]


def query_kernel(blk_count, head_count, chunks_ref, c_query_ref, one_ref, self_ref, *refs):
    early_ref, q_ref, normed = refs
    rows, depth = one_ref.shape
    width = self_ref.shape[1]
    piece = rows // head_count
    for kb in range(blk_count):
        for i in range(head_count):
            place = (my_blk() ^ kb) * head_count + i
            normed[i * piece : (i + 1) * piece, :] = chunks_ref[place]
        if kb == 0:
            early_ref[:, :depth] = one_ref[...]
            early_ref[:, depth : 2 * depth] = normed[...]
            early_ref[:, 2 * depth : 2 * depth + width] = self_ref[...]
            early_ref[:, 2 * depth + width :] = jnp.zeros(
                (rows, early_ref.shape[1] - 2 * depth - width), bf16
            )
        q_ref[kb] = nt(normed[...], c_query_ref[...]).astype(bf16)


def project_kernel(count, enc_ref, *refs):
    owns, arrays, (key_ref, value_ref, weights_ref) = refs[:4], refs[4:-3], refs[-3:]

    @pl.when(pl.program_id(0) == 0)
    def _():
        put_weights(count, owns, arrays, weights_ref)

    key_ref[...] = nt(enc_ref[...], weights_ref[0]).astype(bf16)
    value_ref[...] = nt(enc_ref[...], weights_ref[1]).astype(bf16)


def project(enc, owns, arrays, count):
    slots, depth = enc.shape
    block = pl.BlockSpec((LP, depth), lambda p: (p, 0))
    weights = shaped((4, depth, depth), bf16)
    return pl.pallas_call(
        functools.partial(project_kernel, count),
        grid=(slots // LP,),
        in_specs=[block] + [whole(array.shape) for array in (*owns, *arrays)],
        out_specs=(block, block, whole(weights.shape)),
        out_shape=(shaped(enc.shape, bf16), shaped(enc.shape, bf16), weights),
        cost_estimate=cost(9),
        compiler_params=pltpu.CompilerParams(
            vmem_limit_bytes=VMEM_BYTES, dimension_semantics=("arbitrary",)
        ),
    )(enc, *owns, *arrays)


def spread_pairs(values, target, kb):
    rows = values.shape[0]
    for j in range(values.shape[1] // PAIR):
        pair = values[:, j * PAIR : (j + 1) * PAIR]
        lane = lax.broadcasted_iota(jnp.int32, pair.shape, 1)
        zero = jnp.zeros_like(pair)
        target[kb, j, 0:rows, :] = jnp.where(lane < DHEAD, pair, zero)
        target[kb, j, rows : 2 * rows, :] = jnp.where(lane < DHEAD, zero, pair)


def within(values, length, fill):
    place = LEAST + lax.broadcasted_iota(jnp.int32, (LP - LEAST, values.shape[1]), 0)
    last = jnp.where(place < length, values[LEAST:], fill)
    return jnp.concatenate([values[:LEAST], last], axis=0)


def pair_columns(j):
    return slice(j * PAIR, (j + 1) * PAIR)


def add_pair(target, slot, j, update, factor=None):
    rows = target.shape[2]
    for i in range(2):
        span = slice(j * PAIR + i * DHEAD, j * PAIR + (i + 1) * DHEAD)
        own = update[i * DHEAD : (i + 1) * DHEAD, i * rows : (i + 1) * rows]
        old = target[slot, span, :]
        if factor is not None:
            old = old * factor[:, i * rows : (i + 1) * rows]
        target[slot, span, :] = old + own


def cross_forward_kernel(blk_count, head_count, width, *refs):
    slot_ref, len_ref, q_ref, k_ref, v_ref = refs[:5]
    out_ref, q2, acc, highest, totals, stat, flat, flat_stat, held, probs, factors = refs[5:]
    rows, depth = q_ref.shape[1], q_ref.shape[2]
    pairs = depth // PAIR
    step = pl.program_id(0)

    @pl.when(step == 0)
    def _():
        for kb in range(blk_count):
            spread_pairs(q_ref[kb], q2, kb)
        highest[...] = jnp.full(highest.shape, masked_score, f32)
        totals[...] = jnp.zeros(totals.shape, f32)
        acc[...] = jnp.zeros(acc.shape, f32)

    slot = slot_ref[step]
    for j in range(pairs):
        scores = within(nt(k_ref[:, pair_columns(j)], q2[slot, j]), len_ref[step], masked_score)
        held[j] = scores
        before = highest[slot, j : j + 1, :]
        newest = jnp.maximum(before, jnp.max(scores, axis=0, keepdims=True))
        factors[j : j + 1, :] = jnp.exp(before - newest)
        highest[slot, j : j + 1, :] = newest
    for j in range(pairs):
        raised = jnp.exp(held[j] - highest[slot, j : j + 1, :])
        probs[j] = raised.astype(bf16)
        totals[slot, j : j + 1, :] = totals[slot, j : j + 1, :] * factors[
            j : j + 1, :
        ] + jnp.sum(raised, axis=0, keepdims=True)
    for j in range(pairs):
        update = tn(v_ref[:, pair_columns(j)], probs[j])
        add_pair(acc, slot, j, update, factors[j : j + 1, :])

    @pl.when(step == pl.num_programs(0) - 1)
    def _():
        stat[...] = jnp.zeros(stat.shape, f32)
        piece = rows // head_count
        per = width // DHEAD
        for kb in range(blk_count):
            flat[...] = acc[kb].T
            for kh in range(head_count):
                for head in range(depth // DHEAD):
                    at = ((head // per) ^ kh) * per + head % per
                    lanes = slice((head % 2) * rows, (head % 2 + 1) * rows)
                    stat[at : at + 1, :] = highest[kb, head // 2 : head // 2 + 1, lanes]
                    stat[SECOND_LANE + at : SECOND_LANE + at + 1, :] = totals[
                        kb, head // 2 : head // 2 + 1, lanes
                    ]
                flat_stat[...] = stat[...].T
                mine = rows_of(my_head() ^ kh, piece)
                place = group_place(head_count, kb, kh)
                out_ref[place, :, :depth] = permuted(
                    flat[mine, :].astype(bf16), width, head_count, kh
                )
                out_ref[place, :, depth:] = pack_stats(flat_stat[mine, :])


def cross_forward(slots, lengths, queries, keys, values, head_count, width):
    blk_count, rows, depth = queries.shape
    passages = slots.shape[0]
    piece = rows // head_count
    chunk_count = blk_count * head_count
    pairs = depth // PAIR
    grid = pltpu.PrefetchScalarGridSpec(
        num_scalar_prefetch=2,
        grid=(passages,),
        in_specs=[
            whole((blk_count, rows, depth)),
            pl.BlockSpec((LP, depth), lambda p, *_: (p, 0)),
            pl.BlockSpec((LP, depth), lambda p, *_: (p, 0)),
        ],
        out_specs=whole((chunk_count, piece, depth + STATS)),
        scratch_shapes=[
            pltpu.VMEM((blk_count, pairs, 2 * rows, PAIR), bf16),
            pltpu.VMEM((blk_count, depth, rows), f32),
            pltpu.VMEM((blk_count, 8, 2 * rows), f32),
            pltpu.VMEM((blk_count, 8, 2 * rows), f32),
            pltpu.VMEM((STATS, rows), f32),
            pltpu.VMEM((rows, depth), f32),
            pltpu.VMEM((rows, STATS), f32),
            pltpu.VMEM((pairs, LP, 2 * rows), f32),
            pltpu.VMEM((pairs, LP, 2 * rows), bf16),
            pltpu.VMEM((8, 2 * rows), f32),
        ],
    )
    return pl.pallas_call(
        functools.partial(cross_forward_kernel, blk_count, head_count, width),
        out_shape=shaped((chunk_count, piece, depth + STATS), bf16),
        cost_estimate=cost(15),
        grid_spec=grid,
        compiler_params=pltpu.CompilerParams(
            vmem_limit_bytes=VMEM_BYTES, dimension_semantics=("arbitrary",)
        ),
    )(slots, lengths, queries, keys, values)


def head_matrix(depth):
    head = lax.broadcasted_iota(jnp.int32, (STATS, depth), 0)
    column = lax.broadcasted_iota(jnp.int32, (STATS, depth), 1)
    return (head == column // DHEAD).astype(f32)


def combine_kernel(width, *refs):
    chunks, first_ref, c_out_ref, gain_ref, cross_ref, second_ref, logsum_ref = refs[:7]
    messages = refs[7:]
    piece, depth = cross_ref.shape
    stats = [unpack_stats(chunks[i, :, depth:]) for i in range(chunks.shape[0])]
    highest = stats[0]
    for other in stats[1:]:
        highest = jnp.maximum(highest, other)
    lane = lax.broadcasted_iota(jnp.int32, (piece, STATS), 1)
    real = lane < depth // DHEAD
    weights = [jnp.where(real, jnp.exp(one - highest), 0.0) for one in stats]
    total = sum(w * pltpu.roll(one, STATS - SECOND_LANE, 1) for w, one in zip(weights, stats))
    total = jnp.where(real, total, 1.0)
    logsum_ref[...] = jnp.where(real, highest + jnp.log(total), 0.0)
    spread = head_matrix(depth)
    weighted = exact_nn(jnp.concatenate(weights, axis=0), spread)
    cross = sum(
        chunks[i, :, :depth].astype(f32) * weighted[i * piece : (i + 1) * piece]
        for i in range(chunks.shape[0])
    )
    cross = cross / exact_nn(total, spread)
    cross_ref[...] = cross
    rounded = cross.astype(bf16)
    second = first_ref[...] + nn(rounded, c_out_ref[...])
    second_ref[...] = second
    normed = normalize(second, gain_ref[...].astype(f32)[None, :]).astype(bf16)
    for k, message in enumerate(messages):
        message[:, :depth] = normed
        message[:, depth:] = rounded[:, k * width : (k + 1) * width]


def ffn_kernel(count, *refs):
    chunks = refs[:count]
    cot_ref, w_in_ref, w_back_ref = refs[count : count + 3]
    grads = refs[count + 3 : 2 * count + 3]
    wide_ref, cols_ref, total = refs[2 * count + 3 :]
    piece, depth = grads[0].shape[0], grads[0].shape[1] // 2
    for k, chunk in enumerate(chunks):
        mine = rows_of(my_head() ^ k, piece)
        wide_ref[mine, :depth] = chunk[:, :depth]
        cols_ref[mine, :] = chunk[:, depth:]
    units = w_in_ref.shape[1]
    before = nn(wide_ref[:, :depth], w_in_ref[...])
    root = 0.7978845608028654
    cube = 0.044715
    square = before * before
    bend = jnp.tanh(root * (before + cube * before * square))
    hidden = (0.5 * before * (1.0 + bend)).astype(bf16)
    slope = 0.5 * (1.0 + bend) + 0.5 * before * (1.0 - bend * bend) * root * (
        1.0 + 3.0 * cube * square
    )
    pre_grad = (nt(cot_ref[...], w_back_ref[...]) * slope).astype(bf16)
    total[...] = nt(pre_grad, w_in_ref[...])
    wide_ref[:, depth : depth + units] = hidden
    wide_ref[:, depth + units : depth + 2 * units] = pre_grad
    wide_ref[:, depth + 2 * units :] = cot_ref[...]
    for k, grad in enumerate(grads):
        grad[:, :depth] = total[rows_of(my_head() ^ k, piece), :].astype(bf16)
    total[...] = nn(hidden, w_back_ref[...])
    for k, grad in enumerate(grads):
        grad[:, depth:] = total[rows_of(my_head() ^ k, piece), :].astype(bf16)


def branch_kernel(head_count, width, *refs):
    chunks = refs[:head_count]
    second_ref, gain_ref, cot_ref, c_out_ref, cross_ref, logsum_ref = refs[
        head_count : head_count + 6
    ]
    grad_ref, gain_grad_ref, layer_ref, message_ref = refs[head_count + 6 :]
    piece, depth = second_ref.shape
    received = sum(chunk[...].astype(f32) for chunk in chunks)
    upstream = received[:, :depth]
    layer_ref[...] = (second_ref[...] + received[:, depth:]).astype(bf16)
    grad, gain_grad_ref[...] = norm_back(upstream, second_ref[...], gain_ref[...].astype(f32)[None, :])
    grad = cot_ref[rows_of(my_head(), piece), :].astype(f32) + grad
    grad_ref[...] = grad
    branch = grad.astype(bf16)
    grad_cross = nt(branch, c_out_ref[...]).astype(bf16).astype(f32)
    spread = head_matrix(depth)
    deltas = lax.dot_general(
        grad_cross * cross_ref[...],
        spread,
        (((1,), (1,)), ((), ())),
        precision=lax.Precision.HIGHEST,
        preferred_element_type=f32,
    )
    stats = logsum_ref[...] + pltpu.roll(deltas, SECOND_LANE, 1)
    per = width // DHEAD
    heads = depth // DHEAD
    source = lax.broadcasted_iota(jnp.int32, (STATS, STATS), 0)
    target = lax.broadcasted_iota(jnp.int32, (STATS, STATS), 1)
    place = source % SECOND_LANE
    for k in range(head_count):
        moved = (source - place) + ((place // per) ^ k) * per + place % per
        shuffle = ((target == moved) & (place < heads) & (source < 2 * SECOND_LANE)).astype(f32)
        aligned = exact_nn(stats, shuffle)
        packed = pack_stats(aligned)
        for kb in range(message_ref.shape[0] // head_count):
            entry = group_place(head_count, kb, k)
            message_ref[entry, :, :depth] = branch
            message_ref[entry, :, depth:] = packed


def cross_backward_kernel(blk_count, head_count, width, *refs):
    slot_ref, len_ref, q_ref, c_out_ref, k_ref, v_ref = refs[:6]
    chunks, out_ref, branch_ref, grad_k_ref, grad_v_ref = refs[6:11]
    q2, g2, stats, branch, flat_stat, grad_q, flat = refs[11:18]
    held, grad_probs, probs, grad_scores = refs[18:]
    rows, depth = q_ref.shape[1], q_ref.shape[2]
    pairs = depth // PAIR
    piece = rows // head_count
    step = pl.program_id(0)

    @pl.when(step == 0)
    def _():
        for kb in range(blk_count):
            for i in range(head_count):
                place = (my_blk() ^ kb) * head_count + i
                span = slice(i * piece, (i + 1) * piece)
                branch[span, :] = chunks[place, :, :depth]
                flat_stat[span, :] = unpack_stats(chunks[place, :, depth:])
            if kb == 0:
                branch_ref[...] = branch[...]
            stats[kb] = flat_stat[...].T
            spread_pairs(q_ref[kb], q2, kb)
            spread_pairs(nt(branch[...], c_out_ref[...]).astype(bf16), g2, kb)
        grad_q[...] = jnp.zeros(grad_q.shape, f32)

    slot = slot_ref[step]

    def both_heads(first):
        return jnp.concatenate(
            [stats[slot, first : first + 1, :], stats[slot, first + 1 : first + 2, :]], axis=1
        )

    for j in range(pairs):
        held[j] = nt(k_ref[:, pair_columns(j)], q2[slot, j])
        grad_probs[j] = nt(v_ref[:, pair_columns(j)], g2[slot, j])
    for j in range(pairs):
        raised = within(jnp.exp(held[j] - both_heads(2 * j)), len_ref[step], 0.0)
        probs[j] = raised.astype(bf16)
        grad_scores[j] = (raised * (grad_probs[j] - both_heads(SECOND_LANE + 2 * j))).astype(bf16)
    for j in range(pairs):
        grad_v_ref[:, pair_columns(j)] = nn(probs[j], g2[slot, j]).astype(bf16)
        grad_k_ref[:, pair_columns(j)] = nn(grad_scores[j], q2[slot, j]).astype(bf16)
        add_pair(grad_q, slot, j, tn(k_ref[:, pair_columns(j)], grad_scores[j]))

    @pl.when(step == pl.num_programs(0) - 1)
    def _():
        for kb in range(blk_count):
            flat[...] = grad_q[kb].T
            for kh in range(head_count):
                mine = rows_of(my_head() ^ kh, piece)
                out_ref[group_place(head_count, kb, kh)] = permuted(
                    flat[mine, :].astype(bf16), width, head_count, kh
                )


def cross_backward(slots, lengths, queries, c_out, keys, values, chunks, head_count, width):
    blk_count, rows, depth = queries.shape
    passages = slots.shape[0]
    piece = rows // head_count
    chunk_count = blk_count * head_count
    pairs = depth // PAIR
    passage = pl.BlockSpec((LP, depth), lambda p, *_: (p, 0))
    grid = pltpu.PrefetchScalarGridSpec(
        num_scalar_prefetch=2,
        grid=(passages,),
        in_specs=[
            whole((blk_count, rows, depth)),
            spec_of(c_out),
            passage,
            passage,
            whole(chunks.shape),
        ],
        out_specs=(
            whole((chunk_count, piece, depth)),
            whole((rows, depth)),
            passage,
            passage,
        ),
        scratch_shapes=[
            pltpu.VMEM((blk_count, pairs, 2 * rows, PAIR), bf16),
            pltpu.VMEM((blk_count, pairs, 2 * rows, PAIR), bf16),
            pltpu.VMEM((blk_count, STATS, rows), f32),
            pltpu.VMEM((rows, depth), bf16),
            pltpu.VMEM((rows, STATS), f32),
            pltpu.VMEM((blk_count, depth, rows), f32),
            pltpu.VMEM((rows, depth), f32),
            pltpu.VMEM((pairs, LP, 2 * rows), f32),
            pltpu.VMEM((pairs, LP, 2 * rows), f32),
            pltpu.VMEM((pairs, LP, 2 * rows), bf16),
            pltpu.VMEM((pairs, LP, 2 * rows), bf16),
        ],
    )
    return pl.pallas_call(
        functools.partial(cross_backward_kernel, blk_count, head_count, width),
        out_shape=(
            shaped((chunk_count, piece, depth), bf16),
            shaped((rows, depth), bf16),
            shaped(keys.shape, bf16),
            shaped(keys.shape, bf16),
        ),
        cost_estimate=cost(16),
        grid_spec=grid,
        compiler_params=pltpu.CompilerParams(
            vmem_limit_bytes=VMEM_BYTES, dimension_semantics=("arbitrary",)
        ),
    )(slots, lengths, queries, value_of(c_out), keys, values, chunks)


def first_kernel(*refs):
    chunks, first_ref, gain_ref, c_query_ref, second_grad_ref = refs[:5]
    grad_ref, gain_grad_ref = refs[5:7]
    messages = refs[7:]
    piece, depth = grad_ref.shape
    width = messages[0].shape[1] - depth
    grad_q = sum(chunks[i].astype(f32) for i in range(chunks.shape[0])).astype(bf16)
    upstream = nn(grad_q, c_query_ref[...])
    grad, gain_grad_ref[...] = norm_back(upstream, first_ref[...], gain_ref[...].astype(f32)[None, :])
    grad = second_grad_ref[...] + grad
    grad_ref[...] = grad
    branch = grad.astype(bf16)
    for k, message in enumerate(messages):
        message[:, :depth] = branch
        message[:, depth:] = grad_q[:, k * width : (k + 1) * width]


def self_back_kernel(count, len_ref, *refs):
    chunks = refs[:count]
    w_out_ref, qkv_ref, wq_ref, wk_ref, wv_ref = refs[count : count + 5]
    grads, (sides_ref, total, side_ref) = refs[count + 5 : -3], refs[-3:]
    width, depth = wq_ref.shape
    rows = side_ref.shape[0]
    piece = rows // count
    start = depth + width
    for k, chunk in enumerate(chunks):
        mine = rows_of(my_head() ^ k, piece)
        side_ref[mine, :start] = chunk[...]
    grad_self = nt(side_ref[:, :depth], w_out_ref[...]).astype(bf16)
    allowed = causal(rows, len_ref[0].astype(f32))
    grad_q, grad_k, grad_v = [], [], []
    for h in range(width // DHEAD):
        o = h * DHEAD
        q = qkv_ref[:, o : o + DHEAD]
        k = qkv_ref[:, width + o : width + o + DHEAD]
        v = qkv_ref[:, 2 * width + o : 2 * width + o + DHEAD]
        g = grad_self[:, o : o + DHEAD]
        probs = self_probs(q, k, allowed)
        grad_probs = nt(g, v)
        delta = jnp.sum(probs * grad_probs, axis=-1, keepdims=True)
        grad_scores = (probs * (grad_probs - delta)).astype(bf16)
        grad_q.append(nn(grad_scores, k))
        grad_k.append(tn(grad_scores, q))
        grad_v.append(tn(probs.astype(bf16), g))
    flat = [jnp.concatenate(parts, axis=1).astype(bf16) for parts in (grad_q, grad_k, grad_v)]
    for i, part in enumerate(flat):
        side_ref[:, start + i * width : start + (i + 1) * width] = part
    total[...] = nn(flat[0], wq_ref[...]) + nn(flat[1], wk_ref[...]) + nn(flat[2], wv_ref[...])
    if len(grads) == 1:
        for i in range(count):
            grads[0][i] = total[i * piece : (i + 1) * piece, :].astype(bf16)
    else:
        for k, grad in enumerate(grads):
            grad[...] = total[rows_of(my_head() ^ k, piece), :].astype(bf16)
    for i in range(sides_ref.shape[0]):
        sides_ref[i] = side_ref[...]


def input_kernel(count, *refs):
    chunks = refs[:count]
    dec_ref, gain_ref, first_grad_ref, cross_gain_ref, ffn_gain_ref, layer_ref = refs[count:-1]
    message_ref = refs[-1]
    if count == 1:
        chunks = [chunks[0].at[i] for i in range(chunks[0].shape[0])]
    piece, depth = chunks[0].shape
    upstream = sum(chunk[...].astype(f32) for chunk in chunks)
    values = dec_ref[rows_of(my_head(), piece), :].astype(f32)
    grad, self_gain = norm_back(upstream, values, gain_ref[...].astype(f32)[None, :])
    grad = (first_grad_ref[...] + grad).astype(bf16)
    gains = gain_rows([self_gain, cross_gain_ref[...], ffn_gain_ref[...]])
    fill = jnp.zeros((message_ref.shape[1] - 2 * piece - len(gains), depth), f32)
    gains = jnp.concatenate([*gains, fill], axis=0).astype(bf16)
    for i in range(message_ref.shape[0]):
        message_ref[i, :piece, :] = grad
        message_ref[i, piece : 2 * piece, :] = layer_ref[...]
        message_ref[i, 2 * piece :, :] = gains


def gain_rows(gains):
    rows = []
    for rest in gains:
        for step in range(3):
            rows.append(rest.astype(bf16).astype(f32))
            rest = rest - rows[-1]
    return rows


def gain_sums(rows):
    return [jnp.sum(rows[3 * i : 3 * i + 3, :], axis=0, keepdims=True) for i in range(3)]


def place_kernel(count, *refs):
    chunks, (out_ref, gain_ref, layer_ref) = refs[:-3], refs[-3:]
    piece = out_ref.shape[0] // count
    if len(chunks) == 1:
        chunks = [chunks[0].at[i] for i in range(count)]
        places = range(count)
    else:
        places = [my_head() ^ k for k in range(count)]
    for place, chunk in zip(places, chunks):
        out_ref[rows_of(place, piece), :] = chunk[:piece, :].astype(f32)
        layer_ref[rows_of(place, piece), :] = chunk[piece : 2 * piece, :]
    gains = gain_sums(sum(chunk[2 * piece :, :].astype(f32) for chunk in chunks))
    fill = jnp.zeros((gain_ref.shape[0] - len(gains), gain_ref.shape[1]), f32)
    gain_ref[...] = jnp.concatenate([*gains, fill], axis=0)


def weight_kernel(early_count, late_count, width, *refs):
    early, late = refs[:early_count], refs[early_count : early_count + late_count]
    wq_ref, wk_ref, wv_ref, out_ref, query_ref, normed, side = refs[early_count + late_count :]
    depth = wq_ref.shape[1]
    stack_up(early, normed)
    stack_up(late, side)
    start = depth + width
    qkv = tn(side[:, start:], normed[:, :depth])
    for i, target in enumerate((wq_ref, wk_ref, wv_ref)):
        target[...] = qkv[i * width : (i + 1) * width]
    query_ref[...] = tn(side[:, depth:start], normed[:, depth : 2 * depth])
    out_ref[...] = tn(normed[:, 2 * depth : 2 * depth + width], side[:, :depth])


def stack_up(parts, target):
    start = 0
    if len(parts) == 1 and len(parts[0].shape) == 3:
        place = lax.axis_index("dp")
        entries = [(place ^ k) * 2 + (my_blk() ^ b) for k in (0, 2, 1, 3) for b in (0, 1)]
        rows = parts[0].shape[1]
        for i, entry in enumerate(entries):
            target[i * rows : (i + 1) * rows, :] = parts[0][entry]
        return
    for part in parts:
        target[start : start + part.shape[0], :] = part[...]
        start += part.shape[0]


def wide_kernel(count, *refs):
    in_ref, back_ref, stack = refs[count:]
    depth, units = in_ref.shape
    stack_up(refs[:count], stack)
    in_ref[...] = tn(stack[:, :depth], stack[:, depth + units : depth + 2 * units])
    back_ref[...] = tn(stack[:, depth : depth + units], stack[:, depth + 2 * units :])


def projection_grad_kernel(head_count, plane, *refs):
    keys_ref, values_ref, enc_ref, cols_ref, branch_ref, out_ref, total = refs
    step = pl.program_id(0)
    count, depth = total.shape
    width = cols_ref.shape[1]
    blocks = count // width

    @pl.when(step == 0)
    def _():
        cross = tn(cols_ref[...], branch_ref[...]).astype(bf16)
        if len(out_ref.shape) == 2:
            out_ref[2 * depth :, :] = cross
        else:
            size = width // plane
            for device in range(plane):
                start = depth // 4
                out_ref[device, start : start + size, :] = cross[device * size : (device + 1) * size]

    for weight, grad_ref in enumerate((keys_ref, values_ref)):
        total[...] = tn(grad_ref[...], enc_ref[...])
        if len(out_ref.shape) == 2:
            start = pl.multiple_of(weight * depth + step * count, 16)
            out_ref[pl.ds(start, count), :] = total[...].astype(bf16)
            continue
        size = width // 4
        for block in range(blocks):
            place = pl.multiple_of((step * blocks + block) * size, 16)
            for part in range(4):
                start = block * width + part * size
                device = (part // 2 * 2 + weight) * 2 + part % 2
                out_ref[device, pl.ds(place, size), :] = total[start : start + size, :].astype(bf16)


def projection_grads(key_grads, value_grads, enc, cross_cols, branch, plane, head_count):
    slots, depth = enc.shape
    width = cross_cols.shape[1]
    steps = 2
    block = pl.BlockSpec((slots, depth // steps), lambda j: (0, j))
    if plane == 8:
        out = shaped((plane, -(-(depth // 4 + width // plane) // 16) * 16, depth), bf16)
    else:
        out = shaped((2 * depth + width, depth), bf16)
    return pl.pallas_call(
        functools.partial(projection_grad_kernel, head_count, plane),
        grid=(steps,),
        in_specs=[block, block, whole(enc.shape), whole(cross_cols.shape), whole(branch.shape)],
        out_specs=whole(out.shape),
        out_shape=out,
        scratch_shapes=[pltpu.VMEM((depth // steps, depth), f32)],
        cost_estimate=cost(4),
        compiler_params=pltpu.CompilerParams(
            vmem_limit_bytes=VMEM_BYTES, dimension_semantics=("arbitrary",)
        ),
    )(key_grads, value_grads, enc, cross_cols, branch)


def encoder_grad_kernel(keys_ref, values_ref, key_ref, value_ref, out_ref):
    out_ref[...] = nn(keys_ref[...], key_ref[...]) + nn(values_ref[...], value_ref[...])


def encoder_grads(key_grads, value_grads, key_full, value_full):
    slots, depth = key_grads.shape
    block = pl.BlockSpec((LP, depth), lambda p: (p, 0))
    return pl.pallas_call(
        encoder_grad_kernel,
        grid=(slots // LP,),
        in_specs=[block, block, spec_of(key_full), spec_of(value_full)],
        out_specs=block,
        out_shape=shaped((slots, depth), f32),
        cost_estimate=cost(7 * CFG["t_cost"]),
        compiler_params=pltpu.CompilerParams(
            vmem_limit_bytes=VMEM_BYTES, dimension_semantics=("arbitrary",)
        ),
    )(key_grads, value_grads, value_of(key_full), value_of(value_full))


def share_kernel(shares_ref, blocks_ref, cross_ref):
    count, size = blocks_ref.shape[:2]
    total = sum(shares_ref[i].astype(f32) for i in range(shares_ref.shape[0]))
    for k in range(count):
        blocks_ref[my_head() ^ k] = total[k * size : (k + 1) * size].astype(bf16)
    cross_ref[...] = total[count * size : count * size + cross_ref.shape[0]].astype(bf16)


def spread_kernel(blocks_ref, cross_ref, gains_ref, out_ref):
    size, more = blocks_ref.shape[1], cross_ref.shape[0]
    block = sum(blocks_ref[i].astype(f32) for i in range(blocks_ref.shape[0])).astype(bf16)
    pieces = gain_rows([gains_ref[i : i + 1, :] for i in range(3)])
    fill = out_ref.shape[1] - size - more - len(pieces)
    pieces.append(jnp.zeros((fill, out_ref.shape[2]), f32))
    tail = jnp.concatenate([cross_ref[...].astype(f32), *pieces], axis=0).astype(bf16)
    for device in range(out_ref.shape[0]):
        out_ref[device, :size, :] = block
        out_ref[device, size:, :] = tail


def collect_kernel(shares_ref, key_ref, value_ref, cross_ref, gains_ref):
    plane = shares_ref.shape[0]
    size = key_ref.shape[0] // 4
    more = cross_ref.shape[0] // plane
    total = 0.0
    for device in range(plane):
        place, blk = device // 2, device % 2
        target = value_ref if place % 2 else key_ref
        part = place // 2 * 2 + blk
        share = shares_ref[device].astype(f32)
        target[part * size : (part + 1) * size, :] = share[:size]
        cross_ref[device * more : (device + 1) * more, :] = share[size : size + more]
        total = total + share[size + more :]
    for i, gain in enumerate(gain_sums(total)):
        gains_ref[i : i + 1, :] = gain
    gains_ref[3:, :] = jnp.zeros((gains_ref.shape[0] - 3, gains_ref.shape[1]), f32)


def after(array, *others):
    return lax.optimization_barrier((array, *others))[0]


def hold(arrays, *others):
    arrays = tuple(arrays)
    return list(lax.optimization_barrier((*arrays, *others))[: len(arrays)])


def partner(array, axis, by):
    size = lax.axis_size(axis)
    return lax.ppermute(array, axis, [(i, i ^ by) for i in range(size)])


def hold_lists(one, two):
    together = hold([*one, *two])
    return together[: len(one)], together[len(one) :]


def exchange(array, *axes):
    return lax.all_to_all(array, axes, 0, 0)


def swap_parts(parts):
    return [parts[0]] + [partner(parts[k], "head", k) for k in range(1, len(parts))]


def share_heads(array):
    return [array] + [partner(array, "head", k) for k in range(1, lax.axis_size("head"))]


def across_core(parts):
    return [partner(part, "dp", 1) for part in parts]


def to_chip(array, k):
    axis, by = [("blk", 1), ("dp", 2), (("dp", "blk"), 5)][k - 1]
    return partner(array, axis, by)


def plane_gather(array):
    chips = [array] + [to_chip(array, k) for k in (1, 2, 3)]
    return chips + across_core(chips)


def body(
    dec_in,
    enc_out,
    passage_len,
    dec_len,
    passage_owner,
    gain_self,
    gain_cross,
    gain_ffn,
    w_query,
    w_key,
    w_value,
    w_out,
    c_query,
    c_key,
    c_value,
    c_out,
    w_in,
    w_back,
    cotangent,
):
    blk_count = lax.axis_size("blk")
    dp_count = lax.axis_size("dp")
    head_count = lax.axis_size("head")
    small = blk_count == 2 and dp_count == 4
    chunk_count = blk_count * head_count
    plane = dp_count * blk_count
    width, depth = w_query.shape
    units = w_in.shape[1]
    rows = dec_in.shape[0]
    piece = rows // head_count
    passages = enc_out.shape[0] // LP
    head_place = lax.axis_index("head")
    blk_place = lax.axis_index("blk")
    core = lax.axis_index("dp") % 2
    gain_one, gain_two, gain_three = gain_self, gain_cross, gain_ffn

    half = width // 2
    slots = lax.dynamic_slice_in_dim(passage_owner, head_place * passages, passages) ^ blk_place
    lengths = lax.dynamic_slice_in_dim(passage_len, head_place * passages, passages)

    half = width // 2
    sides = [
        lax.dynamic_slice_in_dim(weight, blk_place % 2 * half, half, 0)
        for weight in (c_key, c_value, c_query, c_out)
    ]
    pair = lax.axis_index("dp") // 2 % 2
    mine = jnp.where(
        core == 0, jnp.where(pair == 0, *sides[:2]), jnp.where(pair == 0, *sides[2:])
    )
    near = [partner(mine, "head", k) for k in range(1, head_count)]
    normed_one, self_qkv, self_flat, *partials = call_self(
        after(dec_in, mine) if CFG["s_o"] == 1 else dec_in,
        dec_len, gain_one, w_query, w_key, w_value, w_out, head_count
    )
    partials = swap_parts(partials)
    if CFG["s_a"] == 1:
        near = hold(near, partials[1])
    elif CFG["s_a"] == 2:
        *near, self_flat = hold([*near, self_flat])
    (near,) = call(
        join_kernel, [shaped((len(near) * half, depth), bf16)], [], near, micros=0.3
    )
    beside = partner(near, "blk", 1)
    arrays = [near, beside, partner(near, "dp", 2)]
    if CFG["s_xy"] == 1 and blk_count == 2:
        arrays.append(partner(near, ("dp", "blk"), 5))
    else:
        arrays.append(partner(beside, "dp", 2))
    arrays = arrays + across_core(arrays)
    first, message = call(
        functools.partial(normed_kernel, head_count),
        [shaped((piece, depth), f32), shaped((chunk_count, piece, depth), bf16)],
        [],
        [*hold(partials, slots, lengths), dec_in, gain_two],
    )
    if CFG["s_a"] == 3:
        message, near, beside = hold([message, near, beside])
    chunks = exchange(message, "blk", "head")
    enc_keys, enc_values, weights = project(
        enc_out, (c_key, c_value, c_query, c_out), arrays, head_count - 1
    )
    key_full, value_full, query_full, cross_out_full = [Weight(weights, i) for i in range(4)]
    early, queries = call(
        functools.partial(query_kernel, blk_count, head_count),
        [
            shaped((rows, -(-(2 * depth + width) // 256) * 256), bf16),
            shaped((blk_count, rows, depth), bf16),
        ],
        [],
        [chunks, query_full, normed_one, self_flat],
        [pltpu.VMEM((rows, depth), bf16)],
    )
    if CFG["e_y"] == 0:
        early_beside = partner(after(early, enc_keys), "blk", 1)
    partials = cross_forward(
        slots, lengths, queries, enc_keys, enc_values, head_count, width
    )
    if CFG["e_y"] == 0:
        partials, early_beside = hold([partials, early_beside])
    cross, second, logsum, *messages = call(
        functools.partial(combine_kernel, width),
        [
            shaped((piece, depth), f32),
            shaped((piece, depth), f32),
            shaped((piece, STATS), f32),
        ]
        + [shaped((piece, depth + width), bf16)] * head_count,
        [],
        [exchange(partials, "blk", "head"), first, cross_out_full, gain_three],
    )
    if CFG["e_y"] == 0:
        early = [early, early_beside] if small else [early]
        if small:
            early += [partner(part, "dp", 2) for part in hold(early, second)]
    else:
        early = [after(early, second)]
        if small:
            early += [partner(early[0], "blk", 1), partner(early[0], "dp", 2)]
    chunks = swap_parts(messages)
    outs = call(
        functools.partial(ffn_kernel, head_count),
        [shaped((piece, 2 * depth), bf16)] * head_count
        + [
            shaped((rows, 2 * depth + 2 * units), bf16),
            shaped((rows, width), bf16),
        ],
        [],
        [*chunks, cotangent, w_in, w_back],
        [pltpu.VMEM((rows, depth), f32)],
    )
    wide, cross_cols = outs[head_count:]
    wide_beside = partner(wide, "blk", 1)
    wide = [wide, wide_beside, partner(wide, "dp", 2)] if small else [wide]
    if small and CFG["e_y"] == 1:
        early.append(partner(after(early[1], wide[0]), "dp", 2))
    upstream = swap_parts(outs[:head_count])
    grad_second, gain_ffn_part, layer, message = call(
        functools.partial(branch_kernel, head_count, width),
        [
            shaped((piece, depth), f32),
            shaped((1, depth), f32),
            shaped((piece, depth), bf16),
            shaped((chunk_count, piece, depth + STATS), bf16),
        ],
        [],
        [*upstream, second, gain_three, cotangent, cross_out_full, cross, logsum],
    )
    if small:
        if CFG["m_e"] == 1:
            message, *early = hold([message, *early])
    branches = exchange(message, "blk", "head")
    if small and CFG["e_c"] == 1:
        early = early + across_core(early)
        branches, *early = hold([branches, *early])
    query_grads, branch_two, enc_key_grads, enc_value_grads = cross_backward(
        slots,
        lengths,
        queries,
        cross_out_full,
        enc_keys,
        enc_values,
        branches,
        head_count,
        width,
    )
    query_grads = exchange(query_grads, "blk", "head")

    if small and CFG["w_x"] == 1:
        enc_key_grads, enc_value_grads = hold([enc_key_grads, enc_value_grads], *wide)
        wide.append(partner(after(wide[1], enc_key_grads), "dp", 2))
    elif small:
        wide.append(partner(wide[1], "dp", 2))
    shares = projection_grads(
        enc_key_grads, enc_value_grads, enc_out, cross_cols, branch_two, plane, head_count
    )
    if small and CFG["w_c"] == 1:
        wide_there = across_core(wide[:3])
        query_grads, shares, *wide_there = hold([query_grads, shares, *wide_there])
    elif CFG["t_cs"] == 1:
        query_grads, shares = hold([query_grads, shares])
    grad_first, gain_cross_part, *messages = call(
        first_kernel,
        [shaped((piece, depth), f32), shaped((1, depth), f32)]
        + [shaped((piece, depth + width), bf16)] * head_count,
        [],
        [query_grads, first, gain_two, query_full, grad_second],
    )
    if CFG["w_xy"] == 1:
        messages = hold(messages, *wide)
    chunks = swap_parts(messages)
    if small:
        if CFG["sh_q"] == 1:
            shares = after(shares, chunks[1])
        elif CFG["sh_q"] == 2:
            shares = after(shares, chunks[-1])
        elif CFG["t_shq"] == 1:
            shares = after(shares, messages[0])
        shares = exchange(shares, "dp", "blk")
    if CFG["e_p"] == 4:
        grad_enc = encoder_grads(
            *hold([enc_key_grads, enc_value_grads], messages[0]), key_full, value_full
        )
        chunks = hold(chunks, grad_enc)
    outs = call(
        functools.partial(self_back_kernel, head_count),
        (
            [shaped((piece, depth), bf16)] * head_count
            if CFG["t_rsz"] == "perm"
            else [shaped((head_count, piece, depth), bf16)]
        )
        + [
            shaped(
                (plane if small and CFG["t_late"] == "a2a" else 1, rows, depth + 4 * width), bf16
            )
        ],
        [dec_len],
        [*chunks, w_out, self_qkv, w_query, w_key, w_value],
        [pltpu.VMEM((rows, depth), f32), pltpu.VMEM((rows, depth + 4 * width), bf16)],
    )
    late = outs[-1]
    if small:
        if CFG["e_c"] == 0:
            early = hold(early, late)
            early = early + across_core(early)
        if CFG["w_c"] == 1:
            wide = wide + wide_there + across_core(hold(wide[3:], late))
        else:
            wide = hold(wide, late)
            wide = wide + across_core(wide)
    if not small:
        late = [late.reshape(late.shape[1:])]
    elif CFG["t_late"] == "a2a":
        late = [exchange(late, "dp", "blk")]
    else:
        late = late.reshape(late.shape[1:])
        late = [late, partner(late, "blk", 1), partner(late, "dp", 2)]
        if CFG["l_d"] == 1:
            late.append(partner(late[0], ("dp", "blk"), 5))
    if CFG["t_rsz"] == "perm":
        upstream = swap_parts(outs[:head_count])
    else:
        upstream = [exchange(outs[0], "head")]
    if small and CFG["l_p"] == 2:
        joined = hold([*upstream, *late])
        upstream, late = joined[: len(upstream)], joined[len(upstream) :]
        late.append(partner(late[1], "dp", 2))
    if CFG["t_shg"] == 1:
        (shares,) = hold([shares], *upstream)
    elif CFG["t_shg"] == 2:
        (shares,) = hold([shares], upstream[1])
    (message,) = call(
        functools.partial(input_kernel, len(upstream)),
        [shaped((head_count if CFG["t_agz"] == "a2a" else 1, 2 * piece + 16, depth), bf16)],
        [],
        [*upstream, dec_in, gain_one, grad_first, gain_cross_part, gain_ffn_part, layer],
        micros=3 * CFG["t_cost"],
    )
    if small and CFG["t_late"] == "perm" and CFG["l_p"] == 1:
        message, *late = hold([message, *late])
        late.append(partner(late[1], "dp", 2))
    if CFG["t_agz"] == "perm":
        chunks = share_heads(message.reshape(message.shape[1:]))
    else:
        chunks = [exchange(message, "head")]
    if CFG["t_shg"] == 3:
        shares = after(shares, chunks[1])
    elif CFG["t_shg"] == 4:
        shares = after(shares, message)
    pair = [enc_key_grads, enc_value_grads]
    if CFG["e_p"] == 1:
        pair = hold(pair, *upstream)
    elif CFG["e_p"] == 2:
        pair = hold(pair, message)
    elif CFG["e_p"] == 3:
        pair = hold(pair, chunks[1])
    if CFG["e_p"] != 4:
        grad_enc = encoder_grads(*pair, key_full, value_full)
        if CFG["e_p"] > 0:
            chunks = hold(chunks, grad_enc)
    if CFG["b_p"] == 3:
        wide = hold(wide, message)
    elif CFG["b_p"] == 4:
        wide = hold(wide, upstream[0])
    broad = call(
        functools.partial(wide_kernel, len(wide)),
        [shaped((depth, units), f32), shaped((units, depth), f32)],
        [],
        wide,
        [pltpu.VMEM((sum(part.shape[0] for part in wide), wide[0].shape[1]), bf16)],
        8 * CFG["t_cost"],
    )
    if CFG["b_p"] == 3 or CFG["b_p"] == 4:
        chunks = hold(chunks, broad[0])
    if small and CFG["l_p"] == 2 and CFG["l_xy"] == 1:
        *chunks, late[-1] = hold([*chunks, late[-1]])
    if small and CFG["t_late"] == "perm" and CFG["l_p"] == 0:
        joined = hold([*chunks, *late])
        chunks, late = joined[: len(chunks)], joined[len(chunks) :]
        if len(late) == 3:
            late.append(partner(late[1], "dp", 2))
    elif CFG["l_xy"] == 1:
        chunks = hold(chunks, late[-1])
    grad_in, gains, layer_out = call(
        functools.partial(place_kernel, head_count),
        [shaped((rows, depth), f32), shaped((8, depth), f32), shaped((rows, depth), bf16)],
        [],
        chunks,
        micros=3 * CFG["t_cost"],
    )
    if small:
        blocks, cross_share = call(
            share_kernel,
            [
                shaped((head_count, width // 4, depth), bf16),
                shaped((width // plane, depth), bf16),
            ],
            [],
            [shares],
            micros=3 * CFG["t_cost"],
        )
        blocks = exchange(blocks, "head")
        if CFG["t_p"] == 4:
            blocks, late[3] = hold([blocks, late[3]])
        if CFG["t_p"] == 1:
            (blocks,) = hold([blocks], grad_enc, broad[0], *late)
        elif CFG["t_p"] == 2:
            (blocks,) = hold([blocks], *late)
        elif CFG["t_p"] == 3:
            (blocks,) = hold([blocks], grad_enc, *late)
        (shares,) = call(
            spread_kernel,
            [shaped((plane, width // 4 + width // plane + 24, depth), bf16)],
            [],
            [blocks, cross_share, gains],
            micros=3 * CFG["t_cost"],
        )
        grad_c_key, grad_c_value, grad_c_out, gains = call(
            collect_kernel,
            [shaped((width, depth), f32)] * 3 + [shaped((8, depth), f32)],
            [],
            [exchange(shares, "dp", "blk")],
            micros=3 * CFG["t_cost"],
        )
    else:
        gains, shares = lax.psum((gains, shares.astype(f32)), ("dp", "blk"))
        blocks = shares[: 2 * depth].reshape(2, head_count, width, depth)
        blocks = jnp.swapaxes(blocks, 0, 1)
        blocks = sum(swap_parts([blocks[k] for k in range(head_count)]))
        grad_c_key, grad_c_value = blocks[0], blocks[1]
        grad_c_out = shares[2 * depth :]


    if small and CFG["t_late"] == "perm":
        late = late + across_core(late)
    slim = call(
        functools.partial(weight_kernel, len(early), len(late), width),
        [shaped((width, depth), f32)] * 5,
        [],
        [*early, *late],
        [
            pltpu.VMEM((sum(part.shape[0] for part in early), early[0].shape[1]), bf16),
            pltpu.VMEM((plane * rows if small else rows, late[0].shape[-1]), bf16),
        ],
        6 * CFG["t_cost"],
    )
    if not small:
        slim, broad = lax.psum((tuple(slim), tuple(broad)), ("dp", "blk"))
    return (
        layer_out,
        grad_in,
        grad_enc,
        gains[0],
        gains[1],
        gains[2],
        *slim,
        grad_c_key,
        grad_c_value,
        grad_c_out,
        *broad,
    )


def solution(mesh):
    rows = P(("dp", "blk"), None)
    enc = P(("dp", "blk", "head"), None)
    each = P(("dp", "blk"))
    heads = P("head", None)
    return jax.shard_map(
        body,
        mesh=mesh,
        in_specs=(
            rows,
            enc,
            each,
            each,
            each,
            P(),
            P(),
            P(),
            *[heads] * 8,
            P(None, "head"),
            heads,
            rows,
        ),
        out_specs=(rows, rows, enc, P(), P(), P(), *[heads] * 8, P(None, "head"), heads),
        check_vma=False,
    )
```

```python
import functools

import jax
import jax.numpy as jnp
from jax import lax
from jax.experimental import pallas as pl
from jax.experimental.pallas import tpu as pltpu
from jax.sharding import PartitionSpec as P

CFG = dict(
    s_o=1, s_a=1, s_xy=1, l_d=1, l_q=1, e_w=0, x_p=1, t_cost=0.05, k1=0.1, vmem=64, s_rs="f32", m_e=1, t_shg=3, e_c=0, w_c=0,
    t_late="perm", t_rsz="perm", t_agz="perm", t_shq=1, sh_q=0, cost=1.0, t_cs=1,
    t_p=0, w_x=1, w_xy=1, l_p=0, l_xy=0, e_p=4, b_p=0, e_y=1,
)
DHEAD = 64
LP = 384
LEAST = 3 * LP // 4
norm_epsilon = 1e-06
masked_score = -1e30
bf16 = jnp.bfloat16
f32 = jnp.float32
PAIR = 2 * DHEAD
STATS = 128
SECOND_LANE = 16
SPLIT_LANE = 32
VMEM_BYTES = CFG["vmem"] * 1024 * 1024


def nn(left, right):
    return lax.dot_general(left, right, (((1,), (0,)), ((), ())), preferred_element_type=f32)


def nt(left, right):
    return lax.dot_general(left, right, (((1,), (1,)), ((), ())), preferred_element_type=f32)


def tn(left, right):
    return lax.dot_general(left, right, (((0,), (0,)), ((), ())), preferred_element_type=f32)


def exact_nn(left, right):
    return lax.dot_general(
        left,
        right,
        (((1,), (0,)), ((), ())),
        precision=lax.Precision.HIGHEST,
        preferred_element_type=f32,
    )


def norm_scale(values):
    return lax.rsqrt(jnp.mean(values * values, axis=-1, keepdims=True) + norm_epsilon)


def normalize(values, gain):
    return values * norm_scale(values) * gain


def norm_back(upstream, values, gain):
    scale = norm_scale(values)
    unit = values * scale
    scaled = upstream * gain
    grad = scale * (scaled - unit * jnp.mean(scaled * unit, axis=-1, keepdims=True))
    return grad, jnp.sum(upstream * unit, axis=0, keepdims=True)


def cost(micros):
    return pl.CostEstimate(flops=0, bytes_accessed=int(micros * CFG["cost"] * 3e6), transcendentals=0)


def smem():
    return pl.BlockSpec(memory_space=pltpu.SMEM)


def shaped(shape, dtype):
    return jax.ShapeDtypeStruct(shape, dtype)


def whole(shape):
    return pl.BlockSpec(shape, lambda *_: (0,) * len(shape), pipeline_mode=pl.Buffered(1))


class Weight:
    def __init__(self, array, index):
        self.array, self.index = array, index
        self.shape = array.shape[1:]


def spec_of(array):
    if isinstance(array, Weight):
        block = (None, *array.shape)
        index = array.index
        return pl.BlockSpec(block, lambda *_: (index, 0, 0), pipeline_mode=pl.Buffered(1))
    return whole(array.shape)


def value_of(array):
    return array.array if isinstance(array, Weight) else array


def call(kernel, outs, scalars, arrays, scratch=(), micros=3.5, steps=1):
    def out_spec(out):
        if steps == 1:
            return whole(out.shape)
        return pl.BlockSpec((out.shape[0], out.shape[1] // steps), lambda n: (0, n))

    return pl.pallas_call(
        kernel,
        grid=(steps,),
        out_shape=tuple(outs),
        in_specs=[smem()] * len(scalars) + [spec_of(array) for array in arrays],
        out_specs=tuple(out_spec(out) for out in outs),
        scratch_shapes=list(scratch),
        cost_estimate=cost(micros),
        compiler_params=pltpu.CompilerParams(
            vmem_limit_bytes=VMEM_BYTES, dimension_semantics=("arbitrary",)
        ),
    )(*scalars, *[value_of(array) for array in arrays])


def my_head():
    return lax.axis_index("head")


def my_core():
    return lax.axis_index("dp") % 2


def my_blk():
    return lax.axis_index("blk")


def my_chip():
    return lax.axis_index("dp") // 2 * 2 + lax.axis_index("blk") % 2


def pack_stats(values):
    high = values.astype(bf16).astype(f32)
    middle = (values - high).astype(bf16).astype(f32)
    lowest = values - high - middle
    return (
        high + pltpu.roll(middle, SPLIT_LANE, 1) + pltpu.roll(lowest, 2 * SPLIT_LANE, 1)
    ).astype(bf16)


def unpack_stats(packed):
    packed = packed.astype(f32)
    return (
        packed
        + pltpu.roll(packed, STATS - SPLIT_LANE, 1)
        + pltpu.roll(packed, STATS - 2 * SPLIT_LANE, 1)
    )


def group_place(head_count, kb, kh):
    return (my_blk() ^ kb) * head_count + (my_head() ^ kh)


def rows_of(place, count):
    if isinstance(place, int):
        return slice(place * count, (place + 1) * count)
    return pl.ds(pl.multiple_of(place * count, count), count)


def head_blocks(width, head_count, shift):
    return [(j ^ shift) * width for j in range(head_count)]


def permuted(values, width, head_count, shift):
    if shift == 0:
        return values
    return jnp.concatenate(
        [values[:, o : o + width] for o in head_blocks(width, head_count, shift)], axis=1
    )


def self_probs(q, k, allowed):
    scores = jnp.where(allowed, nt(q, k), masked_score)
    raised = jnp.exp(scores - jnp.max(scores, axis=-1, keepdims=True))
    return raised / jnp.sum(raised, axis=-1, keepdims=True)


def causal(rows, length):
    at_q = lax.broadcasted_iota(jnp.int32, (rows, rows), 0)
    at_k = lax.broadcasted_iota(jnp.int32, (rows, rows), 1)
    return (at_k <= at_q) & (at_k.astype(f32) < length)


def self_kernel(dec_ref, len_ref, gain_ref, wq_ref, wk_ref, wv_ref, w_out_ref, *refs):
    normed_ref, qkv_ref, out_ref, *partials = refs[:-1]
    total = refs[-1]
    rows = normed_ref.shape[0]
    width = wq_ref.shape[0]
    normed = normalize(dec_ref[...].astype(f32), gain_ref[...].astype(f32)[None, :]).astype(bf16)
    normed_ref[...] = normed
    for i, weight in enumerate((wq_ref, wk_ref, wv_ref)):
        qkv_ref[:, i * width : (i + 1) * width] = nt(normed, weight[...]).astype(bf16)
    allowed = causal(rows, len_ref[0].astype(f32))
    outs = []
    for h in range(width // DHEAD):
        o = h * DHEAD
        probs = self_probs(
            qkv_ref[:, o : o + DHEAD], qkv_ref[:, width + o : width + o + DHEAD], allowed
        )
        outs.append(nn(probs.astype(bf16), qkv_ref[:, 2 * width + o : 2 * width + o + DHEAD]))
    attended = jnp.concatenate(outs, axis=1).astype(bf16)
    out_ref[...] = attended
    total[...] = nn(attended, w_out_ref[...])
    piece = rows // len(partials)
    for k, partial in enumerate(partials):
        partial[...] = total[rows_of(my_head() ^ k, piece), :].astype(partial.dtype)


def call_self(dec_in, dec_len, gain, w_query, w_key, w_value, w_out, head_count):
    rows, depth = dec_in.shape
    width = w_query.shape[0]
    arrays = (dec_in, dec_len, gain, w_query, w_key, w_value, w_out)
    outs = [
        shaped((rows, depth), bf16),
        shaped((rows, 3 * width), bf16),
        shaped((rows, width), bf16),
    ] + [shaped((rows // head_count, depth), f32 if CFG["s_rs"] == "f32" else bf16)] * head_count
    return pl.pallas_call(
        self_kernel,
        grid=(1,),
        out_shape=tuple(outs),
        in_specs=[smem() if array is dec_len else whole(array.shape) for array in arrays],
        out_specs=tuple(whole(out.shape) for out in outs),
        scratch_shapes=[pltpu.VMEM((rows, depth), f32)],
        cost_estimate=cost(CFG["k1"]),
        compiler_params=pltpu.CompilerParams(
            vmem_limit_bytes=VMEM_BYTES, dimension_semantics=("arbitrary",)
        ),
    )(*arrays)


def normed_kernel(count, *refs):
    chunks = refs[:count]
    dec_ref, gain_ref, first_ref, message_ref = refs[count:]
    piece = first_ref.shape[0]
    first = dec_ref[rows_of(my_head(), piece), :].astype(f32) + sum(
        chunk[...].astype(f32) for chunk in chunks
    )
    first_ref[...] = first
    normed = normalize(first, gain_ref[...].astype(f32)[None, :]).astype(bf16)
    for i in range(message_ref.shape[0]):
        message_ref[i] = normed


def join_kernel(*refs):
    start = 0
    for part in refs[:-1]:
        refs[-1][start : start + part.shape[0], :] = part[...]
        start += part.shape[0]


def put_weights(count, owns, arrays, out_ref):
    rows = owns[0].shape[0]
    half = rows // 2
    for weight, own in enumerate(owns):
        out_ref[weight, :rows, :] = own[...]
    pair = lax.axis_index("dp") // 2 % 2
    for place, array in enumerate(arrays):
        weight = (my_core() ^ place // 4) * 2 + (pair ^ place // 2 % 2)
        side = my_blk() % 2 ^ place % 2
        for k in range(count):
            start = pl.multiple_of((k + 1) * rows + side * half, half)
            out_ref[weight, pl.ds(start, half), :] = array[k * half : (k + 1) * half, :]


def query_kernel(blk_count, head_count, chunks_ref, c_query_ref, one_ref, self_ref, *refs):
    early_ref, q_ref, normed = refs
    rows, depth = one_ref.shape
    width = self_ref.shape[1]
    piece = rows // head_count
    for kb in range(blk_count):
        for i in range(head_count):
            place = (my_blk() ^ kb) * head_count + i
            normed[i * piece : (i + 1) * piece, :] = chunks_ref[place]
        if kb == 0:
            early_ref[:, :depth] = one_ref[...]
            early_ref[:, depth : 2 * depth] = normed[...]
            early_ref[:, 2 * depth : 2 * depth + width] = self_ref[...]
            early_ref[:, 2 * depth + width :] = jnp.zeros(
                (rows, early_ref.shape[1] - 2 * depth - width), bf16
            )
        q_ref[kb] = nt(normed[...], c_query_ref[...]).astype(bf16)


def project_kernel(count, enc_ref, *refs):
    owns, arrays, (key_ref, value_ref, weights_ref) = refs[:4], refs[4:-3], refs[-3:]

    @pl.when(pl.program_id(0) == 0)
    def _():
        put_weights(count, owns, arrays, weights_ref)

    key_ref[...] = nt(enc_ref[...], weights_ref[0]).astype(bf16)
    value_ref[...] = nt(enc_ref[...], weights_ref[1]).astype(bf16)


def project(enc, owns, arrays, count):
    slots, depth = enc.shape
    block = pl.BlockSpec((LP, depth), lambda p: (p, 0))
    weights = shaped((4, depth, depth), bf16)
    return pl.pallas_call(
        functools.partial(project_kernel, count),
        grid=(slots // LP,),
        in_specs=[block] + [whole(array.shape) for array in (*owns, *arrays)],
        out_specs=(block, block, whole(weights.shape)),
        out_shape=(shaped(enc.shape, bf16), shaped(enc.shape, bf16), weights),
        cost_estimate=cost(9),
        compiler_params=pltpu.CompilerParams(
            vmem_limit_bytes=VMEM_BYTES, dimension_semantics=("arbitrary",)
        ),
    )(enc, *owns, *arrays)


def spread_pairs(values, target, kb):
    rows = values.shape[0]
    for j in range(values.shape[1] // PAIR):
        pair = values[:, j * PAIR : (j + 1) * PAIR]
        lane = lax.broadcasted_iota(jnp.int32, pair.shape, 1)
        zero = jnp.zeros_like(pair)
        target[kb, j, 0:rows, :] = jnp.where(lane < DHEAD, pair, zero)
        target[kb, j, rows : 2 * rows, :] = jnp.where(lane < DHEAD, zero, pair)


def within(values, length, fill):
    place = LEAST + lax.broadcasted_iota(jnp.int32, (LP - LEAST, values.shape[1]), 0)
    last = jnp.where(place < length, values[LEAST:], fill)
    return jnp.concatenate([values[:LEAST], last], axis=0)


def pair_columns(j):
    return slice(j * PAIR, (j + 1) * PAIR)


def add_pair(target, slot, j, update, factor=None):
    rows = target.shape[2]
    for i in range(2):
        span = slice(j * PAIR + i * DHEAD, j * PAIR + (i + 1) * DHEAD)
        own = update[i * DHEAD : (i + 1) * DHEAD, i * rows : (i + 1) * rows]
        old = target[slot, span, :]
        if factor is not None:
            old = old * factor[:, i * rows : (i + 1) * rows]
        target[slot, span, :] = old + own


def cross_forward_kernel(blk_count, head_count, width, *refs):
    slot_ref, len_ref, q_ref, k_ref, v_ref = refs[:5]
    out_ref, q2, acc, highest, totals, stat, flat, flat_stat, held, probs, factors = refs[5:]
    rows, depth = q_ref.shape[1], q_ref.shape[2]
    pairs = depth // PAIR
    step = pl.program_id(0)

    @pl.when(step == 0)
    def _():
        for kb in range(blk_count):
            spread_pairs(q_ref[kb], q2, kb)
        highest[...] = jnp.full(highest.shape, masked_score, f32)
        totals[...] = jnp.zeros(totals.shape, f32)
        acc[...] = jnp.zeros(acc.shape, f32)

    slot = slot_ref[step]
    for j in range(pairs):
        scores = within(nt(k_ref[:, pair_columns(j)], q2[slot, j]), len_ref[step], masked_score)
        held[j] = scores
        before = highest[slot, j : j + 1, :]
        newest = jnp.maximum(before, jnp.max(scores, axis=0, keepdims=True))
        factors[j : j + 1, :] = jnp.exp(before - newest)
        highest[slot, j : j + 1, :] = newest
    for j in range(pairs):
        raised = jnp.exp(held[j] - highest[slot, j : j + 1, :])
        probs[j] = raised.astype(bf16)
        totals[slot, j : j + 1, :] = totals[slot, j : j + 1, :] * factors[
            j : j + 1, :
        ] + jnp.sum(raised, axis=0, keepdims=True)
    for j in range(pairs):
        update = tn(v_ref[:, pair_columns(j)], probs[j])
        add_pair(acc, slot, j, update, factors[j : j + 1, :])

    @pl.when(step == pl.num_programs(0) - 1)
    def _():
        stat[...] = jnp.zeros(stat.shape, f32)
        piece = rows // head_count
        per = width // DHEAD
        for kb in range(blk_count):
            flat[...] = acc[kb].T
            for kh in range(head_count):
                for head in range(depth // DHEAD):
                    at = ((head // per) ^ kh) * per + head % per
                    lanes = slice((head % 2) * rows, (head % 2 + 1) * rows)
                    stat[at : at + 1, :] = highest[kb, head // 2 : head // 2 + 1, lanes]
                    stat[SECOND_LANE + at : SECOND_LANE + at + 1, :] = totals[
                        kb, head // 2 : head // 2 + 1, lanes
                    ]
                flat_stat[...] = stat[...].T
                mine = rows_of(my_head() ^ kh, piece)
                place = group_place(head_count, kb, kh)
                out_ref[place, :, :depth] = permuted(
                    flat[mine, :].astype(bf16), width, head_count, kh
                )
                out_ref[place, :, depth:] = pack_stats(flat_stat[mine, :])


def cross_forward(slots, lengths, queries, keys, values, head_count, width):
    blk_count, rows, depth = queries.shape
    passages = slots.shape[0]
    piece = rows // head_count
    chunk_count = blk_count * head_count
    pairs = depth // PAIR
    grid = pltpu.PrefetchScalarGridSpec(
        num_scalar_prefetch=2,
        grid=(passages,),
        in_specs=[
            whole((blk_count, rows, depth)),
            pl.BlockSpec((LP, depth), lambda p, *_: (p, 0)),
            pl.BlockSpec((LP, depth), lambda p, *_: (p, 0)),
        ],
        out_specs=whole((chunk_count, piece, depth + STATS)),
        scratch_shapes=[
            pltpu.VMEM((blk_count, pairs, 2 * rows, PAIR), bf16),
            pltpu.VMEM((blk_count, depth, rows), f32),
            pltpu.VMEM((blk_count, 8, 2 * rows), f32),
            pltpu.VMEM((blk_count, 8, 2 * rows), f32),
            pltpu.VMEM((STATS, rows), f32),
            pltpu.VMEM((rows, depth), f32),
            pltpu.VMEM((rows, STATS), f32),
            pltpu.VMEM((pairs, LP, 2 * rows), f32),
            pltpu.VMEM((pairs, LP, 2 * rows), bf16),
            pltpu.VMEM((8, 2 * rows), f32),
        ],
    )
    return pl.pallas_call(
        functools.partial(cross_forward_kernel, blk_count, head_count, width),
        out_shape=shaped((chunk_count, piece, depth + STATS), bf16),
        cost_estimate=cost(15),
        grid_spec=grid,
        compiler_params=pltpu.CompilerParams(
            vmem_limit_bytes=VMEM_BYTES, dimension_semantics=("arbitrary",)
        ),
    )(slots, lengths, queries, keys, values)


def head_matrix(depth):
    head = lax.broadcasted_iota(jnp.int32, (STATS, depth), 0)
    column = lax.broadcasted_iota(jnp.int32, (STATS, depth), 1)
    return (head == column // DHEAD).astype(f32)


def combine_kernel(width, *refs):
    chunks, first_ref, c_out_ref, gain_ref, cross_ref, second_ref, logsum_ref = refs[:7]
    messages = refs[7:]
    piece, depth = cross_ref.shape
    stats = [unpack_stats(chunks[i, :, depth:]) for i in range(chunks.shape[0])]
    highest = stats[0]
    for other in stats[1:]:
        highest = jnp.maximum(highest, other)
    lane = lax.broadcasted_iota(jnp.int32, (piece, STATS), 1)
    real = lane < depth // DHEAD
    weights = [jnp.where(real, jnp.exp(one - highest), 0.0) for one in stats]
    total = sum(w * pltpu.roll(one, STATS - SECOND_LANE, 1) for w, one in zip(weights, stats))
    total = jnp.where(real, total, 1.0)
    logsum_ref[...] = jnp.where(real, highest + jnp.log(total), 0.0)
    spread = head_matrix(depth)
    weighted = exact_nn(jnp.concatenate(weights, axis=0), spread)
    cross = sum(
        chunks[i, :, :depth].astype(f32) * weighted[i * piece : (i + 1) * piece]
        for i in range(chunks.shape[0])
    )
    cross = cross / exact_nn(total, spread)
    cross_ref[...] = cross
    rounded = cross.astype(bf16)
    second = first_ref[...] + nn(rounded, c_out_ref[...])
    second_ref[...] = second
    normed = normalize(second, gain_ref[...].astype(f32)[None, :]).astype(bf16)
    for k, message in enumerate(messages):
        message[:, :depth] = normed
        message[:, depth:] = rounded[:, k * width : (k + 1) * width]


def ffn_kernel(count, *refs):
    chunks = refs[:count]
    cot_ref, w_in_ref, w_back_ref = refs[count : count + 3]
    grads = refs[count + 3 : 2 * count + 3]
    wide_ref, cols_ref, total = refs[2 * count + 3 :]
    piece, depth = grads[0].shape[0], grads[0].shape[1] // 2
    for k, chunk in enumerate(chunks):
        mine = rows_of(my_head() ^ k, piece)
        wide_ref[mine, :depth] = chunk[:, :depth]
        cols_ref[mine, :] = chunk[:, depth:]
    units = w_in_ref.shape[1]
    before = nn(wide_ref[:, :depth], w_in_ref[...])
    root = 0.7978845608028654
    cube = 0.044715
    square = before * before
    bend = jnp.tanh(root * (before + cube * before * square))
    hidden = (0.5 * before * (1.0 + bend)).astype(bf16)
    slope = 0.5 * (1.0 + bend) + 0.5 * before * (1.0 - bend * bend) * root * (
        1.0 + 3.0 * cube * square
    )
    pre_grad = (nt(cot_ref[...], w_back_ref[...]) * slope).astype(bf16)
    total[...] = nt(pre_grad, w_in_ref[...])
    wide_ref[:, depth : depth + units] = hidden
    wide_ref[:, depth + units : depth + 2 * units] = pre_grad
    wide_ref[:, depth + 2 * units :] = cot_ref[...]
    for k, grad in enumerate(grads):
        grad[:, :depth] = total[rows_of(my_head() ^ k, piece), :].astype(bf16)
    total[...] = nn(hidden, w_back_ref[...])
    for k, grad in enumerate(grads):
        grad[:, depth:] = total[rows_of(my_head() ^ k, piece), :].astype(bf16)


def branch_kernel(head_count, width, *refs):
    chunks = refs[:head_count]
    second_ref, gain_ref, cot_ref, c_out_ref, cross_ref, logsum_ref = refs[
        head_count : head_count + 6
    ]
    grad_ref, gain_grad_ref, layer_ref, message_ref = refs[head_count + 6 :]
    piece, depth = second_ref.shape
    received = sum(chunk[...].astype(f32) for chunk in chunks)
    upstream = received[:, :depth]
    layer_ref[...] = (second_ref[...] + received[:, depth:]).astype(bf16)
    grad, gain_grad_ref[...] = norm_back(upstream, second_ref[...], gain_ref[...].astype(f32)[None, :])
    grad = cot_ref[rows_of(my_head(), piece), :].astype(f32) + grad
    grad_ref[...] = grad
    branch = grad.astype(bf16)
    grad_cross = nt(branch, c_out_ref[...]).astype(bf16).astype(f32)
    spread = head_matrix(depth)
    deltas = lax.dot_general(
        grad_cross * cross_ref[...],
        spread,
        (((1,), (1,)), ((), ())),
        precision=lax.Precision.HIGHEST,
        preferred_element_type=f32,
    )
    stats = logsum_ref[...] + pltpu.roll(deltas, SECOND_LANE, 1)
    per = width // DHEAD
    heads = depth // DHEAD
    source = lax.broadcasted_iota(jnp.int32, (STATS, STATS), 0)
    target = lax.broadcasted_iota(jnp.int32, (STATS, STATS), 1)
    place = source % SECOND_LANE
    for k in range(head_count):
        moved = (source - place) + ((place // per) ^ k) * per + place % per
        shuffle = ((target == moved) & (place < heads) & (source < 2 * SECOND_LANE)).astype(f32)
        aligned = exact_nn(stats, shuffle)
        packed = pack_stats(aligned)
        for kb in range(message_ref.shape[0] // head_count):
            entry = group_place(head_count, kb, k)
            message_ref[entry, :, :depth] = branch
            message_ref[entry, :, depth:] = packed


def cross_backward_kernel(blk_count, head_count, width, *refs):
    slot_ref, len_ref, q_ref, c_out_ref, k_ref, v_ref = refs[:6]
    chunks, out_ref, branch_ref, grad_k_ref, grad_v_ref = refs[6:11]
    q2, g2, stats, branch, flat_stat, grad_q, flat = refs[11:18]
    held, grad_probs, probs, grad_scores = refs[18:]
    rows, depth = q_ref.shape[1], q_ref.shape[2]
    pairs = depth // PAIR
    piece = rows // head_count
    step = pl.program_id(0)

    @pl.when(step == 0)
    def _():
        for kb in range(blk_count):
            for i in range(head_count):
                place = (my_blk() ^ kb) * head_count + i
                span = slice(i * piece, (i + 1) * piece)
                branch[span, :] = chunks[place, :, :depth]
                flat_stat[span, :] = unpack_stats(chunks[place, :, depth:])
            if kb == 0:
                branch_ref[...] = branch[...]
            stats[kb] = flat_stat[...].T
            spread_pairs(q_ref[kb], q2, kb)
            spread_pairs(nt(branch[...], c_out_ref[...]).astype(bf16), g2, kb)
        grad_q[...] = jnp.zeros(grad_q.shape, f32)

    slot = slot_ref[step]

    def both_heads(first):
        return jnp.concatenate(
            [stats[slot, first : first + 1, :], stats[slot, first + 1 : first + 2, :]], axis=1
        )

    for j in range(pairs):
        held[j] = nt(k_ref[:, pair_columns(j)], q2[slot, j])
        grad_probs[j] = nt(v_ref[:, pair_columns(j)], g2[slot, j])
    for j in range(pairs):
        raised = within(jnp.exp(held[j] - both_heads(2 * j)), len_ref[step], 0.0)
        probs[j] = raised.astype(bf16)
        grad_scores[j] = (raised * (grad_probs[j] - both_heads(SECOND_LANE + 2 * j))).astype(bf16)
    for j in range(pairs):
        grad_v_ref[:, pair_columns(j)] = nn(probs[j], g2[slot, j]).astype(bf16)
        grad_k_ref[:, pair_columns(j)] = nn(grad_scores[j], q2[slot, j]).astype(bf16)
        add_pair(grad_q, slot, j, tn(k_ref[:, pair_columns(j)], grad_scores[j]))

    @pl.when(step == pl.num_programs(0) - 1)
    def _():
        for kb in range(blk_count):
            flat[...] = grad_q[kb].T
            for kh in range(head_count):
                mine = rows_of(my_head() ^ kh, piece)
                out_ref[group_place(head_count, kb, kh)] = permuted(
                    flat[mine, :].astype(bf16), width, head_count, kh
                )


def cross_backward(slots, lengths, queries, c_out, keys, values, chunks, head_count, width):
    blk_count, rows, depth = queries.shape
    passages = slots.shape[0]
    piece = rows // head_count
    chunk_count = blk_count * head_count
    pairs = depth // PAIR
    passage = pl.BlockSpec((LP, depth), lambda p, *_: (p, 0))
    grid = pltpu.PrefetchScalarGridSpec(
        num_scalar_prefetch=2,
        grid=(passages,),
        in_specs=[
            whole((blk_count, rows, depth)),
            spec_of(c_out),
            passage,
            passage,
            whole(chunks.shape),
        ],
        out_specs=(
            whole((chunk_count, piece, depth)),
            whole((rows, depth)),
            passage,
            passage,
        ),
        scratch_shapes=[
            pltpu.VMEM((blk_count, pairs, 2 * rows, PAIR), bf16),
            pltpu.VMEM((blk_count, pairs, 2 * rows, PAIR), bf16),
            pltpu.VMEM((blk_count, STATS, rows), f32),
            pltpu.VMEM((rows, depth), bf16),
            pltpu.VMEM((rows, STATS), f32),
            pltpu.VMEM((blk_count, depth, rows), f32),
            pltpu.VMEM((rows, depth), f32),
            pltpu.VMEM((pairs, LP, 2 * rows), f32),
            pltpu.VMEM((pairs, LP, 2 * rows), f32),
            pltpu.VMEM((pairs, LP, 2 * rows), bf16),
            pltpu.VMEM((pairs, LP, 2 * rows), bf16),
        ],
    )
    return pl.pallas_call(
        functools.partial(cross_backward_kernel, blk_count, head_count, width),
        out_shape=(
            shaped((chunk_count, piece, depth), bf16),
            shaped((rows, depth), bf16),
            shaped(keys.shape, bf16),
            shaped(keys.shape, bf16),
        ),
        cost_estimate=cost(16),
        grid_spec=grid,
        compiler_params=pltpu.CompilerParams(
            vmem_limit_bytes=VMEM_BYTES, dimension_semantics=("arbitrary",)
        ),
    )(slots, lengths, queries, value_of(c_out), keys, values, chunks)


def first_kernel(*refs):
    chunks, first_ref, gain_ref, c_query_ref, second_grad_ref = refs[:5]
    grad_ref, gain_grad_ref = refs[5:7]
    messages = refs[7:]
    piece, depth = grad_ref.shape
    width = messages[0].shape[1] - depth
    grad_q = sum(chunks[i].astype(f32) for i in range(chunks.shape[0])).astype(bf16)
    upstream = nn(grad_q, c_query_ref[...])
    grad, gain_grad_ref[...] = norm_back(upstream, first_ref[...], gain_ref[...].astype(f32)[None, :])
    grad = second_grad_ref[...] + grad
    grad_ref[...] = grad
    branch = grad.astype(bf16)
    for k, message in enumerate(messages):
        message[:, :depth] = branch
        message[:, depth:] = grad_q[:, k * width : (k + 1) * width]


def self_back_kernel(count, len_ref, *refs):
    chunks = refs[:count]
    w_out_ref, qkv_ref, wq_ref, wk_ref, wv_ref = refs[count : count + 5]
    grads, (sides_ref, total, side_ref) = refs[count + 5 : -3], refs[-3:]
    width, depth = wq_ref.shape
    rows = side_ref.shape[0]
    piece = rows // count
    start = depth + width
    for k, chunk in enumerate(chunks):
        mine = rows_of(my_head() ^ k, piece)
        side_ref[mine, :start] = chunk[...]
    grad_self = nt(side_ref[:, :depth], w_out_ref[...]).astype(bf16)
    allowed = causal(rows, len_ref[0].astype(f32))
    grad_q, grad_k, grad_v = [], [], []
    for h in range(width // DHEAD):
        o = h * DHEAD
        q = qkv_ref[:, o : o + DHEAD]
        k = qkv_ref[:, width + o : width + o + DHEAD]
        v = qkv_ref[:, 2 * width + o : 2 * width + o + DHEAD]
        g = grad_self[:, o : o + DHEAD]
        probs = self_probs(q, k, allowed)
        grad_probs = nt(g, v)
        delta = jnp.sum(probs * grad_probs, axis=-1, keepdims=True)
        grad_scores = (probs * (grad_probs - delta)).astype(bf16)
        grad_q.append(nn(grad_scores, k))
        grad_k.append(tn(grad_scores, q))
        grad_v.append(tn(probs.astype(bf16), g))
    flat = [jnp.concatenate(parts, axis=1).astype(bf16) for parts in (grad_q, grad_k, grad_v)]
    for i, part in enumerate(flat):
        side_ref[:, start + i * width : start + (i + 1) * width] = part
    total[...] = nn(flat[0], wq_ref[...]) + nn(flat[1], wk_ref[...]) + nn(flat[2], wv_ref[...])
    if len(grads) == 1:
        for i in range(count):
            grads[0][i] = total[i * piece : (i + 1) * piece, :].astype(bf16)
    else:
        for k, grad in enumerate(grads):
            grad[...] = total[rows_of(my_head() ^ k, piece), :].astype(bf16)
    for i in range(sides_ref.shape[0]):
        sides_ref[i] = side_ref[...]


def input_kernel(count, *refs):
    chunks = refs[:count]
    dec_ref, gain_ref, first_grad_ref, cross_gain_ref, ffn_gain_ref, layer_ref = refs[count:-1]
    message_ref = refs[-1]
    if count == 1:
        chunks = [chunks[0].at[i] for i in range(chunks[0].shape[0])]
    piece, depth = chunks[0].shape
    upstream = sum(chunk[...].astype(f32) for chunk in chunks)
    values = dec_ref[rows_of(my_head(), piece), :].astype(f32)
    grad, self_gain = norm_back(upstream, values, gain_ref[...].astype(f32)[None, :])
    grad = (first_grad_ref[...] + grad).astype(bf16)
    gains = gain_rows([self_gain, cross_gain_ref[...], ffn_gain_ref[...]])
    fill = jnp.zeros((message_ref.shape[1] - 2 * piece - len(gains), depth), f32)
    gains = jnp.concatenate([*gains, fill], axis=0).astype(bf16)
    for i in range(message_ref.shape[0]):
        message_ref[i, :piece, :] = grad
        message_ref[i, piece : 2 * piece, :] = layer_ref[...]
        message_ref[i, 2 * piece :, :] = gains


def gain_rows(gains):
    rows = []
    for rest in gains:
        for step in range(3):
            rows.append(rest.astype(bf16).astype(f32))
            rest = rest - rows[-1]
    return rows


def gain_sums(rows):
    return [jnp.sum(rows[3 * i : 3 * i + 3, :], axis=0, keepdims=True) for i in range(3)]


def place_kernel(count, *refs):
    chunks, (out_ref, gain_ref, layer_ref) = refs[:-3], refs[-3:]
    piece = out_ref.shape[0] // count
    if len(chunks) == 1:
        chunks = [chunks[0].at[i] for i in range(count)]
        places = range(count)
    else:
        places = [my_head() ^ k for k in range(count)]
    for place, chunk in zip(places, chunks):
        out_ref[rows_of(place, piece), :] = chunk[:piece, :].astype(f32)
        layer_ref[rows_of(place, piece), :] = chunk[piece : 2 * piece, :]
    gains = gain_sums(sum(chunk[2 * piece :, :].astype(f32) for chunk in chunks))
    fill = jnp.zeros((gain_ref.shape[0] - len(gains), gain_ref.shape[1]), f32)
    gain_ref[...] = jnp.concatenate([*gains, fill], axis=0)


def weight_kernel(early_count, late_count, width, *refs):
    early, late = refs[:early_count], refs[early_count : early_count + late_count]
    wq_ref, wk_ref, wv_ref, out_ref, query_ref, normed, side = refs[early_count + late_count :]
    depth = wq_ref.shape[1]
    stack_up(early, normed)
    stack_up(late, side)
    start = depth + width
    qkv = tn(side[:, start:], normed[:, :depth])
    for i, target in enumerate((wq_ref, wk_ref, wv_ref)):
        target[...] = qkv[i * width : (i + 1) * width]
    query_ref[...] = tn(side[:, depth:start], normed[:, depth : 2 * depth])
    out_ref[...] = tn(normed[:, 2 * depth : 2 * depth + width], side[:, :depth])


def stack_up(parts, target):
    start = 0
    if len(parts) == 1 and len(parts[0].shape) == 3:
        place = lax.axis_index("dp")
        entries = [(place ^ k) * 2 + (my_blk() ^ b) for k in (0, 2, 1, 3) for b in (0, 1)]
        rows = parts[0].shape[1]
        for i, entry in enumerate(entries):
            target[i * rows : (i + 1) * rows, :] = parts[0][entry]
        return
    for part in parts:
        target[start : start + part.shape[0], :] = part[...]
        start += part.shape[0]


def wide_kernel(count, *refs):
    in_ref, back_ref, stack = refs[count:]
    depth, units = in_ref.shape
    stack_up(refs[:count], stack)
    in_ref[...] = tn(stack[:, :depth], stack[:, depth + units : depth + 2 * units])
    back_ref[...] = tn(stack[:, depth : depth + units], stack[:, depth + 2 * units :])


def projection_grad_kernel(head_count, plane, *refs):
    keys_ref, values_ref, enc_ref, cols_ref, branch_ref, out_ref, total = refs
    step = pl.program_id(0)
    count, depth = total.shape
    width = cols_ref.shape[1]
    blocks = count // width

    @pl.when(step == 0)
    def _():
        cross = tn(cols_ref[...], branch_ref[...]).astype(bf16)
        if len(out_ref.shape) == 2:
            out_ref[2 * depth :, :] = cross
        else:
            size = width // plane
            for device in range(plane):
                start = depth // 4
                out_ref[device, start : start + size, :] = cross[device * size : (device + 1) * size]

    for weight, grad_ref in enumerate((keys_ref, values_ref)):
        total[...] = tn(grad_ref[...], enc_ref[...])
        if len(out_ref.shape) == 2:
            start = pl.multiple_of(weight * depth + step * count, 16)
            out_ref[pl.ds(start, count), :] = total[...].astype(bf16)
            continue
        size = width // 4
        for block in range(blocks):
            place = pl.multiple_of((step * blocks + block) * size, 16)
            for part in range(4):
                start = block * width + part * size
                device = (part // 2 * 2 + weight) * 2 + part % 2
                out_ref[device, pl.ds(place, size), :] = total[start : start + size, :].astype(bf16)


def projection_grads(key_grads, value_grads, enc, cross_cols, branch, plane, head_count):
    slots, depth = enc.shape
    width = cross_cols.shape[1]
    steps = 2
    block = pl.BlockSpec((slots, depth // steps), lambda j: (0, j))
    if plane == 8:
        out = shaped((plane, -(-(depth // 4 + width // plane) // 16) * 16, depth), bf16)
    else:
        out = shaped((2 * depth + width, depth), bf16)
    return pl.pallas_call(
        functools.partial(projection_grad_kernel, head_count, plane),
        grid=(steps,),
        in_specs=[block, block, whole(enc.shape), whole(cross_cols.shape), whole(branch.shape)],
        out_specs=whole(out.shape),
        out_shape=out,
        scratch_shapes=[pltpu.VMEM((depth // steps, depth), f32)],
        cost_estimate=cost(4),
        compiler_params=pltpu.CompilerParams(
            vmem_limit_bytes=VMEM_BYTES, dimension_semantics=("arbitrary",)
        ),
    )(key_grads, value_grads, enc, cross_cols, branch)


def encoder_grad_kernel(keys_ref, values_ref, key_ref, value_ref, out_ref):
    out_ref[...] = nn(keys_ref[...], key_ref[...]) + nn(values_ref[...], value_ref[...])


def encoder_grads(key_grads, value_grads, key_full, value_full):
    slots, depth = key_grads.shape
    block = pl.BlockSpec((LP, depth), lambda p: (p, 0))
    return pl.pallas_call(
        encoder_grad_kernel,
        grid=(slots // LP,),
        in_specs=[block, block, spec_of(key_full), spec_of(value_full)],
        out_specs=block,
        out_shape=shaped((slots, depth), f32),
        cost_estimate=cost(7 * CFG["t_cost"]),
        compiler_params=pltpu.CompilerParams(
            vmem_limit_bytes=VMEM_BYTES, dimension_semantics=("arbitrary",)
        ),
    )(key_grads, value_grads, value_of(key_full), value_of(value_full))


def share_kernel(shares_ref, blocks_ref, cross_ref):
    count, size = blocks_ref.shape[:2]
    total = sum(shares_ref[i].astype(f32) for i in range(shares_ref.shape[0]))
    for k in range(count):
        blocks_ref[my_head() ^ k] = total[k * size : (k + 1) * size].astype(bf16)
    cross_ref[...] = total[count * size : count * size + cross_ref.shape[0]].astype(bf16)


def spread_kernel(blocks_ref, cross_ref, gains_ref, out_ref):
    size, more = blocks_ref.shape[1], cross_ref.shape[0]
    block = sum(blocks_ref[i].astype(f32) for i in range(blocks_ref.shape[0])).astype(bf16)
    pieces = gain_rows([gains_ref[i : i + 1, :] for i in range(3)])
    fill = out_ref.shape[1] - size - more - len(pieces)
    pieces.append(jnp.zeros((fill, out_ref.shape[2]), f32))
    tail = jnp.concatenate([cross_ref[...].astype(f32), *pieces], axis=0).astype(bf16)
    for device in range(out_ref.shape[0]):
        out_ref[device, :size, :] = block
        out_ref[device, size:, :] = tail


def collect_kernel(shares_ref, key_ref, value_ref, cross_ref, *gain_refs):
    plane = shares_ref.shape[0]
    size = key_ref.shape[0] // 4
    more = cross_ref.shape[0] // plane
    total = 0.0
    for device in range(plane):
        place, blk = device // 2, device % 2
        target = value_ref if place % 2 else key_ref
        part = place // 2 * 2 + blk
        share = shares_ref[device].astype(f32)
        target[part * size : (part + 1) * size, :] = share[:size]
        cross_ref[device * more : (device + 1) * more, :] = share[size : size + more]
        total = total + share[size + more :]
    for gain_ref, gain in zip(gain_refs, gain_sums(total)):
        gain_ref[...] = gain[0]


def after(array, *others):
    return lax.optimization_barrier((array, *others))[0]


def hold(arrays, *others):
    arrays = tuple(arrays)
    return list(lax.optimization_barrier((*arrays, *others))[: len(arrays)])


def partner(array, axis, by):
    size = lax.axis_size(axis)
    return lax.ppermute(array, axis, [(i, i ^ by) for i in range(size)])


def hold_lists(one, two):
    together = hold([*one, *two])
    return together[: len(one)], together[len(one) :]


def exchange(array, *axes):
    return lax.all_to_all(array, axes, 0, 0)


def swap_parts(parts):
    return [parts[0]] + [partner(parts[k], "head", k) for k in range(1, len(parts))]


def share_heads(array):
    return [array] + [partner(array, "head", k) for k in range(1, lax.axis_size("head"))]


def across_core(parts):
    return [partner(part, "dp", 1) for part in parts]


def to_chip(array, k):
    axis, by = [("blk", 1), ("dp", 2), (("dp", "blk"), 5)][k - 1]
    return partner(array, axis, by)


def plane_gather(array):
    chips = [array] + [to_chip(array, k) for k in (1, 2, 3)]
    return chips + across_core(chips)


def body(
    dec_in,
    enc_out,
    passage_len,
    dec_len,
    passage_owner,
    gain_self,
    gain_cross,
    gain_ffn,
    w_query,
    w_key,
    w_value,
    w_out,
    c_query,
    c_key,
    c_value,
    c_out,
    w_in,
    w_back,
    cotangent,
):
    blk_count = lax.axis_size("blk")
    dp_count = lax.axis_size("dp")
    head_count = lax.axis_size("head")
    small = blk_count == 2 and dp_count == 4
    chunk_count = blk_count * head_count
    plane = dp_count * blk_count
    width, depth = w_query.shape
    units = w_in.shape[1]
    rows = dec_in.shape[0]
    piece = rows // head_count
    passages = enc_out.shape[0] // LP
    head_place = lax.axis_index("head")
    blk_place = lax.axis_index("blk")
    core = lax.axis_index("dp") % 2
    gain_one, gain_two, gain_three = gain_self, gain_cross, gain_ffn

    half = width // 2
    slots = lax.dynamic_slice_in_dim(passage_owner, head_place * passages, passages) ^ blk_place
    lengths = lax.dynamic_slice_in_dim(passage_len, head_place * passages, passages)

    half = width // 2
    sides = [
        lax.dynamic_slice_in_dim(weight, blk_place % 2 * half, half, 0)
        for weight in (c_key, c_value, c_query, c_out)
    ]
    pair = lax.axis_index("dp") // 2 % 2
    mine = jnp.where(
        core == 0, jnp.where(pair == 0, *sides[:2]), jnp.where(pair == 0, *sides[2:])
    )
    near = [partner(mine, "head", k) for k in range(1, head_count)]
    normed_one, self_qkv, self_flat, *partials = call_self(
        after(dec_in, mine) if CFG["s_o"] == 1 else dec_in,
        dec_len, gain_one, w_query, w_key, w_value, w_out, head_count
    )
    partials = swap_parts(partials)
    if CFG["s_a"] == 1:
        near = hold(near, partials[1])
    elif CFG["s_a"] == 2:
        *near, self_flat = hold([*near, self_flat])
    (near,) = call(
        join_kernel, [shaped((len(near) * half, depth), bf16)], [], near, micros=0.3
    )
    beside = partner(near, "blk", 1)
    arrays = [near, beside, partner(near, "dp", 2)]
    if CFG["s_xy"] == 1 and blk_count == 2:
        arrays.append(partner(near, ("dp", "blk"), 5))
    else:
        arrays.append(partner(beside, "dp", 2))
    arrays = arrays + across_core(arrays)
    first, message = call(
        functools.partial(normed_kernel, head_count),
        [shaped((piece, depth), f32), shaped((chunk_count, piece, depth), bf16)],
        [],
        [*hold(partials, slots, lengths), dec_in, gain_two],
    )
    if CFG["s_a"] == 3:
        message, near, beside = hold([message, near, beside])
    chunks = exchange(message, "blk", "head")
    enc_keys, enc_values, weights = project(
        enc_out, (c_key, c_value, c_query, c_out), arrays, head_count - 1
    )
    key_full, value_full, query_full, cross_out_full = [Weight(weights, i) for i in range(4)]
    early, queries = call(
        functools.partial(query_kernel, blk_count, head_count),
        [
            shaped((rows, -(-(2 * depth + width) // 256) * 256), bf16),
            shaped((blk_count, rows, depth), bf16),
        ],
        [],
        [chunks, query_full, normed_one, self_flat],
        [pltpu.VMEM((rows, depth), bf16)],
    )
    if CFG["e_y"] == 0:
        early_beside = partner(after(early, enc_keys), "blk", 1)
    partials = cross_forward(
        slots, lengths, queries, enc_keys, enc_values, head_count, width
    )
    if CFG["e_y"] == 0:
        partials, early_beside = hold([partials, early_beside])
    cross, second, logsum, *messages = call(
        functools.partial(combine_kernel, width),
        [
            shaped((piece, depth), f32),
            shaped((piece, depth), f32),
            shaped((piece, STATS), f32),
        ]
        + [shaped((piece, depth + width), bf16)] * head_count,
        [],
        [exchange(partials, "blk", "head"), first, cross_out_full, gain_three],
    )
    if CFG["e_y"] == 0:
        early = [early, early_beside] if small else [early]
        if small:
            early += [partner(part, "dp", 2) for part in hold(early, second)]
    else:
        early = [after(early, second)]
        if small:
            early += [partner(early[0], "blk", 1), partner(early[0], "dp", 2)]
    chunks = swap_parts(messages)
    outs = call(
        functools.partial(ffn_kernel, head_count),
        [shaped((piece, 2 * depth), bf16)] * head_count
        + [
            shaped((rows, 2 * depth + 2 * units), bf16),
            shaped((rows, width), bf16),
        ],
        [],
        [*chunks, cotangent, w_in, w_back],
        [pltpu.VMEM((rows, depth), f32)],
    )
    wide, cross_cols = outs[head_count:]
    wide_beside = partner(wide, "blk", 1)
    wide = [wide, wide_beside, partner(wide, "dp", 2)] if small else [wide]
    if small and CFG["e_y"] == 1:
        early.append(partner(after(early[1], wide[0]), "dp", 2))
    upstream = swap_parts(outs[:head_count])
    grad_second, gain_ffn_part, layer, message = call(
        functools.partial(branch_kernel, head_count, width),
        [
            shaped((piece, depth), f32),
            shaped((1, depth), f32),
            shaped((piece, depth), bf16),
            shaped((chunk_count, piece, depth + STATS), bf16),
        ],
        [],
        [*upstream, second, gain_three, cotangent, cross_out_full, cross, logsum],
    )
    if small:
        if CFG["m_e"] == 1:
            message, *early = hold([message, *early])
    branches = exchange(message, "blk", "head")
    if small and CFG["e_c"] == 1:
        early = early + across_core(early)
        branches, *early = hold([branches, *early])
    query_grads, branch_two, enc_key_grads, enc_value_grads = cross_backward(
        slots,
        lengths,
        queries,
        cross_out_full,
        enc_keys,
        enc_values,
        branches,
        head_count,
        width,
    )
    query_grads = exchange(query_grads, "blk", "head")

    if small and CFG["w_x"] == 1:
        enc_key_grads, enc_value_grads = hold([enc_key_grads, enc_value_grads], *wide)
        wide.append(partner(after(wide[1], enc_key_grads), "dp", 2))
    elif small:
        wide.append(partner(wide[1], "dp", 2))
    shares = projection_grads(
        enc_key_grads, enc_value_grads, enc_out, cross_cols, branch_two, plane, head_count
    )
    if small and CFG["w_c"] == 1:
        wide_there = across_core(wide[:3])
        query_grads, shares, *wide_there = hold([query_grads, shares, *wide_there])
    elif CFG["t_cs"] == 1:
        query_grads, shares = hold([query_grads, shares])
    grad_first, gain_cross_part, *messages = call(
        first_kernel,
        [shaped((piece, depth), f32), shaped((1, depth), f32)]
        + [shaped((piece, depth + width), bf16)] * head_count,
        [],
        [query_grads, first, gain_two, query_full, grad_second],
    )
    if small and CFG["e_w"] in (4, 5):
        given = hold([*early, *wide[:3]], enc_key_grads) if CFG["e_w"] == 4 else [*early, *wide[:3]]
        there = across_core(given)
        messages, there = hold_lists(messages, there)
    if CFG["w_xy"] == 1:
        messages = hold(messages, *wide)
    chunks = swap_parts(messages)
    if small:
        if CFG["sh_q"] == 1:
            shares = after(shares, chunks[1])
        elif CFG["sh_q"] == 2:
            shares = after(shares, chunks[-1])
        elif CFG["t_shq"] == 1:
            shares = after(shares, messages[0])
        shares = exchange(shares, "dp", "blk")
    if small and CFG["e_w"] in (4, 5):
        early, wide = early + there[:4], wide + there[4:]
        last = across_core(hold(wide[3:4], chunks[1] if CFG["x_p"] == 1 else messages[0]))
        chunks, last = hold_lists(chunks, last)
        wide = wide + last
    if small and 1 <= CFG["e_w"] <= 3:
        both = [*early, *wide]
        if CFG["e_w"] == 1:
            both = hold(both, messages[0])
        elif CFG["e_w"] == 3:
            both = hold(both, chunks[1])
        there = across_core(both)
        chunks, there = hold_lists(chunks, there)
        early, wide = both[:4] + there[:4], both[4:] + there[4:]
    if CFG["e_p"] == 4:
        grad_enc = encoder_grads(
            *hold([enc_key_grads, enc_value_grads], messages[0]), key_full, value_full
        )
        chunks = hold(chunks, grad_enc)
    outs = call(
        functools.partial(self_back_kernel, head_count),
        (
            [shaped((piece, depth), bf16)] * head_count
            if CFG["t_rsz"] == "perm"
            else [shaped((head_count, piece, depth), bf16)]
        )
        + [
            shaped(
                (plane if small and CFG["t_late"] == "a2a" else 1, rows, depth + 4 * width), bf16
            )
        ],
        [dec_len],
        [*chunks, w_out, self_qkv, w_query, w_key, w_value],
        [pltpu.VMEM((rows, depth), f32), pltpu.VMEM((rows, depth + 4 * width), bf16)],
    )
    late = outs[-1]
    if small and CFG["e_w"] == 0:
        if CFG["e_c"] == 0:
            early = hold(early, late)
            early = early + across_core(early)
        if CFG["w_c"] == 1:
            wide = wide + wide_there + across_core(hold(wide[3:], late))
        else:
            wide = hold(wide, late)
            wide = wide + across_core(wide)
    if CFG["t_rsz"] == "perm":
        upstream = swap_parts(outs[:head_count])
    else:
        upstream = [exchange(outs[0], "head")]
    if small and CFG["l_p"] == 2:
        joined = hold([*upstream, *late])
        upstream, late = joined[: len(upstream)], joined[len(upstream) :]
        late.append(partner(late[1], "dp", 2))
    if CFG["t_shg"] == 1:
        (shares,) = hold([shares], *upstream)
    elif CFG["t_shg"] == 2:
        (shares,) = hold([shares], upstream[1])
    if CFG["l_q"] < 2:
        if CFG["l_q"] == 1:
            late = after(late, upstream[-1])
        if not small:
            late = [late.reshape(late.shape[1:])]
        elif CFG["t_late"] == "a2a":
            late = [exchange(late, "dp", "blk")]
        else:
            late = late.reshape(late.shape[1:])
            late = [late, partner(late, "blk", 1), partner(late, "dp", 2)]
            if CFG["l_d"] == 1:
                late.append(partner(late[0], ("dp", "blk"), 5))
    (message,) = call(
        functools.partial(input_kernel, len(upstream)),
        [shaped((head_count if CFG["t_agz"] == "a2a" else 1, 2 * piece + 16, depth), bf16)],
        [],
        [*upstream, dec_in, gain_one, grad_first, gain_cross_part, gain_ffn_part, layer],
        micros=3 * CFG["t_cost"],
    )
    if small and CFG["t_late"] == "perm" and CFG["l_p"] == 1:
        message, *late = hold([message, *late])
        late.append(partner(late[1], "dp", 2))
    if CFG["l_q"] == 2:
        late = after(late, message)
        if not small:
            late = [late.reshape(late.shape[1:])]
        elif CFG["t_late"] == "a2a":
            late = [exchange(late, "dp", "blk")]
        else:
            late = late.reshape(late.shape[1:])
            late = [late, partner(late, "blk", 1), partner(late, "dp", 2)]
            if CFG["l_d"] == 1:
                late.append(partner(late[0], ("dp", "blk"), 5))
    if CFG["t_agz"] == "perm":
        chunks = share_heads(message.reshape(message.shape[1:]))
    else:
        chunks = [exchange(message, "head")]
    if CFG["l_q"] == 3:
        late = after(late, chunks[1])
        if not small:
            late = [late.reshape(late.shape[1:])]
        elif CFG["t_late"] == "a2a":
            late = [exchange(late, "dp", "blk")]
        else:
            late = late.reshape(late.shape[1:])
            late = [late, partner(late, "blk", 1), partner(late, "dp", 2)]
            if CFG["l_d"] == 1:
                late.append(partner(late[0], ("dp", "blk"), 5))
    if CFG["t_shg"] == 3:
        shares = after(shares, chunks[1])
    elif CFG["t_shg"] == 4:
        shares = after(shares, message)
    pair = [enc_key_grads, enc_value_grads]
    if CFG["e_p"] == 1:
        pair = hold(pair, *upstream)
    elif CFG["e_p"] == 2:
        pair = hold(pair, message)
    elif CFG["e_p"] == 3:
        pair = hold(pair, chunks[1])
    if CFG["e_p"] != 4:
        grad_enc = encoder_grads(*pair, key_full, value_full)
        if CFG["e_p"] > 0:
            chunks = hold(chunks, grad_enc)
    if CFG["b_p"] == 3:
        wide = hold(wide, message)
    elif CFG["b_p"] == 4:
        wide = hold(wide, upstream[0])
    broad = call(
        functools.partial(wide_kernel, len(wide)),
        [shaped((depth, units), f32), shaped((units, depth), f32)],
        [],
        wide,
        [pltpu.VMEM((sum(part.shape[0] for part in wide), wide[0].shape[1]), bf16)],
        8 * CFG["t_cost"],
    )
    if CFG["b_p"] == 3 or CFG["b_p"] == 4:
        chunks = hold(chunks, broad[0])
    if small and CFG["l_p"] == 2 and CFG["l_xy"] == 1:
        *chunks, late[-1] = hold([*chunks, late[-1]])
    if small and CFG["t_late"] == "perm" and CFG["l_p"] == 0:
        joined = hold([*chunks, *late])
        chunks, late = joined[: len(chunks)], joined[len(chunks) :]
        if len(late) == 3:
            late.append(partner(late[1], "dp", 2))
    elif CFG["l_xy"] == 1:
        chunks = hold(chunks, late[-1])
    grad_in, gains, layer_out = call(
        functools.partial(place_kernel, head_count),
        [shaped((rows, depth), f32), shaped((8, depth), f32), shaped((rows, depth), bf16)],
        [],
        chunks,
        micros=3 * CFG["t_cost"],
    )
    if small:
        blocks, cross_share = call(
            share_kernel,
            [
                shaped((head_count, width // 4, depth), bf16),
                shaped((width // plane, depth), bf16),
            ],
            [],
            [shares],
            micros=3 * CFG["t_cost"],
        )
        blocks = exchange(blocks, "head")
        if CFG["t_p"] == 4:
            blocks, late[3] = hold([blocks, late[3]])
        if CFG["t_p"] == 1:
            (blocks,) = hold([blocks], grad_enc, broad[0], *late)
        elif CFG["t_p"] == 2:
            (blocks,) = hold([blocks], *late)
        elif CFG["t_p"] == 3:
            (blocks,) = hold([blocks], grad_enc, *late)
        (shares,) = call(
            spread_kernel,
            [shaped((plane, width // 4 + width // plane + 24, depth), bf16)],
            [],
            [blocks, cross_share, gains],
            micros=3 * CFG["t_cost"],
        )
        grad_c_key, grad_c_value, grad_c_out, *gains = call(
            collect_kernel,
            [shaped((width, depth), f32)] * 3 + [shaped((depth,), f32)] * 3,
            [],
            [exchange(shares, "dp", "blk")],
            micros=3 * CFG["t_cost"],
        )
    else:
        gains, shares = lax.psum((gains, shares.astype(f32)), ("dp", "blk"))
        blocks = shares[: 2 * depth].reshape(2, head_count, width, depth)
        blocks = jnp.swapaxes(blocks, 0, 1)
        blocks = sum(swap_parts([blocks[k] for k in range(head_count)]))
        grad_c_key, grad_c_value = blocks[0], blocks[1]
        grad_c_out = shares[2 * depth :]


    if small and CFG["t_late"] == "perm":
        late = late + across_core(late)
    slim = call(
        functools.partial(weight_kernel, len(early), len(late), width),
        [shaped((width, depth), f32)] * 5,
        [],
        [*early, *late],
        [
            pltpu.VMEM((sum(part.shape[0] for part in early), early[0].shape[1]), bf16),
            pltpu.VMEM((plane * rows if small else rows, late[0].shape[-1]), bf16),
        ],
        6 * CFG["t_cost"],
    )
    if not small:
        slim, broad = lax.psum((tuple(slim), tuple(broad)), ("dp", "blk"))
    return (
        layer_out,
        grad_in,
        grad_enc,
        gains[0],
        gains[1],
        gains[2],
        *slim,
        grad_c_key,
        grad_c_value,
        grad_c_out,
        *broad,
    )


def solution(mesh):
    rows = P(("dp", "blk"), None)
    enc = P(("dp", "blk", "head"), None)
    each = P(("dp", "blk"))
    heads = P("head", None)
    return jax.shard_map(
        body,
        mesh=mesh,
        in_specs=(
            rows,
            enc,
            each,
            each,
            each,
            P(),
            P(),
            P(),
            *[heads] * 8,
            P(None, "head"),
            heads,
            rows,
        ),
        out_specs=(rows, rows, enc, P(), P(), P(), *[heads] * 8, P(None, "head"), heads),
        check_vma=False,
    )
```
